32 devices in a mesh: view: 2 (over core), dp: 16 (over z, y, x).
Axes of the slice: x: 2, y: 2, z: 4, core: 2. Of those that a mesh axis runs over, the one named last changes fastest.
Arguments:
- augmented: bfloat16 [2, 64, 32, 32, 3], P('view', 'dp'), may hold values from -8 to 8
- shake_ratio: int32 [2, 64], P('view', 'dp'), may hold values from 0 to 16
- labels: int32 [64], P('dp'), may hold values from 0 to 9
- labelled: int32 [64], P('dp'), may hold values from 0 to 1
- view_order: int32 [64], replicated, may hold values from 0 to 63, each once
- stem_weight: float32 [27, 96], replicated, may hold values from -1.25 to 1.25
- conv_weight: float32 [4, 864, 96], replicated, may hold values from -0.21875 to 0.21875
- head_weight: float32 [96, 10], replicated, may hold values from -2.5 to 2.5
- norm_param: float32 [2, 4, 96], replicated, may hold values from 0.25 to 1.75
- teacher_stem: float32 [27, 96], replicated, may hold values from -1.25 to 1.25
- teacher_conv: float32 [4, 864, 96], replicated, may hold values from -0.21875 to 0.21875
- teacher_head: float32 [96, 10], replicated, may hold values from -2.5 to 2.5
- teacher_norm: float32 [2, 4, 96], replicated, may hold values from 0.25 to 1.75
- first_stem: float32 [27, 96], replicated, may hold values from -0.00021362305 to 0.00021362305
- first_conv: float32 [4, 864, 96], replicated, may hold values from -0.00021362305 to 0.00021362305
- first_head: float32 [96, 10], replicated, may hold values from -0.00021362305 to 0.00021362305
- first_norm: float32 [2, 4, 96], replicated, may hold values from -0.0017089844 to 0.0017089844
- second_stem: float32 [27, 96], replicated, may hold values from 1.1901361e-09 to 4.7605444e-09
- second_conv: float32 [4, 864, 96], replicated, may hold values from 1.1901361e-09 to 4.7605444e-09
- second_head: float32 [96, 10], replicated, may hold values from 1.1901361e-09 to 4.7605444e-09
- second_norm: float32 [2, 4, 96], replicated, may hold values from 7.616871e-08 to 3.0467484e-07
Outputs:
- grad_norm: float32 [], replicated
- cross_sum: float32 [], replicated
- labelled_count: float32 [], replicated
- consistency_sum: float32 [], replicated
- new_stem: float32 [27, 96], replicated
- stem_first: float32 [27, 96], replicated
- stem_second: float32 [27, 96], replicated
- stem_teacher: float32 [27, 96], replicated
- new_conv: float32 [4, 864, 96], replicated
- conv_first: float32 [4, 864, 96], replicated
- conv_second: float32 [4, 864, 96], replicated
- conv_teacher: float32 [4, 864, 96], replicated
- new_head: float32 [96, 10], replicated
- head_first: float32 [96, 10], replicated
- head_second: float32 [96, 10], replicated
- head_teacher: float32 [96, 10], replicated
- new_norm: float32 [2, 4, 96], replicated
- norm_first: float32 [2, 4, 96], replicated
- norm_second: float32 [2, 4, 96], replicated
- norm_teacher: float32 [2, 4, 96], replicated
- stem_copy: bfloat16 [27, 96], replicated
- conv_copy: bfloat16 [4, 864, 96], replicated
- head_copy: bfloat16 [96, 10], replicated
The draws below stay inside these ranges and needn't reach their ends.
Inputs may be any that keep to these rules, and one draw needn't show every extreme that they name: `view_order`: each image number appears once.
All inputs are finite; a program needn't handle non-finite values.
Results may differ from the reference program's by a relative error of at most 0.00125.
The reference program's roundings to bfloat16 on the way count: a program that leaves them out, or rounds other values in their place, can miss the bound.
Values may be sent and summed in bfloat16 or wider, within the bound.
No kernel may reach another device: no remote copies, remote signals or barrier semaphores. Data moves between devices by JAX's collectives and lax.ppermute only.
A program may use at most 128 MiB of HBM per device.

```python
import math
import jax
import jax.numpy as jnp
from jax import lax

C = 96
CLASSES = 10
SIDE = 32
STEP = 5
IMAGES = 64
NPAR = 336096


def draw_augmented(key, part):
    key = jax.random.fold_in(key, 11)
    places = jnp.arange(IMAGES, dtype=jnp.float32) / IMAGES
    factor = 0.6 + 1.2 * places
    values = jnp.clip(jax.random.normal(key, (2, IMAGES, SIDE, SIDE, 3), jnp.float32), -4.0, 4.0)
    return (values * factor[None, :, None, None, None]).astype(jnp.bfloat16)


def draw_labelled(key, part):
    key = jax.random.fold_in(key, 12)
    picks = jax.random.randint(key, (IMAGES,), 0, 1000)
    levels = 200 + 600 * jnp.arange(IMAGES, dtype=jnp.int32) // IMAGES
    return (picks < levels).astype(jnp.int32)


def touch_ends(values, own_key, smallest, top_value):
    place = [jax.random.randint(jax.random.fold_in(own_key, axis), (), 0, length) for axis, length in enumerate(values.shape)]
    longest = values.shape.index(max(values.shape))
    neighbour = place[:longest] + [(place[longest] + 1) % values.shape[longest]] + place[longest + 1:]
    return values.at[tuple(place)].set(smallest).at[tuple(neighbour)].set(top_value)


def scatter_about(key, dims, width, bound, kind=jnp.bfloat16):
    array = width * jax.random.normal(key, dims, jnp.float32)
    return jnp.clip(array, min=-bound, max=bound).astype(kind)


def setup_inputs(seed: int = 0) -> dict:
    seeds = jax.random.split(jax.random.key(seed), 22)
    augmented = draw_augmented(jax.random.fold_in(seeds[21], 71), 0)
    shake_ratio = touch_ends(jax.random.randint(seeds[1], (2, IMAGES), 0, 17), jax.random.fold_in(seeds[1], 1), 0, 16).astype(jnp.int32)
    labels = touch_ends(jax.random.randint(seeds[2], (IMAGES,), 0, CLASSES), jax.random.fold_in(seeds[2], 1), 0, CLASSES - 1).astype(jnp.int32)
    labelled = draw_labelled(jax.random.fold_in(seeds[21], 71), 0)
    view_order = jax.random.permutation(seeds[4], IMAGES).astype(jnp.int32)
    stem_weight = scatter_about(seeds[5], (27, C), 27 ** -0.5, 1.25, jnp.float32)
    conv_weight = scatter_about(seeds[6], (4, 9 * C, C), (9 * C) ** -0.5, 0.21875, jnp.float32)
    head_weight = scatter_about(seeds[7], (C, CLASSES), (C // 16) ** -0.5, 2.5, jnp.float32)
    norm_param = jnp.clip(1.0 + 0.15 * jax.random.normal(seeds[8], (2, 4, C), jnp.float32), 0.25, 1.75)
    teacher_stem = scatter_about(seeds[9], (27, C), 27 ** -0.5, 1.25, jnp.float32)
    teacher_conv = scatter_about(seeds[10], (4, 9 * C, C), (9 * C) ** -0.5, 0.21875, jnp.float32)
    teacher_head = scatter_about(seeds[11], (C, CLASSES), (C // 16) ** -0.5, 2.5, jnp.float32)
    teacher_norm = jnp.clip(1.0 + 0.15 * jax.random.normal(seeds[12], (2, 4, C), jnp.float32), 0.25, 1.75)
    first_stem = scatter_about(seeds[13], (27, C), (0.02 / NPAR ** 0.5), 0.00021362305, jnp.float32)
    first_conv = scatter_about(seeds[14], (4, 9 * C, C), (0.02 / NPAR ** 0.5), 0.00021362305, jnp.float32)
    first_head = scatter_about(seeds[15], (C, CLASSES), (0.02 / NPAR ** 0.5), 0.00021362305, jnp.float32)
    first_norm = scatter_about(seeds[16], (2, 4, C), (0.16 / NPAR ** 0.5), 0.0017089844, jnp.float32)
    second_stem = jnp.clip(jnp.exp(jax.random.uniform(seeds[17], (27, C), jnp.float32, math.log(1.190136100781558e-09), math.log(4.760544403126232e-09))), 1.190136100781558e-09, 4.760544403126232e-09)
    second_conv = jnp.clip(jnp.exp(jax.random.uniform(seeds[18], (4, 9 * C, C), jnp.float32, math.log(1.190136100781558e-09), math.log(4.760544403126232e-09))), 1.190136100781558e-09, 4.760544403126232e-09)
    second_head = jnp.clip(jnp.exp(jax.random.uniform(seeds[19], (C, CLASSES), jnp.float32, math.log(1.190136100781558e-09), math.log(4.760544403126232e-09))), 1.190136100781558e-09, 4.760544403126232e-09)
    second_norm = jnp.clip(jnp.exp(jax.random.uniform(seeds[20], (2, 4, C), jnp.float32, math.log(7.616871045001972e-08), math.log(3.0467484180007887e-07))), 7.616871045001972e-08, 3.0467484180007887e-07)
    return dict(augmented=augmented, shake_ratio=shake_ratio, labels=labels, labelled=labelled, view_order=view_order, stem_weight=stem_weight, conv_weight=conv_weight, head_weight=head_weight, norm_param=norm_param, teacher_stem=teacher_stem, teacher_conv=teacher_conv, teacher_head=teacher_head, teacher_norm=teacher_norm, first_stem=first_stem, first_conv=first_conv, first_head=first_head, first_norm=first_norm, second_stem=second_stem, second_conv=second_conv, second_head=second_head, second_norm=second_norm)


EPS_NORM = 1e-05
LEARN_RATE = 0.03
BETA_FIRST = 0.5
BETA_SECOND = 0.5
WEIGHT_DECAY = 0.0001
ADAM_EPS = 1e-08
CLIP_LIMIT = 0.02
TEACHER_KEEP = 0.9
CONS_WEIGHT = 10.0
HIGHEST = lax.Precision.HIGHEST

@jax.custom_vjp
def low(v):
    return lax.optimization_barrier(v.astype(jnp.bfloat16)).astype(jnp.float32)

@jax.custom_vjp
def low_back(v):
    return v

def low_keep(v):
    return (low(v), None)

def low_pass(kept, grad):
    return (grad,)

def back_keep(v):
    return (v, None)

def back_low(kept, grad):
    return (low(grad),)
low.defvjp(low_keep, low_pass)
low_back.defvjp(back_keep, back_low)

def convolve(inputs, weight):
    kernel = weight.reshape(3, 3, weight.shape[0] // 9, weight.shape[1])
    return lax.conv_general_dilated(inputs, kernel, (1, 1), 'SAME', dimension_numbers=('NHWC', 'HWIO', 'NHWC'), precision=HIGHEST)

def batch_norm(values, gain, shift):
    average = lax.optimization_barrier(jnp.mean(values, axis=(0, 1, 2)))
    spread = lax.optimization_barrier(jnp.mean(values * values, axis=(0, 1, 2))) - average * average
    return (values - average) * lax.rsqrt(spread + EPS_NORM) * gain + shift

def forward(weights, images, alpha):
    stem_weight, conv_weight, head_weight, norm_param = weights
    stem_out = low_back(convolve(images, low(stem_weight)))
    stem_low = low(stem_out)
    mixed = stem_out
    for branch in range(2):
        first = low_back(convolve(stem_low, low(conv_weight[2 * branch])))
        hidden = low(jax.nn.silu(batch_norm(first, norm_param[0, 2 * branch], norm_param[1, 2 * branch])))
        second = low_back(convolve(hidden, low(conv_weight[2 * branch + 1])))
        result = jax.nn.silu(batch_norm(second, norm_param[0, 2 * branch + 1], norm_param[1, 2 * branch + 1]))
        factor = alpha if branch == 0 else 1.0 - alpha
        mixed = mixed + factor[:, None, None, None] * result
    pooled = lax.optimization_barrier(jnp.mean(mixed, axis=(1, 2)))
    return low_back(jnp.dot(low(pooled), low(head_weight), precision=HIGHEST))

def adam_update(gradient, weight, first, second, teacher, factor):
    clipped = gradient * factor
    first_new = BETA_FIRST * first + (1.0 - BETA_FIRST) * clipped
    second_new = BETA_SECOND * second + (1.0 - BETA_SECOND) * clipped * clipped
    first_hat = first_new / (1.0 - BETA_FIRST ** STEP)
    second_hat = second_new / (1.0 - BETA_SECOND ** STEP)
    weight_new = weight - LEARN_RATE * (first_hat / (jnp.sqrt(second_hat) + ADAM_EPS) + WEIGHT_DECAY * weight)
    teacher_new = TEACHER_KEEP * teacher + (1.0 - TEACHER_KEEP) * weight_new
    return (weight_new, first_new, second_new, teacher_new)

def reference(augmented, shake_ratio, labels, labelled, view_order, stem_weight, conv_weight, head_weight, norm_param, teacher_stem, teacher_conv, teacher_head, teacher_norm, first_stem, first_conv, first_head, first_norm, second_stem, second_conv, second_head, second_norm):
    images = augmented.astype(jnp.float32)
    alphas = (shake_ratio.astype(jnp.float32) + 1.0) / 18.0
    teacher = (teacher_stem, teacher_conv, teacher_head, teacher_norm)
    teacher_prob = [low(jax.nn.softmax(forward(teacher, images[view], alphas[view]), axis=-1)) for view in range(2)]
    inverse = jnp.zeros((IMAGES,), jnp.int32).at[view_order].set(jnp.arange(IMAGES, dtype=jnp.int32))
    targets = (teacher_prob[1][inverse], teacher_prob[0][view_order])
    mask_float = labelled.astype(jnp.float32)
    labelled_count = jnp.sum(mask_float)
    onehot = (labels[:, None] == jnp.arange(CLASSES, dtype=jnp.int32)[None, :]).astype(jnp.float32)

    def objective(*weights):
        cross = jnp.zeros((), jnp.float32)
        consistency = jnp.zeros((), jnp.float32)
        for view in range(2):
            logits = forward(weights, images[view], alphas[view])
            log_prob = jax.nn.log_softmax(logits, axis=-1)
            if view == 0:
                cross = -jnp.sum(mask_float * lax.optimization_barrier(jnp.sum(onehot * log_prob, axis=-1)))
            consistency = consistency + jnp.sum((jnp.exp(log_prob) - targets[view]) ** 2)
        return (cross / labelled_count + CONS_WEIGHT * consistency / (2 * IMAGES), (cross, consistency))
    weights_now = (stem_weight, conv_weight, head_weight, norm_param)
    loss_value, pullback, sums = jax.vjp(objective, *weights_now, has_aux=True)
    gradients = pullback(jnp.ones_like(loss_value))
    grad_norm = jnp.sqrt(sum((jnp.sum(g * g) for g in gradients)))
    factor = CLIP_LIMIT / jnp.maximum(grad_norm, CLIP_LIMIT)
    firsts = (first_stem, first_conv, first_head, first_norm)
    seconds = (second_stem, second_conv, second_head, second_norm)
    results = []
    for k in range(4):
        results.extend(adam_update(gradients[k], weights_now[k], firsts[k], seconds[k], teacher[k], factor))
    copies = [results[4 * k].astype(jnp.bfloat16) for k in range(3)]
    return (grad_norm, sums[0], labelled_count, sums[1], results[0], results[1], results[2], results[3], results[4], results[5], results[6], results[7], results[8], results[9], results[10], results[11], results[12], results[13], results[14], results[15], copies[0], copies[1], copies[2])
```

```python
import functools

import jax
import jax.numpy as jnp
from jax import lax
from jax.experimental import pallas as pl
from jax.experimental.pallas import tpu as pltpu
from jax.sharding import PartitionSpec as P

CLASSES = 10
STEP = 5
EPS_NORM = 1e-05
LEARN_RATE = 0.03
BETA_FIRST = 0.5
BETA_SECOND = 0.5
WEIGHT_DECAY = 0.0001
ADAM_EPS = 1e-08
CLIP_LIMIT = 0.02
TEACHER_KEEP = 0.9
CONS_WEIGHT = 10.0

F32 = jnp.float32
BF16 = jnp.bfloat16
LANE = 128
CH = 96
SIDE = 32
CELLS = SIDE * SIDE
TAPS = 9
WIDE = TAPS * CH
BLOCKS = -(-WIDE // LANE)
STEM_ROWS = 80
PADDED = CELLS + 2 * SIDE
PARAMS = pltpu.CompilerParams(vmem_limit_bytes=56 * 1024 * 1024)


def dot(a, b):
    return jnp.dot(a, b, preferred_element_type=F32)


def dot_rows(a, b):
    return lax.dot_general(a, b, (((0,), (0,)), ((), ())), preferred_element_type=F32)


def dot_lanes(a, b):
    return lax.dot_general(a, b, (((1,), (1,)), ((), ())), preferred_element_type=F32)


def column_places():
    return lax.broadcasted_iota(jnp.int32, (CELLS, 1), 0) & (SIDE - 1)


def fill_taps(ref, values, column, base=0):
    left = jnp.where(column > 0, pltpu.roll(values, 1, 0), 0.0)
    right = jnp.where(column < SIDE - 1, pltpu.roll(values, CELLS - 1, 0), 0.0)
    ref[SIDE : SIDE + CELLS, base : base + LANE] = left.astype(BF16)
    ref[SIDE : SIDE + CELLS, base + LANE : base + 2 * LANE] = values.astype(BF16)
    ref[SIDE : SIDE + CELLS, base + 2 * LANE : base + 3 * LANE] = right.astype(BF16)


def clear_edges(ref):
    edge = jnp.zeros((SIDE, ref.shape[1]), BF16)
    ref[0:SIDE, :] = edge
    ref[SIDE + CELLS :, :] = edge


def two_rows(ref):
    return jnp.concatenate([ref[0:CELLS, :], ref[SIDE : SIDE + CELLS, :]], axis=1)


def three_rows(ref):
    return jnp.concatenate(
        [ref[0:CELLS, :], ref[SIDE : SIDE + CELLS, :], ref[2 * SIDE : 2 * SIDE + CELLS, :]], axis=1
    )


def fold_rows(both):
    lower = jnp.concatenate([both[SIDE:, LANE:], jnp.zeros((SIDE, LANE), F32)], axis=0)
    return both[:, :LANE] + lower


def tap_block(raw, tap):
    return raw[:, tap * CH : (tap + 1) * CH]


def image_taps(image):
    place = lax.broadcasted_iota(jnp.int32, (1, CELLS), 1)
    across, down = place & (SIDE - 1), place // SIDE
    padded = jnp.concatenate([image.astype(F32), jnp.zeros((5, CELLS), F32)], axis=0)
    parts = []
    for ky in range(3):
        for kx in range(3):
            dy, dx = ky - 1, kx - 1
            inside = (across + dx >= 0) & (across + dx < SIDE) & (down + dy >= 0) & (down + dy < SIDE)
            moved = padded if dy == dx == 0 else pltpu.roll(padded, (-(SIDE * dy + dx)) % CELLS, 1)
            parts.append(jnp.where(inside, moved, 0.0))
    parts.append(jnp.zeros((8, CELLS), F32))
    return jnp.concatenate(parts, axis=0).astype(BF16)


def pad_lanes(row):
    return jnp.concatenate([row, jnp.zeros((row.shape[0], LANE - row.shape[1]), row.dtype)], axis=1)


def norm_terms(sums, squares, cell_count):
    average = sums / cell_count
    inverse = lax.rsqrt(squares / cell_count - average * average + EPS_NORM)
    return average, inverse


def column_sum(values):
    return jnp.sum(values, axis=0, keepdims=True)


def silu_slope(half, tanh):
    return 0.5 * (1.0 + tanh) * (1.0 + half * (1.0 - tanh))


def first_kernel(
    image_ref, stem_s, stem_t, cws0, cws2, cwt0, cwt2,
    first_ref, low_ref, pooled_ref, msg_ref,
    wst32, wst, wf, xp, acc,
):
    step = pl.program_id(0)
    images = pl.num_programs(0)
    column = column_places()

    @pl.when(step == 0)
    def _():
        wst32[...] = jnp.zeros(wst32.shape, F32)
        for n, stem in enumerate((stem_s, stem_t)):
            for tap in range(TAPS):
                wst32[8 * tap : 8 * tap + 3, n * LANE : n * LANE + CH] = stem[3 * tap : 3 * tap + 3, :]
        wst[...] = wst32[...].astype(BF16)
        wf[...] = jnp.zeros(wf.shape, BF16)
        for n, pair in enumerate(((cws0, cws2), (cwt0, cwt2))):
            for b, raw in enumerate(pair):
                for tap in range(TAPS):
                    wf[n, tap * LANE : tap * LANE + CH, b * LANE : b * LANE + CH] = jnp.transpose(
                        tap_block(raw, tap)
                    ).astype(BF16)
        for n in range(2):
            clear_edges(xp.at[n])
        acc[...] = jnp.zeros(acc.shape, F32)

    stems = dot_rows(image_taps(image_ref[...]), wst[...])
    for n in range(2):
        stem = stems[:, n * LANE : (n + 1) * LANE]
        total = column_sum(stem)
        pooled_ref[n, pl.ds(step, 1), :] = total
        pooled_ref[n, pl.ds(step + images, 1), :] = total
        if n == 0:
            low_ref[...] = stem.astype(BF16)
        fill_taps(xp.at[n], stem, column)
        out = dot(three_rows(xp.at[n]), wf[n])
        first_ref[n] = out
        for b in range(2):
            part = out[:, b * LANE : (b + 1) * LANE]
            row = 4 * n + 2 * b
            acc[row : row + 1, :] += column_sum(part)
            acc[row + 1 : row + 2, :] += column_sum(part * part)

    @pl.when(step == images - 1)
    def _():
        msg_ref[...] = jnp.broadcast_to(acc[...][None], msg_ref.shape)


def forward_weight_kernel(raw_ref, w_ref):
    w_ref[...] = jnp.zeros(w_ref.shape, BF16)
    for ky in range(3):
        for kx in range(3):
            row = min(ky, 1) * 3 * LANE + kx * LANE
            lane = LANE if ky == 2 else 0
            w_ref[row : row + CH, lane : lane + CH] = jnp.transpose(tap_block(raw_ref, ky * 3 + kx)).astype(BF16)


def backward_weight_kernel(raw_ref, w_ref):
    w_ref[...] = jnp.zeros(w_ref.shape, BF16)
    for ky in range(3):
        for kx in range(3):
            row = min(ky, 1) * 3 * LANE + kx * LANE
            lane = LANE if ky == 2 else 0
            w_ref[row : row + CH, lane : lane + CH] = tap_block(raw_ref, (2 - ky) * 3 + 2 - kx).astype(BF16)


def norm_rows(sums, norm, terms, first_row, norm_index, cell_count):
    for b in range(2):
        row = first_row + 2 * b
        average, inverse = norm_terms(sums[row : row + 1], sums[row + 1 : row + 2], cell_count)
        gain = pad_lanes(norm[0, 2 * b + norm_index : 2 * b + norm_index + 1, :])
        shift = pad_lanes(norm[1, 2 * b + norm_index : 2 * b + norm_index + 1, :])
        scale = inverse * gain
        terms[8 * b : 8 * b + 1, :] = 0.5 * scale
        terms[8 * b + 1 : 8 * b + 2, :] = 0.5 * (shift - average * scale)
        terms[8 * b + 2 : 8 * b + 3, :] = inverse
        terms[8 * b + 3 : 8 * b + 4, :] = -average * inverse
        terms[8 * b + 4 : 8 * b + 5, :] = scale


def term(terms, b, k):
    return terms[8 * b + k : 8 * b + k + 1, :]


def second_kernel(
    cell_count, first_ref, recv_ref, norm_s, norm_t, ws_ref, wt_ref,
    second_ref, msg_ref,
    xp, terms_s, terms_t, acc,
):
    step = pl.program_id(0)
    images = pl.num_programs(0)
    column = column_places()

    @pl.when(step == 0)
    def _():
        sums = jnp.sum(recv_ref[...], axis=0)
        norm_rows(sums, norm_s, terms_s, 0, 0, cell_count)
        norm_rows(sums, norm_t, terms_t, 4, 0, cell_count)
        for k in range(4):
            clear_edges(xp.at[k])
        acc[...] = jnp.zeros(acc.shape, F32)

    for n, (terms, w) in enumerate(((terms_s, ws_ref), (terms_t, wt_ref))):
        for b in range(2):
            k = 2 * n + b
            half = first_ref[n, :, b * LANE : (b + 1) * LANE] * term(terms, b, 0) + term(terms, b, 1)
            fill_taps(xp.at[k], half + half * jnp.tanh(half), column)
            out = fold_rows(dot(two_rows(xp.at[k]), w[b]))
            second_ref[n, :, b * LANE : (b + 1) * LANE] = out
            acc[2 * k : 2 * k + 1, :] += column_sum(out)
            acc[2 * k + 1 : 2 * k + 2, :] += column_sum(out * out)

    @pl.when(step == images - 1)
    def _():
        msg_ref[...] = jnp.broadcast_to(acc[...][None], msg_ref.shape)


def head_rows(head_ref):
    padded = jnp.concatenate([head_ref[...], jnp.zeros((LANE - CLASSES, CH), F32)], axis=0)
    return pad_lanes(padded).astype(BF16)


def alpha_of(ratio_ref, step):
    return (ratio_ref[0, step].astype(F32) + 1.0) / 18.0


def class_lanes(rows):
    return lax.broadcasted_iota(jnp.int32, (rows, LANE), 1) < CLASSES


def log_softmax(logits, valid):
    top = jnp.max(jnp.where(valid, logits, -3e38), axis=1, keepdims=True)
    moved = logits - top
    total = jnp.sum(jnp.where(valid, jnp.exp(moved), 0.0), axis=1, keepdims=True)
    return moved - jnp.log(total)


def teacher_kernel(
    cell_count, ratio_ref, second_ref, recv_ref, norm, head_ref, stem_sum_ref,
    prob_ref,
    terms, pooled,
):
    step = pl.program_id(0)
    images = pl.num_programs(0)

    @pl.when(step == 0)
    def _():
        norm_rows(jnp.sum(recv_ref[...], axis=0), norm, terms, 4, 1, cell_count)

    alpha = alpha_of(ratio_ref, step)
    total = jnp.zeros((1, LANE), F32)
    for b in range(2):
        half = second_ref[:, b * LANE : (b + 1) * LANE] * term(terms, b, 0) + term(terms, b, 1)
        total += (alpha if b == 0 else 1.0 - alpha) * column_sum(half + half * jnp.tanh(half))
    pooled[pl.ds(step, 1), :] = total
    pooled[pl.ds(step + images, 1), :] = total

    @pl.when(step == images - 1)
    def _():
        low = ((pooled[...] + stem_sum_ref[...]) / CELLS).astype(BF16)
        rows = 2 * images
        logits = dot_lanes(low, head_rows(head_ref))
        valid = class_lanes(rows)
        first_rows = lax.broadcasted_iota(jnp.int32, (rows, LANE), 0) < images
        prob = jnp.where(valid & first_rows, jnp.exp(log_softmax(logits, valid)), 0.0)
        prob_ref[...] = pltpu.roll(prob.astype(BF16).astype(F32), 16, 1)


def student_kernel(
    cell_count, ratio_ref, labels_ref, labelled_ref, order_ref,
    second_ref, recv_ref, norm, head_ref, stem_sum_ref,
    msg_ref,
    terms, pooled, slopes,
):
    step = pl.program_id(0)
    images = pl.num_programs(0)

    @pl.when(step == 0)
    def _():
        norm_rows(jnp.sum(recv_ref[...], axis=0), norm, terms, 0, 1, cell_count)

    alpha = alpha_of(ratio_ref, step)
    total = jnp.zeros((1, LANE), F32)
    for b in range(2):
        values = second_ref[:, b * LANE : (b + 1) * LANE]
        half = values * term(terms, b, 0) + term(terms, b, 1)
        tanh = jnp.tanh(half)
        total += (alpha if b == 0 else 1.0 - alpha) * column_sum(half + half * tanh)
        slope = silu_slope(half, tanh)
        normal = values * term(terms, b, 2) + term(terms, b, 3)
        slopes[b, pl.ds(step, 1), :] = column_sum(slope)
        slopes[b, pl.ds(step + images, 1), :] = column_sum(slope * normal)
    pooled[pl.ds(step, 1), :] = total
    pooled[pl.ds(step + images, 1), :] = total

    @pl.when(step == images - 1)
    def _():
        dp_index = lax.axis_index("dp")
        low = ((pooled[...] + stem_sum_ref[...]) / CELLS).astype(BF16)
        logits = dot_lanes(low, head_rows(head_ref))
        rows = 2 * images
        info = jnp.where(class_lanes(rows), logits, 0.0)
        lane = lax.broadcasted_iota(jnp.int32, (rows, LANE), 1)
        row = lax.broadcasted_iota(jnp.int32, (rows, LANE), 0)
        for k in range(images):
            facts = (
                alpha_of(ratio_ref, k),
                labels_ref[k].astype(F32),
                labelled_ref[k].astype(F32),
                order_ref[dp_index * images + k].astype(F32),
            )
            for place, fact in enumerate(facts):
                info = jnp.where((row == k) & (lane == 32 + place), fact, info)
        msg_ref[:, 0:LANE] = slopes[0]
        msg_ref[:, LANE : 2 * LANE] = slopes[1]
        msg_ref[:, 2 * LANE :] = jnp.where(row < images, info, low.astype(F32))


def loss_part(images, all_images, cell_count, recv_ref, head_ref, rows_ref, means, small_ref):
    view = lax.axis_index("view")
    count = recv_ref.shape[0] * 2 * images
    raw = recv_ref[:, :, 2 * LANE :].reshape(count, LANE)
    row = lax.broadcasted_iota(jnp.int32, (count, 1), 0)
    part = row & (2 * images - 1)
    once = part < images
    facts = jnp.where(once, raw, pltpu.roll(raw, images, 0))
    image = ((row // (2 * images)) * images + (part & (images - 1))).astype(F32)
    alpha = facts[:, 32:33]
    label = facts[:, 33:34]
    labelled = facts[:, 34:35]
    order = facts[:, 35:36]
    eye = row == lax.broadcasted_iota(jnp.int32, (count, count), 1)
    image_lane = jnp.sum(jnp.where(eye, image, 0.0), axis=0, keepdims=True)
    order_lane = jnp.sum(jnp.where(eye, order, 0.0), axis=0, keepdims=True)
    first_lane = jnp.sum(jnp.where(eye & once, 1.0, 0.0), axis=0, keepdims=True)
    is_one = jnp.where(view == 0, 1.0, 0.0)
    ours = is_one * image + (1.0 - is_one) * order
    theirs = is_one * order_lane + (1.0 - is_one) * image_lane
    match = jnp.where((ours == theirs) & (first_lane > 0.5), 1.0, 0.0).astype(BF16)
    valid = class_lanes(count)
    other = pltpu.roll(facts, LANE - 16, 1)
    target = dot(match, jnp.where(valid, other, 0.0).astype(BF16))
    log_prob = jnp.where(valid, log_softmax(jnp.where(valid, facts, 0.0), valid), 0.0)
    probs = jnp.where(valid, jnp.exp(log_prob), 0.0)
    lane = lax.broadcasted_iota(jnp.int32, (count, LANE), 1)
    onehot = jnp.where(lane.astype(F32) == label, 1.0, 0.0)
    total = jnp.sum(jnp.where(once, labelled, 0.0), axis=0, keepdims=True)
    mask = labelled * is_one
    away = probs - target
    grad_prob = CONS_WEIGHT / all_images * away
    grad = mask * (probs - onehot) / total + probs * (
        grad_prob - jnp.sum(probs * grad_prob, axis=1, keepdims=True)
    )
    grad_low = grad.astype(BF16)
    dmix = dot(grad_low, head_rows(head_ref)) / CELLS
    weights = (dmix * alpha, dmix * (1.0 - alpha))
    for b in range(2):
        product = weights[b] * recv_ref[:, :, b * LANE : (b + 1) * LANE].reshape(count, LANE)
        plain = column_sum(jnp.where(once, product, 0.0))
        normal = column_sum(jnp.where(once, 0.0, product))
        means[2 * b : 2 * b + 1, :] = plain / cell_count
        means[2 * b + 1 : 2 * b + 2, :] = normal / cell_count
        rows_ref[b] = weights[b]
        small_ref[16 + 2 * b : 16 + 2 * b + 1, :] = plain
        small_ref[16 + 2 * b + 1 : 16 + 2 * b + 2, :] = normal
    rows_ref[2] = dmix
    cross = -jnp.sum(
        jnp.where(once, mask * jnp.sum(onehot * log_prob, axis=1, keepdims=True), 0.0), axis=0, keepdims=True
    )
    consistency = jnp.sum(
        jnp.where(once, jnp.sum(away * away, axis=1, keepdims=True), 0.0), axis=0, keepdims=True
    )
    lane_row = lax.broadcasted_iota(jnp.int32, (1, LANE), 1)
    small_ref[20:21, :] = jnp.where(
        lane_row == 0, cross, jnp.where(lane_row == 1, consistency, jnp.where(lane_row == 2, total, 0.0))
    )
    small_ref[21:24, :] = jnp.zeros((3, LANE), F32)
    pooled = jnp.where(once, 0.0, raw).astype(BF16)
    small_ref[0:16, :] = dot_rows(grad_low, pooled)[0:16, :]


def pack_grad(ref, blocks):
    side_by_side = jnp.concatenate(blocks + [jnp.zeros((CH, BLOCKS * LANE - WIDE), F32)], axis=1)
    for k in range(BLOCKS):
        ref[k * CH : (k + 1) * CH, :] = side_by_side[:, k * LANE : (k + 1) * LANE]
    if ref.shape[0] > BLOCKS * CH:
        ref[BLOCKS * CH :, :] = jnp.zeros((ref.shape[0] - BLOCKS * CH, LANE), F32)


def keep_and_send(keep_ref, send_ref, blocks):
    view = lax.axis_index("view")
    for own, ref in ((0, keep_ref), (1, send_ref)):
        @pl.when(view == own)
        def _():
            pack_grad(ref, blocks[0])

        @pl.when(view != own)
        def _():
            pack_grad(ref, blocks[1])


def back_second_kernel(
    cell_count, all_images,
    second_ref, first_ref, recv1_ref, recv2_ref, recv3_ref, norm, head_ref, w_ref,
    du_ref, msg_ref, keep_ref, send_ref, small_ref, dmix_ref,
    xd, xh, terms1, terms2, rows_ref, means, acc, gacc,
):
    step = pl.program_id(0)
    images = pl.num_programs(0)
    rows = dmix_ref.shape[0]
    column = column_places()
    base = lax.axis_index("dp") * rows

    @pl.when(step == 0)
    def _():
        norm_rows(jnp.sum(recv1_ref[...], axis=0), norm, terms1, 0, 0, cell_count)
        norm_rows(jnp.sum(recv2_ref[...], axis=0), norm, terms2, 0, 1, cell_count)
        loss_part(rows // 2, all_images, cell_count, recv3_ref, head_ref, rows_ref, means, small_ref)
        dmix_ref[...] = rows_ref[2, pl.ds(pl.multiple_of(base, rows), rows), :]
        for b in range(2):
            clear_edges(xd.at[b])
            clear_edges(xh.at[b])
        acc[...] = jnp.zeros(acc.shape, F32)
        gacc[...] = jnp.zeros(gacc.shape, F32)

    for b in range(2):
        lanes = slice(b * LANE, (b + 1) * LANE)
        values = second_ref[:, lanes]
        half = values * term(terms2, b, 0) + term(terms2, b, 1)
        slope = silu_slope(half, jnp.tanh(half))
        weight = rows_ref[b, pl.ds(base + step, 1), :]
        normal = values * term(terms2, b, 2) + term(terms2, b, 3)
        dy = term(terms2, b, 4) * (
            slope * weight - means[2 * b : 2 * b + 1, :] - normal * means[2 * b + 1 : 2 * b + 2, :]
        )
        fill_taps(xd.at[b], dy, column)
        before = first_ref[:, lanes]
        half1 = before * term(terms1, b, 0) + term(terms1, b, 1)
        tanh1 = jnp.tanh(half1)
        fill_taps(xh.at[b], half1 + half1 * tanh1, column)
        dh = fold_rows(dot(two_rows(xd.at[b]), w_ref[b]))
        du = dh * silu_slope(half1, tanh1)
        du_ref[:, lanes] = du
        normal1 = before * term(terms1, b, 2) + term(terms1, b, 3)
        acc[2 * b : 2 * b + 1, :] += column_sum(du)
        acc[2 * b + 1 : 2 * b + 2, :] += column_sum(du * normal1)
        pair = jnp.concatenate(
            [xd[b, SIDE : SIDE + CELLS, LANE : 2 * LANE], xd[b, 0:CELLS, LANE : 2 * LANE]], axis=1
        )
        gacc[b] += dot_rows(pair, two_rows(xh.at[b]))

    @pl.when(step == images - 1)
    def _():
        msg_ref[...] = jnp.broadcast_to(acc[...][None], msg_ref.shape)
        blocks = []
        for b in range(2):
            blocks.append([])
            for tap in range(TAPS):
                ky, kx = tap // 3, tap % 3
                row = LANE if ky == 2 else 0
                lane = min(ky, 1) * 3 * LANE + kx * LANE
                blocks[b].append(gacc[b, row : row + CH, lane : lane + CH])
        keep_and_send(keep_ref, send_ref, blocks)


def back_weight_kernel(
    cell_count,
    du_ref, first_ref, low_ref, recv1_ref, recv5_ref, norm,
    taps_ref, keep_ref, send_ref, sums_ref,
    xl, terms1, means, gacc,
):
    step = pl.program_id(0)
    images = pl.num_programs(0)
    column = column_places()

    @pl.when(step == 0)
    def _():
        norm_rows(jnp.sum(recv1_ref[...], axis=0), norm, terms1, 0, 0, cell_count)
        sums = jnp.sum(recv5_ref[...], axis=0)
        sums_ref[...] = sums
        means[...] = sums / cell_count
        clear_edges(xl)
        gacc[...] = jnp.zeros(gacc.shape, F32)

    clear_edges(taps_ref)
    for b in range(2):
        lanes = slice(b * LANE, (b + 1) * LANE)
        normal = first_ref[:, lanes] * term(terms1, b, 2) + term(terms1, b, 3)
        dy = term(terms1, b, 4) * (
            du_ref[:, lanes] - means[2 * b : 2 * b + 1, :] - normal * means[2 * b + 1 : 2 * b + 2, :]
        )
        fill_taps(taps_ref, dy, column, 3 * LANE * b)
    fill_taps(xl, low_ref[...].astype(F32), column)
    pair = jnp.concatenate(
        [taps_ref[SIDE : SIDE + CELLS, LANE : 2 * LANE], taps_ref[SIDE : SIDE + CELLS, 4 * LANE : 5 * LANE]], axis=1
    )
    gacc[...] += dot_rows(pair, three_rows(xl))

    @pl.when(step == images - 1)
    def _():
        keep_and_send(
            keep_ref, send_ref,
            [
                [gacc[b * LANE : b * LANE + CH, tap * LANE : tap * LANE + CH] for tap in range(TAPS)]
                for b in range(2)
            ],
        )


def back_stem_kernel(taps_ref, image_ref, dmix_ref, w_ref, stem_ref, sacc):
    step = pl.program_id(0)
    images = pl.num_programs(0)

    @pl.when(step == 0)
    def _():
        sacc[...] = jnp.zeros(sacc.shape, F32)

    weight = jnp.concatenate(
        [w_ref[0, 0 : 3 * LANE, :], w_ref[1, 0 : 3 * LANE, :], w_ref[0, 3 * LANE :, :], w_ref[1, 3 * LANE :, :]],
        axis=0,
    )
    dstem = fold_rows(dot(two_rows(taps_ref), weight)) + dmix_ref[pl.ds(step, 1), :]
    sacc[...] += dot(image_taps(image_ref[...]), dstem.astype(BF16))

    @pl.when(step == images - 1)
    def _():
        rows = [sacc[8 * tap : 8 * tap + 3, :] for tap in range(TAPS)]
        stem_ref[...] = jnp.concatenate(rows + [jnp.zeros((5, LANE), F32)], axis=0)


def adam_terms(gradient, factor, weight, first, second, teacher):
    clipped = gradient * factor
    first_new = BETA_FIRST * first + (1.0 - BETA_FIRST) * clipped
    second_new = BETA_SECOND * second + (1.0 - BETA_SECOND) * clipped * clipped
    first_hat = first_new / (1.0 - BETA_FIRST**STEP)
    second_hat = second_new / (1.0 - BETA_SECOND**STEP)
    weight_new = weight - LEARN_RATE * (
        first_hat / (jnp.sqrt(second_hat) + ADAM_EPS) + WEIGHT_DECAY * weight
    )
    return weight_new, first_new, second_new, TEACHER_KEEP * teacher + (1.0 - TEACHER_KEEP) * weight_new


def update_kernel(
    own_ref, other_ref, own_stem, other_stem, own_small, other_small, own_sums, other_sums,
    cw, cf, cs, ct, sw, sf, ss, st, hw, hf, hs, ht, nw, nf, ns, nt,
    cw_o, cf_o, cs_o, ct_o, cb_o, sw_o, sf_o, ss_o, st_o, sb_o, hw_o, hf_o, hs_o, ht_o, hb_o,
    nw_o, nf_o, ns_o, nt_o, scalar_ref,
    factor_ref,
):
    conv = pl.program_id(0)
    view = lax.axis_index("view")

    def both(a, b):
        return a[...] + b[...]

    @pl.when(conv == 0)
    def _():
        small = both(own_small, other_small)
        sums = both(own_sums, other_sums)
        stem = jnp.sum(both(own_stem, other_stem), axis=0)[:27, :CH]
        head = small[:CLASSES, :CH]
        gains = jnp.concatenate([sums[1:2], small[17:18], sums[3:4], small[19:20]], axis=0)[:, :CH]
        shifts = jnp.concatenate([sums[0:1], small[16:17], sums[2:3], small[18:19]], axis=0)[:, :CH]
        total = jnp.zeros((1, 1), F32)
        for part in (stem, head, gains, shifts):
            total += jnp.sum(jnp.sum(part * part, axis=1, keepdims=True), axis=0, keepdims=True)
        for ref in (own_ref, other_ref):
            for k in range(2):
                values = ref[k]
                column = jnp.sum(values * values, axis=0, keepdims=True)
                total += jnp.sum(column, axis=1, keepdims=True)
        norm = jnp.sqrt(total)
        factor = CLIP_LIMIT / jnp.maximum(norm, CLIP_LIMIT)
        factor_ref[...] = jnp.broadcast_to(factor, factor_ref.shape)
        lane = lax.broadcasted_iota(jnp.int32, (1, LANE), 1)
        scalar_ref[...] = jnp.where(lane == 3, norm, jnp.where(lane == 2, own_small[20:21, :], small[20:21, :]))
        sw_o[...], sf_o[...], ss_o[...], st_o[...] = adam_terms(stem, factor, sw[...], sf[...], ss[...], st[...])
        sb_o[...] = sw_o[...].astype(BF16)
        hw_o[...], hf_o[...], hs_o[...], ht_o[...] = adam_terms(head, factor, hw[...], hf[...], hs[...], ht[...])
        hb_o[...] = hw_o[...].astype(BF16)
        for k, part in enumerate((gains, shifts)):
            nw_o[k], nf_o[k], ns_o[k], nt_o[k] = adam_terms(part, factor, nw[k], nf[k], ns[k], nt[k])

    def update(ref, second):
        blocks = [ref[second, k * CH : (k + 1) * CH, :] for k in range(BLOCKS)]
        gradient = jnp.concatenate(blocks, axis=1)[:, :WIDE]
        weight, first, second_moment, teacher = adam_terms(
            gradient, factor_ref[0:1, 0:1], cw[...], cf[...], cs[...], ct[...]
        )
        cw_o[...] = weight
        cf_o[...] = first
        cs_o[...] = second_moment
        ct_o[...] = teacher
        cb_o[...] = weight.astype(BF16)

    mine = conv // 2 == view

    @pl.when(mine)
    def _():
        update(own_ref, conv & 1)

    @pl.when(jnp.logical_not(mine))
    def _():
        update(other_ref, conv & 1)


def whole(shape):
    return pl.BlockSpec(shape, lambda i: (0,) * len(shape))


def scalars():
    return pl.BlockSpec(memory_space=pltpu.SMEM)


def conv_part(k):
    return pl.BlockSpec((None, CH, WIDE), lambda i: (k, 0, 0))


def per_image(net):
    return pl.BlockSpec((None, None, CELLS, 2 * LANE), lambda i: (i, net, 0, 0))


def struct(shape, kind=F32):
    return jax.ShapeDtypeStruct(shape, kind)


def share(messages):
    return lax.all_to_all(messages, "dp", 0, 0)


def swap_view(values):
    return lax.ppermute(values, "view", [(0, 1), (1, 0)])


def forward_weights(conv):
    shape = (2, 6 * LANE, 2 * LANE)
    return pl.pallas_call(
        forward_weight_kernel,
        grid=(2,),
        in_specs=[pl.BlockSpec((None, CH, WIDE), lambda i: (2 * i + 1, 0, 0))],
        out_specs=pl.BlockSpec((None,) + shape[1:], lambda i: (i, 0, 0)),
        out_shape=struct(shape, BF16),
        compiler_params=PARAMS,
        cost_estimate=pl.CostEstimate(flops=2_000_000_000, bytes_accessed=4_000_000, transcendentals=0),
        name="forward_weight",
    )(conv)


def backward_weights(conv, first):
    shape = (2, 6 * LANE, 2 * LANE)
    return pl.pallas_call(
        backward_weight_kernel,
        grid=(2,),
        in_specs=[pl.BlockSpec((None, CH, WIDE), lambda i: (2 * i + 1 - first, 0, 0))],
        out_specs=pl.BlockSpec((None,) + shape[1:], lambda i: (i, 0, 0)),
        out_shape=struct(shape, BF16),
        compiler_params=PARAMS,
        cost_estimate=pl.CostEstimate(flops=2_000_000_000, bytes_accessed=4_000_000, transcendentals=0),
        name="backward_weight",
    )(conv)


def shards(
    augmented, shake_ratio, labels, labelled, view_order,
    stem_weight, conv_weight, head_weight, norm_param,
    teacher_stem, teacher_conv, teacher_head, teacher_norm,
    first_stem, first_conv, first_head, first_norm,
    second_stem, second_conv, second_head, second_norm,
):
    images = augmented.shape[1]
    dp = lax.axis_size("dp")
    all_images = images * dp
    cell_count = float(all_images * CELLS)
    rows = dp * 2 * images
    piece = -(-BLOCKS * CH // (dp * 16)) * 16
    conv, conv_t, conv_f, conv_s = (
        jnp.transpose(v, (0, 2, 1)) for v in (conv_weight, teacher_conv, first_conv, second_conv)
    )
    head, head_t, head_f, head_s = (v.T for v in (head_weight, teacher_head, first_head, second_head))
    pixels = jnp.transpose(augmented[0], (0, 3, 1, 2)).reshape(images, 3, CELLS)
    msg = struct((dp, 8, LANE))
    norm_spec = whole((2, 4, CH))
    recv_spec = whole((dp, 8, LANE))
    head_spec = whole((CLASSES, CH))
    image_spec = pl.BlockSpec((None, 3, CELLS), lambda i: (i, 0, 0))
    pair_spec = pl.BlockSpec((None, CELLS, 2 * LANE), lambda i: (i, 0, 0))
    both_spec = pl.BlockSpec((None, 2, CELLS, 2 * LANE), lambda i: (i, 0, 0, 0))
    low_spec = pl.BlockSpec((None, CELLS, LANE), lambda i: (i, 0, 0))
    taps_spec = pl.BlockSpec((None, PADDED, 6 * LANE), lambda i: (i, 0, 0))
    weight_spec = whole((2, 6 * LANE, 2 * LANE))
    grad_spec = whole((dp * piece, LANE))
    grad_shape = struct((dp * piece, LANE))
    taps_scratch = pltpu.VMEM((PADDED, 3 * LANE), BF16)

    def many(scratch, n):
        return pltpu.VMEM((n,) + scratch.shape, scratch.dtype)

    first, low, stem_sums, message = pl.pallas_call(
        first_kernel,
        grid=(images,),
        in_specs=[image_spec, whole((27, CH)), whole((27, CH)), conv_part(0), conv_part(2), conv_part(0), conv_part(2)],
        out_specs=[both_spec, low_spec, whole((2, 2 * images, LANE)), recv_spec],
        out_shape=[
            struct((images, 2, CELLS, 2 * LANE)), struct((images, CELLS, LANE), BF16),
            struct((2, 2 * images, LANE)), msg,
        ],
        scratch_shapes=[
            pltpu.VMEM((STEM_ROWS, 2 * LANE), F32), pltpu.VMEM((STEM_ROWS, 2 * LANE), BF16),
            pltpu.VMEM((2, 9 * LANE, 2 * LANE), BF16), many(taps_scratch, 2), pltpu.VMEM((8, LANE), F32),
        ],
        compiler_params=PARAMS,
        name="first_conv",
    )(pixels, stem_weight, teacher_stem, conv, conv, conv_t, conv_t)
    recv1 = share(message)
    weight_s, weight_t = forward_weights(conv), forward_weights(conv_t)

    second, message = pl.pallas_call(
        functools.partial(second_kernel, cell_count),
        grid=(images,),
        in_specs=[both_spec, recv_spec, norm_spec, norm_spec, weight_spec, weight_spec],
        out_specs=[both_spec, recv_spec],
        out_shape=[struct((images, 2, CELLS, 2 * LANE)), msg],
        scratch_shapes=[
            many(taps_scratch, 4), pltpu.VMEM((16, LANE), F32), pltpu.VMEM((16, LANE), F32), pltpu.VMEM((8, LANE), F32),
        ],
        compiler_params=PARAMS,
        name="second_conv",
    )(first, recv1, norm_param, teacher_norm, weight_s, weight_t)
    recv2 = share(message)
    back_weight_two, back_weight_one = backward_weights(conv, 0), backward_weights(conv, 1)

    stem_spec = lambda n: pl.BlockSpec((None, 2 * images, LANE), lambda i: (n, 0, 0))
    prob = pl.pallas_call(
        functools.partial(teacher_kernel, cell_count),
        grid=(images,),
        in_specs=[scalars(), per_image(1), recv_spec, norm_spec, head_spec, stem_spec(1)],
        out_specs=whole((2 * images, LANE)),
        out_shape=struct((2 * images, LANE)),
        scratch_shapes=[pltpu.VMEM((16, LANE), F32), pltpu.VMEM((2 * images, LANE), F32)],
        compiler_params=PARAMS,
        name="teacher_logits",
    )(shake_ratio, second, recv2, teacher_norm, head_t, stem_sums)
    other = swap_view(prob)
    facts = pl.pallas_call(
        functools.partial(student_kernel, cell_count),
        grid=(images,),
        in_specs=[scalars(), scalars(), scalars(), scalars(), per_image(0), recv_spec, norm_spec, head_spec, stem_spec(0)],
        out_specs=whole((2 * images, 3 * LANE)),
        out_shape=struct((2 * images, 3 * LANE)),
        scratch_shapes=[
            pltpu.VMEM((16, LANE), F32), pltpu.VMEM((2 * images, LANE), F32), pltpu.VMEM((2, 2 * images, LANE), F32),
        ],
        compiler_params=PARAMS,
        cost_estimate=pl.CostEstimate(flops=4_000_000_000, bytes_accessed=8_000_000, transcendentals=0),
        name="student_logits",
    )(shake_ratio, labels, labelled, view_order, second, recv2, norm_param, head, stem_sums)
    facts = facts + jnp.pad(other, ((0, 0), (2 * LANE, 0)))
    recv3 = share(jnp.broadcast_to(facts[None], (dp,) + facts.shape))

    du, message, keep, send, small, dmix = pl.pallas_call(
        functools.partial(back_second_kernel, cell_count, float(all_images)),
        grid=(images,),
        in_specs=[
            per_image(0), per_image(0), recv_spec, recv_spec, whole((dp, 2 * images, 3 * LANE)), norm_spec, head_spec,
            weight_spec,
        ],
        out_specs=[pair_spec, recv_spec, grad_spec, grad_spec, whole((24, LANE)), whole((2 * images, LANE))],
        out_shape=[
            struct((images, CELLS, 2 * LANE)), msg, grad_shape, grad_shape, struct((24, LANE)),
            struct((2 * images, LANE)),
        ],
        scratch_shapes=[
            many(taps_scratch, 2), many(taps_scratch, 2), pltpu.VMEM((16, LANE), F32), pltpu.VMEM((16, LANE), F32),
            pltpu.VMEM((3, rows, LANE), F32), pltpu.VMEM((8, LANE), F32),
            pltpu.VMEM((8, LANE), F32), pltpu.VMEM((2, 2 * LANE, 6 * LANE), F32),
        ],
        compiler_params=PARAMS,
        name="back_second",
    )(second, first, recv1, recv2, recv3, norm_param, head, back_weight_two)
    recv5 = share(message)
    small_other = swap_view(small)

    def scatter(keep, send):
        halves = keep + swap_view(send)
        return jnp.sum(share(halves.reshape(dp, piece, LANE)), axis=0)

    piece_two = scatter(keep, send)

    taps, keep, send, sums = pl.pallas_call(
        functools.partial(back_weight_kernel, cell_count),
        grid=(images,),
        in_specs=[pair_spec, per_image(0), low_spec, recv_spec, recv_spec, norm_spec],
        out_specs=[taps_spec, grad_spec, grad_spec, whole((8, LANE))],
        out_shape=[struct((images, PADDED, 6 * LANE), BF16), grad_shape, grad_shape, struct((8, LANE))],
        scratch_shapes=[
            taps_scratch, pltpu.VMEM((16, LANE), F32), pltpu.VMEM((8, LANE), F32),
            pltpu.VMEM((2 * LANE, 9 * LANE), F32),
        ],
        compiler_params=PARAMS,
        cost_estimate=pl.CostEstimate(flops=8_000_000_000, bytes_accessed=16_000_000, transcendentals=0),
        name="back_weight",
    )(du, first, low, recv1, recv5, norm_param)
    piece_one = scatter(keep, send)
    sums_other = swap_view(sums)

    stem_grad = pl.pallas_call(
        back_stem_kernel,
        grid=(images,),
        in_specs=[taps_spec, image_spec, whole((2 * images, LANE)), weight_spec],
        out_specs=whole((SIDE, LANE)),
        out_shape=struct((SIDE, LANE)),
        scratch_shapes=[pltpu.VMEM((STEM_ROWS, LANE), F32)],
        compiler_params=PARAMS,
        cost_estimate=pl.CostEstimate(flops=8_000_000_000, bytes_accessed=16_000_000, transcendentals=0),
        name="back_stem",
    )(taps, pixels, dmix, back_weight_one)

    parts = jnp.concatenate([piece_one, piece_two, stem_grad], axis=0)
    gathered = share(jnp.broadcast_to(parts[None], (dp,) + parts.shape))
    own = jnp.stack([gathered[:, :piece], gathered[:, piece : 2 * piece]]).reshape(2, dp * piece, LANE)
    own_stem = gathered[:, 2 * piece :]
    other_grads, other_stem = swap_view(own), swap_view(own_stem)

    conv_block = pl.BlockSpec((None, CH, WIDE), lambda i: (i, 0, 0))
    stem_block, norm_block = whole((27, CH)), norm_spec
    grads_spec, parts_spec = whole((2, dp * piece, LANE)), whole((dp, SIDE, LANE))
    outs = pl.pallas_call(
        update_kernel,
        grid=(4,),
        in_specs=[grads_spec] * 2 + [parts_spec] * 2 + [whole((24, LANE))] * 2 + [whole((8, LANE))] * 2
        + [conv_block] * 4 + [stem_block] * 4 + [head_spec] * 4 + [norm_block] * 4,
        out_specs=[conv_block] * 5 + [stem_block] * 5 + [head_spec] * 5 + [norm_block] * 4 + [whole((1, LANE))],
        out_shape=[struct((4, CH, WIDE))] * 4 + [struct((4, CH, WIDE), BF16)]
        + [struct((27, CH))] * 4 + [struct((27, CH), BF16)]
        + [struct((CLASSES, CH))] * 4 + [struct((CLASSES, CH), BF16)]
        + [struct((2, 4, CH))] * 4 + [struct((1, LANE))],
        scratch_shapes=[pltpu.VMEM((8, LANE), F32)],
        compiler_params=PARAMS,
        name="update",
    )(
        own, other_grads, own_stem, other_stem, small, small_other, sums, sums_other,
        conv, conv_f, conv_s, conv_t, stem_weight, first_stem, second_stem, teacher_stem,
        head, head_f, head_s, head_t, norm_param, first_norm, second_norm, teacher_norm,
    )
    convs = [jnp.transpose(v, (0, 2, 1)) for v in outs[:5]]
    stems = outs[5:10]
    heads = [v.T for v in outs[10:15]]
    norms = outs[15:19]
    scalar = outs[19][0]
    return (
        scalar[3], scalar[0], scalar[2], scalar[1],
        *stems[:4], *convs[:4], *heads[:4], *norms, stems[4], convs[4], heads[4],
    )


def solution(mesh):
    in_specs = (
        (P("view", "dp", None, None, None), P("view", "dp"), P("dp"), P("dp")) + (P(),) * 17
    )
    return jax.shard_map(shards, mesh=mesh, in_specs=in_specs, out_specs=(P(),) * 23, check_vma=False)
```

```python
import functools

import jax
import jax.numpy as jnp
from jax import lax
from jax.experimental import pallas as pl
from jax.experimental.pallas import tpu as pltpu
from jax.sharding import PartitionSpec as P

CLASSES = 10
STEP = 5
EPS_NORM = 1e-05
LEARN_RATE = 0.03
BETA_FIRST = 0.5
BETA_SECOND = 0.5
WEIGHT_DECAY = 0.0001
ADAM_EPS = 1e-08
CLIP_LIMIT = 0.02
TEACHER_KEEP = 0.9
CONS_WEIGHT = 10.0

F32 = jnp.float32
BF16 = jnp.bfloat16
LANE = 128
CH = 96
SIDE = 32
CELLS = SIDE * SIDE
IMAGES = 4
QUARTERS = 4
ACROSS = SIDE // QUARTERS
TILE = IMAGES * QUARTERS
LINE = ACROSS * TILE
STEPS = 4
DEEP = SIDE // STEPS
CHUNK = DEEP * LINE
ALL = SIDE * LINE
TAPS = 9
WIDE = TAPS * CH
BLOCKS = -(-WIDE // LANE)
GRAD_ROWS = BLOCKS * CH
STEM_ROWS = 80
CODE_TOP = 32000.0
FRAME = (SIDE + 2, ACROSS + 2, TILE)
PARAMS = pltpu.CompilerParams(vmem_limit_bytes=24 * 1024 * 1024)


def dot(a, b):
    return jnp.dot(a, b, preferred_element_type=F32)


def dot_rows(a, b):
    return lax.dot_general(a, b, (((0,), (0,)), ((), ())), preferred_element_type=F32)


def dot_lanes(a, b):
    return lax.dot_general(a, b, (((1,), (1,)), ((), ())), preferred_element_type=F32)


def frame_line(frame, first_line, values):
    lines = values.shape[0] // LINE
    width = values.shape[1]
    tiles = values.reshape(lines, ACROSS, TILE, width)
    row = lax.broadcasted_iota(jnp.int32, (1, TILE, 1), 1)
    before = jnp.where(row >= IMAGES, pltpu.roll(tiles[:, ACROSS - 1], IMAGES, 1), 0.0)
    after = jnp.where(row < TILE - IMAGES, pltpu.roll(tiles[:, 0], TILE - IMAGES, 1), 0.0)
    place = slice(first_line + 1, first_line + 1 + lines)
    frame[place, 1 : ACROSS + 1] = tiles.astype(BF16)
    frame[place, 0] = before.astype(BF16)
    frame[place, ACROSS + 1] = after.astype(BF16)


def clear_frame(frame):
    blank = jnp.zeros(frame.shape[1:], BF16)
    frame[0] = blank
    frame[SIDE + 1] = blank


def taps(frame, step, rows):
    parts = []
    for dy in rows:
        for kx in range(3):
            place = step * DEEP + 1 + dy
            lines = frame[place : place + DEEP, kx : kx + ACROSS]
            parts.append(lines.reshape(CHUNK, lines.shape[-1]))
    return jnp.concatenate(parts, axis=1)


def fold_lines(both, carry):
    upper = jnp.concatenate([carry, both[: CHUNK - LINE, LANE:]], axis=0)
    return both[:, :LANE] + upper, both[CHUNK - LINE :, LANE:]


def blank_line():
    return jnp.zeros((LINE, LANE), F32)


def new_lines(step):
    first = 0 if step == 0 else step * DEEP + 1
    return first, min((step + 1) * DEEP + 1, SIDE)


def chunk_rows(step):
    return slice(step * CHUNK, (step + 1) * CHUNK)


def per_image(values, pattern):
    shape = values.shape
    return (values.reshape(shape[0] // 8, 8, shape[1]) * pattern[None]).reshape(shape)


def eight(values):
    parts = values.reshape(values.shape[0] // 8, 8, values.shape[1])
    while parts.shape[0] > 1:
        middle = parts.shape[0] // 2
        rest = parts[2 * middle :]
        parts = parts[:middle] + parts[middle : 2 * middle]
        if rest.shape[0]:
            parts = jnp.concatenate([parts[:-1], parts[-1:] + rest], axis=0) if middle > 1 else parts + rest
    return parts[0]


def both_halves(sums):
    return sums + pltpu.roll(sums, IMAGES, 0)


def tap_block(raw, tap):
    return raw[:, tap * CH : (tap + 1) * CH]


def image_lines(image_ref, plain, moved):
    plain[...] = jnp.zeros(plain.shape, F32)
    for channel in range(3):
        side_by_side = jnp.concatenate([image_ref[i, channel].astype(F32) for i in range(IMAGES)], axis=1)
        plain[pl.ds(8 + channel, SIDE, stride=8), :] = side_by_side
    source = lax.broadcasted_iota(jnp.int32, (LANE, LANE), 0)
    target = lax.broadcasted_iota(jnp.int32, (LANE, LANE), 1)
    same = source // SIDE == (target & (IMAGES - 1))
    across = ((target // IMAGES) & (QUARTERS - 1)) * ACROSS + target // TILE
    for kx in range(3):
        picks = jnp.where(same & ((source & (SIDE - 1)) == across + (kx - 1)), 1.0, 0.0).astype(BF16)
        moved[kx] = dot(plain[...].astype(BF16), picks)


def image_taps(moved, first_line, lines):
    columns = []
    for line in range(lines):
        place = (first_line + line) * 8
        parts = [moved[kx, place : place + 24, :] for kx in range(3)]
        columns.append(jnp.concatenate(parts + [jnp.zeros((8, LANE), F32)], axis=0))
    return jnp.concatenate(columns, axis=1).astype(BF16)


def stem_row(tap):
    return (tap % 3) * 24 + (tap // 3) * 8


def pad_lanes(row):
    return jnp.concatenate([row, jnp.zeros((row.shape[0], LANE - row.shape[1]), row.dtype)], axis=1)


def norm_terms(sums, squares, cell_count):
    average = sums / cell_count
    inverse = lax.rsqrt(squares / cell_count - average * average + EPS_NORM)
    return average, inverse


def column_sum(values):
    return jnp.sum(values, axis=0, keepdims=True)


def silu_slope(half, tanh):
    return 0.5 * (1.0 + tanh) * (1.0 + half * (1.0 - tanh))


def first_kernel(
    image_hbm, stem_s_hbm, stem_t_hbm, raw_s, raw_t,
    first_s, first_t, frame_s, moved_ref, pooled_ref, msg_ref,
    plain, wst32, wst, wf, frame_t, image_ref, stem_s, stem_t, raw, sems,
):
    coming = [
        pltpu.make_async_copy(source, target, sems.at[k])
        for k, (source, target) in enumerate((
            (image_hbm, image_ref), (stem_s_hbm, stem_s), (stem_t_hbm, stem_t),
            (raw_s.at[0], raw.at[0]), (raw_s.at[2], raw.at[1]), (raw_t.at[0], raw.at[2]), (raw_t.at[2], raw.at[3]),
        ))
    ]
    for copy in coming:
        copy.start()
    for copy in coming[:3]:
        copy.wait()
    image_lines(image_ref, plain, moved_ref)
    wst32[...] = jnp.zeros(wst32.shape, F32)
    for n, stem in enumerate((stem_s, stem_t)):
        for tap in range(TAPS):
            row = stem_row(tap)
            wst32[row : row + 3, n * LANE : n * LANE + CH] = stem[3 * tap : 3 * tap + 3, :]
    wst[...] = wst32[...].astype(BF16)
    wf[...] = jnp.zeros(wf.shape, BF16)
    for copy in coming[3:]:
        copy.wait()
    for n in range(2):
        for b in range(2):
            for tap in range(TAPS):
                wf[n, tap * LANE : tap * LANE + CH, b * LANE : b * LANE + CH] = jnp.transpose(
                    tap_block(raw.at[2 * n + b], tap)
                ).astype(BF16)
    clear_frame(frame_s)
    clear_frame(frame_t)
    pooled = [0.0, 0.0]
    sums = [0.0] * 8
    for step in range(STEPS):
        first_line, end = new_lines(step)
        stems = dot_rows(image_taps(moved_ref, first_line, end - first_line), wst[...])
        for n, (frame, out_ref) in enumerate(((frame_s, first_s), (frame_t, first_t))):
            stem = stems[:, n * LANE : (n + 1) * LANE]
            pooled[n] += eight(stem)
            frame_line(frame, first_line, stem)
            out = dot(taps(frame, step, (-1, 0, 1)), wf[n])
            out_ref[chunk_rows(step), :] = out
            for b in range(2):
                part = out[:, b * LANE : (b + 1) * LANE]
                sums[4 * n + 2 * b] += eight(part)
                sums[4 * n + 2 * b + 1] += eight(part * part)
    for n in range(2):
        pooled_ref[n] = both_halves(pooled[n])
    spread_sums(msg_ref, sums)


def total_of(refs):
    total = refs[0][...]
    for ref in refs[1:]:
        total = total + ref[...]
    return total


def spread_sums(msg_ref, sums):
    sums = [column_sum(part) for part in sums]
    if len(sums) < 8:
        sums.append(jnp.zeros((8 - len(sums), LANE), F32))
    msg_ref[...] = jnp.concatenate(sums, axis=0)


def forward_weight_kernel(raw_ref, w_ref):
    w_ref[...] = jnp.zeros(w_ref.shape, BF16)
    for ky in range(3):
        for kx in range(3):
            row = (ky // 2) * 3 * LANE + kx * LANE
            lane = LANE if ky == 0 else 0
            w_ref[row : row + CH, lane : lane + CH] = jnp.transpose(tap_block(raw_ref, ky * 3 + kx)).astype(BF16)


def backward_weight_kernel(cw0, cw1, cw2, cw3, two_ref, one_ref):
    two_ref[...] = jnp.zeros(two_ref.shape, BF16)
    one_ref[...] = jnp.zeros(one_ref.shape, BF16)
    for ky in range(3):
        for kx in range(3):
            tap = (2 - ky) * 3 + 2 - kx
            lane = LANE if ky == 0 else 0
            for b, (inner, outer) in enumerate(((cw0, cw1), (cw2, cw3))):
                row = (ky // 2) * 3 * LANE + kx * LANE
                two_ref[b, row : row + CH, lane : lane + CH] = tap_block(outer, tap).astype(BF16)
                row = (ky // 2) * 6 * LANE + kx * 2 * LANE + b * LANE
                one_ref[row : row + CH, lane : lane + CH] = tap_block(inner, tap).astype(BF16)


def norm_rows(sums, norm, terms, first_row, norm_index, cell_count):
    for b in range(2):
        row = first_row + 2 * b
        average, inverse = norm_terms(sums[row : row + 1], sums[row + 1 : row + 2], cell_count)
        gain = pad_lanes(norm[0, 2 * b + norm_index : 2 * b + norm_index + 1, :])
        shift = pad_lanes(norm[1, 2 * b + norm_index : 2 * b + norm_index + 1, :])
        scale = inverse * gain
        terms[8 * b : 8 * b + 1, :] = 0.5 * scale
        terms[8 * b + 1 : 8 * b + 2, :] = 0.5 * (shift - average * scale)
        terms[8 * b + 2 : 8 * b + 3, :] = inverse
        terms[8 * b + 3 : 8 * b + 4, :] = -average * inverse
        terms[8 * b + 4 : 8 * b + 5, :] = scale


def term(terms, b, k):
    return terms[8 * b + k : 8 * b + k + 1, :]


def second_kernel(
    cell_count, first_s, first_t, recv_ref, norm_s, norm_t, ws_ref, wt_ref,
    second_s, second_t, frame_s, msg_ref,
    frame_t, terms_s, terms_t,
):
    received = total_of(recv_ref)
    norm_rows(received, norm_s, terms_s, 0, 0, cell_count)
    norm_rows(received, norm_t, terms_t, 4, 0, cell_count)
    nets = ((first_s, terms_s, frame_s, ws_ref, second_s), (first_t, terms_t, frame_t, wt_ref, second_t))
    sums = [0.0] * 8
    carry = [blank_line()] * 4
    for _, _, frames, _, _ in nets:
        for b in range(2):
            clear_frame(frames.at[b])
    for step in range(STEPS):
        first_line, end = new_lines(step)
        for n, (source, terms, frames, w, target) in enumerate(nets):
            for b in range(2):
                k = 2 * n + b
                lanes = slice(b * LANE, (b + 1) * LANE)
                half = source[first_line * LINE : end * LINE, lanes] * term(terms, b, 0) + term(terms, b, 1)
                frame_line(frames.at[b], first_line, half + half * jnp.tanh(half))
                out, carry[k] = fold_lines(dot(taps(frames.at[b], step, (0, 1)), w[b]), carry[k])
                target[chunk_rows(step), lanes] = out
                sums[2 * k] += eight(out)
                sums[2 * k + 1] += eight(out * out)
    spread_sums(msg_ref, sums)


def head_rows(head_ref):
    padded = jnp.concatenate([head_ref[...], jnp.zeros((LANE - CLASSES, CH), F32)], axis=0)
    return pad_lanes(padded).astype(BF16)


def alpha_of(ratio_ref, image):
    return (ratio_ref[0, image].astype(F32) + 1.0) / 18.0


def alpha_rows(ratio_ref):
    row = lax.broadcasted_iota(jnp.int32, (2 * IMAGES, LANE), 0) & (IMAGES - 1)
    alpha = jnp.zeros((2 * IMAGES, LANE), F32)
    for k in range(IMAGES):
        alpha = jnp.where(row == k, alpha_of(ratio_ref, k), alpha)
    return alpha


def class_lanes(rows):
    return lax.broadcasted_iota(jnp.int32, (rows, LANE), 1) < CLASSES


def log_softmax(logits, valid):
    top = jnp.max(jnp.where(valid, logits, -3e38), axis=1, keepdims=True)
    moved = logits - top
    total = jnp.sum(jnp.where(valid, jnp.exp(moved), 0.0), axis=1, keepdims=True)
    return moved - jnp.log(total)


def pooled_low(ratio_ref, sums, stem_sums):
    alpha = alpha_rows(ratio_ref)
    total = alpha * both_halves(sums[0]) + (1.0 - alpha) * both_halves(sums[1])
    return ((total + stem_sums) / CELLS).astype(BF16)


def teacher_kernel(
    cell_count, ratio_ref, second_ref, recv_ref, norm, head_ref, stem_sum_ref,
    prob_ref,
    terms,
):
    norm_rows(total_of(recv_ref), norm, terms, 4, 1, cell_count)
    sums = [0.0] * 2
    for step in range(STEPS):
        for b in range(2):
            half = second_ref[chunk_rows(step), b * LANE : (b + 1) * LANE] * term(terms, b, 0) + term(terms, b, 1)
            sums[b] += eight(half + half * jnp.tanh(half))
    low = pooled_low(ratio_ref, sums, stem_sum_ref[1])
    logits = dot_lanes(low, head_rows(head_ref))
    valid = class_lanes(2 * IMAGES)
    first_rows = lax.broadcasted_iota(jnp.int32, (2 * IMAGES, LANE), 0) < IMAGES
    prob = jnp.where(valid & first_rows, jnp.exp(log_softmax(logits, valid)), 0.0)
    prob_ref[...] = pltpu.roll(prob.astype(BF16).astype(F32), 16, 1)


def student_kernel(
    cell_count, ratio_ref, labels_ref, labelled_ref, order_ref,
    second_ref, recv_ref, norm, head_ref, stem_sum_ref, prob_ref,
    msg_ref,
    terms,
):
    norm_rows(total_of(recv_ref), norm, terms, 0, 1, cell_count)
    sums = [0.0] * 6
    for step in range(STEPS):
        for b in range(2):
            values = second_ref[chunk_rows(step), b * LANE : (b + 1) * LANE]
            half = values * term(terms, b, 0) + term(terms, b, 1)
            tanh = jnp.tanh(half)
            sums[b] += eight(half + half * tanh)
            slope = silu_slope(half, tanh)
            normal = values * term(terms, b, 2) + term(terms, b, 3)
            sums[2 + b] += eight(slope)
            sums[4 + b] += eight(slope * normal)
    dp_index = lax.axis_index("dp")
    low = pooled_low(ratio_ref, sums, stem_sum_ref[0])
    logits = dot_lanes(low, head_rows(head_ref))
    rows = 2 * IMAGES
    info = jnp.where(class_lanes(rows), logits, 0.0)
    lane = lax.broadcasted_iota(jnp.int32, (rows, LANE), 1)
    row = lax.broadcasted_iota(jnp.int32, (rows, LANE), 0)
    for k in range(IMAGES):
        facts = (
            alpha_of(ratio_ref, k),
            labels_ref[k].astype(F32),
            labelled_ref[k].astype(F32),
            order_ref[dp_index * IMAGES + k].astype(F32),
        )
        for place, fact in enumerate(facts):
            info = jnp.where((row == k) & (lane == 32 + place), fact, info)
    for b in range(2):
        msg_ref[:, b * LANE : (b + 1) * LANE] = jnp.where(
            row < IMAGES, both_halves(sums[2 + b]), both_halves(sums[4 + b])
        )
    msg_ref[:, 2 * LANE :] = jnp.where(row < IMAGES, info + prob_ref[...], low.astype(F32))


def loss_part(images, all_images, cell_count, recv_refs, head_ref, rows_ref, means, small_ref):
    view = lax.axis_index("view")
    received = jnp.concatenate([ref[...] for ref in recv_refs], axis=0)
    count = received.shape[0] * 2 * images
    received = received.reshape(count, 3 * LANE)
    raw = received[:, 2 * LANE :]
    row = lax.broadcasted_iota(jnp.int32, (count, 1), 0)
    part = row & (2 * images - 1)
    once = part < images
    facts = jnp.where(once, raw, pltpu.roll(raw, images, 0))
    image = (((row // (2 * images)) ^ lax.axis_index("dp")) * images + (part & (images - 1))).astype(F32)
    alpha = facts[:, 32:33]
    label = facts[:, 33:34]
    labelled = facts[:, 34:35]
    order = facts[:, 35:36]
    eye = row == lax.broadcasted_iota(jnp.int32, (count, count), 1)
    image_lane = jnp.sum(jnp.where(eye, image, 0.0), axis=0, keepdims=True)
    order_lane = jnp.sum(jnp.where(eye, order, 0.0), axis=0, keepdims=True)
    first_lane = jnp.sum(jnp.where(eye & once, 1.0, 0.0), axis=0, keepdims=True)
    is_one = jnp.where(view == 0, 1.0, 0.0)
    ours = is_one * image + (1.0 - is_one) * order
    theirs = is_one * order_lane + (1.0 - is_one) * image_lane
    match = jnp.where((ours == theirs) & (first_lane > 0.5), 1.0, 0.0).astype(BF16)
    valid = class_lanes(count)
    other = pltpu.roll(facts, LANE - 16, 1)
    target = dot(match, jnp.where(valid, other, 0.0).astype(BF16))
    log_prob = jnp.where(valid, log_softmax(jnp.where(valid, facts, 0.0), valid), 0.0)
    probs = jnp.where(valid, jnp.exp(log_prob), 0.0)
    lane = lax.broadcasted_iota(jnp.int32, (count, LANE), 1)
    onehot = jnp.where(lane.astype(F32) == label, 1.0, 0.0)
    total = jnp.sum(jnp.where(once, labelled, 0.0), axis=0, keepdims=True)
    mask = labelled * is_one
    away = probs - target
    grad_prob = CONS_WEIGHT / all_images * away
    grad = mask * (probs - onehot) / total + probs * (
        grad_prob - jnp.sum(probs * grad_prob, axis=1, keepdims=True)
    )
    grad_low = grad.astype(BF16)
    dmix = dot(grad_low, head_rows(head_ref)) / CELLS
    weights = (dmix * alpha, dmix * (1.0 - alpha))
    for b in range(2):
        product = weights[b] * received[:, b * LANE : (b + 1) * LANE]
        plain = column_sum(jnp.where(once, product, 0.0))
        normal = column_sum(jnp.where(once, 0.0, product))
        means[2 * b : 2 * b + 1, :] = plain / cell_count
        means[2 * b + 1 : 2 * b + 2, :] = normal / cell_count
        rows_ref[b] = weights[b]
        small_ref[16 + 2 * b : 16 + 2 * b + 1, :] = plain
        small_ref[16 + 2 * b + 1 : 16 + 2 * b + 2, :] = normal
    rows_ref[2] = dmix
    cross = -jnp.sum(
        jnp.where(once, mask * jnp.sum(onehot * log_prob, axis=1, keepdims=True), 0.0), axis=0, keepdims=True
    )
    consistency = jnp.sum(
        jnp.where(once, jnp.sum(away * away, axis=1, keepdims=True), 0.0), axis=0, keepdims=True
    )
    lane_row = lax.broadcasted_iota(jnp.int32, (1, LANE), 1)
    small_ref[20:21, :] = jnp.where(
        lane_row == 0, cross, jnp.where(lane_row == 1, consistency, jnp.where(lane_row == 2, total, 0.0))
    )
    small_ref[21:24, :] = jnp.zeros((3, LANE), F32)
    pooled = jnp.where(once, 0.0, raw).astype(BF16)
    small_ref[0:16, :] = dot_rows(grad_low, pooled)[0:16, :]


def pack_grad(ref, blocks):
    side_by_side = jnp.concatenate(blocks + [jnp.zeros((CH, BLOCKS * LANE - WIDE), F32)], axis=1)
    for k in range(BLOCKS):
        ref[k * CH : (k + 1) * CH, :] = side_by_side[:, k * LANE : (k + 1) * LANE]


def keep_and_send(keep_ref, send_ref, blocks):
    view = lax.axis_index("view")
    for own, ref in ((0, keep_ref), (1, send_ref)):
        @pl.when(view == own)
        def _():
            pack_grad(ref, blocks[0])

        @pl.when(view != own)
        def _():
            pack_grad(ref, blocks[1])


def back_second_kernel(
    cell_count, all_images,
    second_ref, first_ref, recv1_ref, recv2_ref, recv3_ref, norm, head_ref, w_ref,
    du_ref, frames, msg_ref, small_ref, dmix_ref,
    terms1, terms2, rows_ref, means,
):
    rows = 2 * IMAGES
    norm_rows(total_of(recv1_ref), norm, terms1, 0, 0, cell_count)
    norm_rows(total_of(recv2_ref), norm, terms2, 0, 1, cell_count)
    loss_part(IMAGES, all_images, cell_count, recv3_ref, head_ref, rows_ref, means, small_ref)
    dmix_ref[...] = rows_ref[2, 0:rows, :]
    weights = [rows_ref[b, 0:rows, :] for b in range(2)]
    sums = [0.0] * 4
    carry = [blank_line()] * 2
    for b in range(2):
        clear_frame(frames.at[b])
    for step in range(STEPS):
        first_line, end = new_lines(step)
        for b in range(2):
            lanes = slice(b * LANE, (b + 1) * LANE)
            values = second_ref[first_line * LINE : end * LINE, lanes]
            half = values * term(terms2, b, 0) + term(terms2, b, 1)
            slope = silu_slope(half, jnp.tanh(half))
            normal = values * term(terms2, b, 2) + term(terms2, b, 3)
            dy = term(terms2, b, 4) * (
                per_image(slope, weights[b]) - means[2 * b : 2 * b + 1, :] - normal * means[2 * b + 1 : 2 * b + 2, :]
            )
            frame_line(frames.at[b], first_line, dy)
            dh, carry[b] = fold_lines(dot(taps(frames.at[b], step, (0, 1)), w_ref[b]), carry[b])
            before = first_ref[chunk_rows(step), lanes]
            half = before * term(terms1, b, 0) + term(terms1, b, 1)
            du = dh * silu_slope(half, jnp.tanh(half))
            du_ref[chunk_rows(step), lanes] = du
            normal = before * term(terms1, b, 2) + term(terms1, b, 3)
            sums[2 * b] += eight(du)
            sums[2 * b + 1] += eight(du * normal)
    spread_sums(msg_ref, sums)


def middle_lines(frame, first_line):
    return frame[first_line + 1 : first_line + 1 + DEEP, 1 : ACROSS + 1].reshape(CHUNK, frame.shape[-1])


def second_weight_kernel(frame_ref, dy_ref, keep_ref, send_ref, gacc):
    for b in range(2):
        for step in range(STEPS):
            pair = jnp.concatenate(
                [middle_lines(dy_ref.at[b], step * DEEP), middle_lines(dy_ref.at[b], step * DEEP + 1)], axis=1
            )
            product = dot_rows(pair, taps(frame_ref.at[b], step, (0, 1)))
            gacc[b] = product if step == 0 else gacc[b] + product
    blocks = []
    for b in range(2):
        blocks.append([])
        for tap in range(TAPS):
            ky, kx = tap // 3, tap % 3
            row = LANE if ky == 0 else 0
            lane = (ky // 2) * 3 * LANE + kx * LANE
            blocks[b].append(gacc[b, row : row + CH, lane : lane + CH])
    keep_and_send(keep_ref, send_ref, blocks)


def back_weight_kernel(
    cell_count,
    du_ref, first_ref, low_ref, recv1_ref, recv5_ref, norm, small_ref,
    frame_ref, keep_ref, send_ref,
    terms1, gacc,
):
    norm_rows(total_of(recv1_ref), norm, terms1, 0, 0, cell_count)
    sums = total_of(recv5_ref)
    for ref in (keep_ref, send_ref):
        ref[GRAD_ROWS : GRAD_ROWS + 24, :] = small_ref[...]
        ref[GRAD_ROWS + 24 :, :] = sums
    means = sums / cell_count
    clear_frame(frame_ref)
    for step in range(STEPS):
        parts = []
        for b in range(2):
            lanes = slice(b * LANE, (b + 1) * LANE)
            normal = first_ref[chunk_rows(step), lanes] * term(terms1, b, 2) + term(terms1, b, 3)
            parts.append(term(terms1, b, 4) * (
                du_ref[chunk_rows(step), lanes] - means[2 * b : 2 * b + 1, :] - normal * means[2 * b + 1 : 2 * b + 2, :]
            ))
        pair = jnp.concatenate(parts, axis=1)
        frame_line(frame_ref, step * DEEP, pair)
        product = dot_rows(pair.astype(BF16), taps(low_ref, step, (-1, 0, 1)))
        gacc[...] = product if step == 0 else gacc[...] + product
    keep_and_send(
        keep_ref, send_ref,
        [[gacc[b * LANE : b * LANE + CH, tap * LANE : tap * LANE + CH] for tap in range(TAPS)] for b in range(2)],
    )


def back_stem_kernel(frame_ref, moved_ref, dmix_ref, w_ref, stem_ref):
    carry = blank_line()
    total = 0.0
    for step in range(STEPS):
        dstem, carry = fold_lines(dot(taps(frame_ref, step, (0, 1)), w_ref[...]), carry)
        dstem = (dstem.reshape(CHUNK // 8, 8, LANE) + dmix_ref[...][None]).reshape(CHUNK, LANE)
        total += dot(image_taps(moved_ref, step * DEEP, DEEP), dstem.astype(BF16))
    rows = [total[stem_row(tap) : stem_row(tap) + 3, :] for tap in range(TAPS)]
    stem_ref[...] = jnp.concatenate(rows, axis=0)


def code(values):
    top = jnp.max(jnp.abs(values), axis=0, keepdims=True)
    power = jnp.clip(jnp.ceil(jnp.log2(jnp.maximum(top, 1e-30)) + 0.01), -100.0, 100.0)
    counted = jnp.round(values * (jnp.exp2(-power) * CODE_TOP))
    return counted, power


def unit(power):
    return jnp.exp2(power) * (1.0 / CODE_TOP)


def coded_rows(values, rows):
    counted, power = code(values)
    parts = [counted, power]
    if rows - values.shape[0] - 1:
        parts.append(jnp.zeros((rows - values.shape[0] - 1, LANE), F32))
    return jnp.concatenate(parts, axis=0).astype(jnp.int32).astype(jnp.int16)


def decoded(values, count):
    whole_part = values.astype(jnp.int32).astype(F32)
    return whole_part[:count] * unit(whole_part[count : count + 1])


def send_pieces(pieces, outs, shift, share_rows):
    ways = len(outs)
    mine = (lax.axis_index("dp") >> shift) & (ways - 1)
    piece = outs[0].shape[-2] // 2
    for offset, out in enumerate(outs):
        for high in range(out.shape[0]):
            for k in range(2):
                values = pieces[k, high * ways + (mine ^ offset), 0:share_rows, :]
                out[high, k * piece : (k + 1) * piece, :] = coded_rows(values, piece)


def encode_kernel(share_rows, keep2, recv2, keep1, recv1, *refs):
    outs, (total, pieces) = refs[:-2], refs[-2:]
    if total.shape[0] > GRAD_ROWS:
        total[GRAD_ROWS:, :] = jnp.zeros((total.shape[0] - GRAD_ROWS, LANE), F32)
    for k, (keep, recv) in enumerate(((keep1, recv1), (keep2, recv2))):
        total[0:GRAD_ROWS, :] = keep[0:GRAD_ROWS, :] + recv[0:GRAD_ROWS, :]
        for d in range(pieces.shape[1]):
            pieces[k, d, 0:share_rows, :] = total[d * share_rows : (d + 1) * share_rows, :]
    send_pieces(pieces, outs, 0, share_rows)


def summed(recv_refs, high, k, share_rows):
    piece = recv_refs[0].shape[-2] // 2
    value = decoded(recv_refs[0][high, k * piece : (k + 1) * piece, :], share_rows)
    for ref in recv_refs[1:]:
        value += decoded(ref[high, k * piece : (k + 1) * piece, :], share_rows)
    return value


def combine_kernel(share_rows, shift, recv_refs, *refs):
    outs, pieces = refs[:-1], refs[-1]
    for k in range(2):
        for high in range(pieces.shape[1]):
            pieces[k, high, 0:share_rows, :] = summed(recv_refs, high, k, share_rows)
    send_pieces(pieces, outs, shift, share_rows)


def middle_kernel(share_rows, recv_refs, stem_ref, out_ref):
    piece = recv_refs[0].shape[-2] // 2
    for k in range(2):
        out_ref[0, k * piece : (k + 1) * piece, :] = coded_rows(summed(recv_refs, 0, k, share_rows), piece)
    out_ref[0, 2 * piece :, :] = coded_rows(stem_ref[...], SIDE)


def stack_kernel(inner, parts, out_ref):
    count = parts[0].shape[0]
    for k, part in enumerate(parts):
        if inner:
            for entry in range(count):
                out_ref[entry * len(parts) + k] = part[entry]
        else:
            out_ref[k * count : (k + 1) * count] = part[...]


def adam_terms(gradient, factor, weight, first, second, teacher):
    clipped = gradient * factor
    first_new = BETA_FIRST * first + (1.0 - BETA_FIRST) * clipped
    second_new = BETA_SECOND * second + (1.0 - BETA_SECOND) * clipped * clipped
    first_hat = first_new / (1.0 - BETA_FIRST**STEP)
    second_hat = second_new / (1.0 - BETA_SECOND**STEP)
    weight_new = weight - LEARN_RATE * (
        first_hat / (jnp.sqrt(second_hat) + ADAM_EPS) + WEIGHT_DECAY * weight
    )
    return weight_new, first_new, second_new, TEACHER_KEEP * teacher + (1.0 - TEACHER_KEEP) * weight_new


def update_kernel(
    share_rows, own_codes, other_codes, own_facts, other_facts,
    cw, cf, cs, ct, sw, sf, ss, st, hw, hf, hs, ht, nw, nf, ns, nt,
    cw_o, cf_o, cs_o, ct_o, cb_o, sw_o, sf_o, ss_o, st_o, sb_o, hw_o, hf_o, hs_o, ht_o, hb_o,
    nw_o, nf_o, ns_o, nt_o, norm_o, cross_o, count_o, consistency_o,
    factor_ref, own_ref, other_ref, codes,
):
    conv = pl.program_id(0)
    view = lax.axis_index("view")

    @pl.when(conv == 0)
    def _():
        facts = own_facts[...] + other_facts[...]
        small, sums = facts[:24], facts[24:]
        piece = (codes.shape[-2] - SIDE) // 2
        ways, groups = codes.shape[:2]
        dp_index = lax.axis_index("dp")
        stem = jnp.zeros((27, LANE), F32)
        for sources, ref in ((own_codes, own_ref), (other_codes, other_ref)):
            for k, source in enumerate(sources):
                codes[k] = source[...]
            for d in range(ways * groups):
                offset = dp_index ^ d
                low, high = offset & (ways - 1), offset // ways
                for k in range(2):
                    ref[k, d * share_rows : (d + 1) * share_rows, :] = decoded(
                        codes[low, high, k * piece : (k + 1) * piece, :], share_rows
                    )
                stem += decoded(codes[low, high, 2 * piece :, :], 27)
        stem = stem[:, :CH]
        head = small[:CLASSES, :CH]
        gains = jnp.concatenate([sums[1:2], small[17:18], sums[3:4], small[19:20]], axis=0)[:, :CH]
        shifts = jnp.concatenate([sums[0:1], small[16:17], sums[2:3], small[18:19]], axis=0)[:, :CH]
        total = jnp.zeros((1, 1), F32)
        for part in (stem, head, gains, shifts):
            total += jnp.sum(jnp.sum(part * part, axis=1, keepdims=True), axis=0, keepdims=True)
        for ref in (own_ref, other_ref):
            for k in range(2):
                values = ref[k, 0:GRAD_ROWS, :]
                column = jnp.sum(values * values, axis=0, keepdims=True)
                total += jnp.sum(column, axis=1, keepdims=True)
        norm = jnp.sqrt(total)
        factor = CLIP_LIMIT / jnp.maximum(norm, CLIP_LIMIT)
        factor_ref[...] = jnp.broadcast_to(factor, factor_ref.shape)
        norm_o[...] = norm
        cross_o[...] = small[20:21, 0:1]
        consistency_o[...] = small[20:21, 1:2]
        count_o[...] = own_facts[20:21, 2:3]
        sw_o[...], sf_o[...], ss_o[...], st_o[...] = adam_terms(stem, factor, sw[...], sf[...], ss[...], st[...])
        sb_o[...] = sw_o[...].astype(BF16)
        hw_o[...], hf_o[...], hs_o[...], ht_o[...] = adam_terms(head, factor, hw[...], hf[...], hs[...], ht[...])
        hb_o[...] = hw_o[...].astype(BF16)
        for k, part in enumerate((gains, shifts)):
            nw_o[k], nf_o[k], ns_o[k], nt_o[k] = adam_terms(part, factor, nw[k], nf[k], ns[k], nt[k])

    def update(ref, second):
        blocks = [ref[second, k * CH : (k + 1) * CH, :] for k in range(BLOCKS)]
        gradient = jnp.concatenate(blocks, axis=1)[:, :WIDE]
        weight, first, second_moment, teacher = adam_terms(
            gradient, factor_ref[0:1, 0:1], cw[...], cf[...], cs[...], ct[...]
        )
        cw_o[...] = weight
        cf_o[...] = first
        cs_o[...] = second_moment
        ct_o[...] = teacher
        cb_o[...] = weight.astype(BF16)

    mine = conv // 2 == view

    @pl.when(mine)
    def _():
        update(own_ref, conv & 1)

    @pl.when(jnp.logical_not(mine))
    def _():
        update(other_ref, conv & 1)


def whole(shape):
    return pl.BlockSpec(shape, lambda i: (0,) * len(shape))


def scalars():
    return pl.BlockSpec(memory_space=pltpu.SMEM)


def conv_part(k):
    return pl.BlockSpec((None, CH, WIDE), lambda i: (k, 0, 0))


def held():
    return pl.BlockSpec(memory_space=pltpu.VMEM)


def hold(values):
    return pltpu.with_memory_space_constraint(values, pltpu.VMEM)


def struct(shape, kind=F32):
    return jax.ShapeDtypeStruct(shape, kind)


def from_partners(values, shift, ways):
    size = lax.axis_size("dp")
    return [values] + [
        lax.ppermute(values, "dp", [(i, i ^ (offset << shift)) for i in range(size)]) for offset in range(1, ways)
    ]


def stages():
    size = lax.axis_size("dp")
    groups = []
    shift = 0
    while (1 << shift) < size:
        ways = min(4, size >> shift)
        groups.append((shift, ways))
        shift += 2
    return groups


def sum_parts(values):
    groups = stages()
    for shift, ways in groups[:-1]:
        values = sum(from_partners(values, shift, ways))
    return tuple(from_partners(values, *groups[-1]))


def stack(parts, inner):
    shape = (len(parts) * parts[0].shape[0],) + parts[0].shape[1:]
    return pl.pallas_call(
        functools.partial(stack_kernel, inner), out_shape=struct(shape, parts[0].dtype), compiler_params=PARAMS, name="stack"
    )(tuple(parts))


def gather_parts(values, groups):
    inner = groups[0][0] > 0
    for shift, ways in groups[:-1]:
        values = stack(from_partners(values, shift, ways), inner)
    return tuple(from_partners(values, *groups[-1]))


def swap_view(values):
    return lax.ppermute(values, "view", [(0, 1), (1, 0)])


def forward_weights(conv):
    shape = (2, 6 * LANE, 2 * LANE)
    return pl.pallas_call(
        forward_weight_kernel,
        grid=(2,),
        in_specs=[pl.BlockSpec((None, CH, WIDE), lambda i: (2 * i + 1, 0, 0))],
        out_specs=pl.BlockSpec((None,) + shape[1:], lambda i: (i, 0, 0)),
        out_shape=struct(shape, BF16),
        compiler_params=PARAMS,
        cost_estimate=pl.CostEstimate(flops=2_000_000_000, bytes_accessed=4_000_000, transcendentals=0),
        name="forward_weight",
    )(conv)


def backward_weights(conv):
    return pl.pallas_call(
        backward_weight_kernel,
        grid=(1,),
        in_specs=[conv_part(k) for k in range(4)],
        out_specs=[whole((2, 6 * LANE, 2 * LANE)), whole((12 * LANE, 2 * LANE))],
        out_shape=[struct((2, 6 * LANE, 2 * LANE), BF16), struct((12 * LANE, 2 * LANE), BF16)],
        compiler_params=PARAMS,
        cost_estimate=pl.CostEstimate(flops=4_000_000_000, bytes_accessed=8_000_000, transcendentals=0),
        name="backward_weight",
    )(conv, conv, conv, conv)


def shards(
    augmented, shake_ratio, labels, labelled, view_order,
    stem_weight, conv_weight, head_weight, norm_param,
    teacher_stem, teacher_conv, teacher_head, teacher_norm,
    first_stem, first_conv, first_head, first_norm,
    second_stem, second_conv, second_head, second_norm,
):
    dp = lax.axis_size("dp")
    all_images = IMAGES * dp
    cell_count = float(all_images * CELLS)
    rows = dp * 2 * IMAGES
    share_rows = -(-GRAD_ROWS // dp)
    piece = -(-(share_rows + 1) // 16) * 16
    conv, conv_t, conv_f, conv_s = (
        jnp.transpose(v, (0, 2, 1)) for v in (conv_weight, teacher_conv, first_conv, second_conv)
    )
    head, head_t, head_f, head_s = (v.T for v in (head_weight, teacher_head, first_head, second_head))
    pixels = jnp.transpose(augmented[0], (0, 3, 1, 2))
    msg = struct((8, LANE))
    groups = stages()
    last_ways = groups[-1][1]
    recv_spec = (held(),) * last_ways
    norm_spec = whole((2, 4, CH))
    head_spec = whole((CLASSES, CH))
    moved_shape = (3, (SIDE + 4) * 8, LANE)
    frame_one, frame_two, frame_pair = FRAME + (LANE,), (2,) + FRAME + (LANE,), FRAME + (2 * LANE,)
    values_shape, grad_shape = (ALL, 2 * LANE), struct((GRAD_ROWS, LANE))
    terms_scratch = pltpu.VMEM((16, LANE), F32)

    first_s, first_t, low, moved, stem_sums, message = pl.pallas_call(
        first_kernel,
        in_specs=[pl.BlockSpec(memory_space=pltpu.HBM)] * 5,
        out_specs=[held()] * 6,
        out_shape=[
            pltpu.VMEM(values_shape, F32), pltpu.VMEM(values_shape, F32), pltpu.VMEM(frame_one, BF16),
            pltpu.VMEM(moved_shape, F32), struct((2, 8, LANE)), msg,
        ],
        scratch_shapes=[
            pltpu.VMEM(moved_shape[1:], F32), pltpu.VMEM((STEM_ROWS, 2 * LANE), F32),
            pltpu.VMEM((STEM_ROWS, 2 * LANE), BF16), pltpu.VMEM((2, 9 * LANE, 2 * LANE), BF16),
            pltpu.VMEM(frame_one, BF16), pltpu.VMEM((IMAGES, 3, SIDE, SIDE), BF16), pltpu.VMEM((27, CH), F32),
            pltpu.VMEM((27, CH), F32), pltpu.VMEM((4, CH, WIDE), F32), pltpu.SemaphoreType.DMA((7,)),
        ],
        compiler_params=PARAMS,
        name="first_conv",
    )(*(pltpu.with_memory_space_constraint(v, pltpu.HBM) for v in (pixels, stem_weight, teacher_stem, conv, conv_t)))
    first_s, first_t, low, moved = (hold(v) for v in (first_s, first_t, low, moved))
    recv1 = sum_parts(message)
    weight_s, weight_t = forward_weights(conv), forward_weights(conv_t)

    second_s, second_t, hidden, message = pl.pallas_call(
        functools.partial(second_kernel, cell_count),
        in_specs=[held()] * 2 + [recv_spec] + [held()] * 4,
        out_specs=[held()] * 4,
        out_shape=[
            pltpu.VMEM(values_shape, F32), pltpu.VMEM(values_shape, F32), pltpu.VMEM(frame_two, BF16), msg,
        ],
        scratch_shapes=[pltpu.VMEM(frame_two, BF16), terms_scratch, terms_scratch],
        compiler_params=PARAMS,
        name="second_conv",
    )(first_s, first_t, recv1, norm_param, teacher_norm, weight_s, weight_t)
    second_s, second_t, hidden = (hold(v) for v in (second_s, second_t, hidden))
    recv2 = sum_parts(message)

    prob = pl.pallas_call(
        functools.partial(teacher_kernel, cell_count),
        in_specs=[scalars(), held(), recv_spec] + [held()] * 3,
        out_specs=held(),
        out_shape=struct((8, LANE)),
        scratch_shapes=[terms_scratch],
        compiler_params=PARAMS,
        name="teacher_logits",
    )(shake_ratio, second_t, recv2, teacher_norm, head_t, stem_sums)
    prob, conv_later = lax.optimization_barrier((prob, conv))
    other = swap_view(prob)
    back_weight_two, back_weight_one = backward_weights(conv_later)
    other, back_weight_two = lax.optimization_barrier((other, back_weight_two))
    facts = pl.pallas_call(
        functools.partial(student_kernel, cell_count),
        in_specs=[scalars()] * 4 + [held(), recv_spec] + [held()] * 4,
        out_specs=held(),
        out_shape=struct((8, 3 * LANE)),
        scratch_shapes=[terms_scratch],
        compiler_params=PARAMS,
        cost_estimate=pl.CostEstimate(flops=4_000_000_000, bytes_accessed=8_000_000, transcendentals=0),
        name="student_logits",
    )(shake_ratio, labels, labelled, view_order, second_s, recv2, norm_param, head, stem_sums, other)
    recv3 = gather_parts(facts.reshape(1, 8, 3 * LANE), groups)

    du, dy, message, small, dmix = pl.pallas_call(
        functools.partial(back_second_kernel, cell_count, float(all_images)),
        in_specs=[held()] * 2 + [recv_spec] * 3 + [held()] * 3,
        out_specs=[held()] * 5,
        out_shape=[
            pltpu.VMEM(values_shape, F32), pltpu.VMEM(frame_two, BF16), msg, struct((24, LANE)), struct((8, LANE)),
        ],
        scratch_shapes=[
            terms_scratch, terms_scratch, pltpu.VMEM((3, rows, LANE), F32), pltpu.VMEM((8, LANE), F32),
        ],
        compiler_params=PARAMS,
        name="back_second",
    )(second_s, first_s, recv1, recv2, recv3, norm_param, head, back_weight_two)
    du, dy = hold(du), hold(dy)
    recv5 = sum_parts(message)
    keep2, send2 = pl.pallas_call(
        second_weight_kernel,
        in_specs=[held()] * 2,
        out_specs=[held()] * 2,
        out_shape=[grad_shape] * 2,
        scratch_shapes=[pltpu.VMEM((2, 2 * LANE, 6 * LANE), F32)],
        compiler_params=PARAMS,
        cost_estimate=pl.CostEstimate(flops=8_000_000_000, bytes_accessed=16_000_000, transcendentals=0),
        name="second_weight",
    )(hidden, dy)
    recv_grad2 = swap_view(send2)

    frame, keep1, send1 = pl.pallas_call(
        functools.partial(back_weight_kernel, cell_count),
        in_specs=[held()] * 3 + [recv_spec] * 2 + [held()] * 2,
        out_specs=[held()] * 3,
        out_shape=[pltpu.VMEM(frame_pair, BF16)] + [struct((GRAD_ROWS + 32, LANE))] * 2,
        scratch_shapes=[terms_scratch, pltpu.VMEM((2 * LANE, 9 * LANE), F32)],
        compiler_params=PARAMS,
        cost_estimate=pl.CostEstimate(flops=8_000_000_000, bytes_accessed=16_000_000, transcendentals=0),
        name="back_weight",
    )(du, first_s, low, recv1, recv5, norm_param, small)
    frame = hold(frame)
    recv_grad1 = swap_view(send1)
    def code_shapes(group):
        shift, ways = group
        return [struct(((dp >> shift) // ways, 2 * piece, LANE), jnp.int16)] * ways

    def piece_scratch(count):
        return pltpu.VMEM((2, count, piece, LANE), F32)

    coded = pl.pallas_call(
        functools.partial(encode_kernel, share_rows),
        out_shape=code_shapes(groups[0]),
        scratch_shapes=[pltpu.VMEM((max(dp * share_rows, GRAD_ROWS), LANE), F32), piece_scratch(dp)],
        compiler_params=PARAMS,
        name="encode",
    )(keep2, recv_grad2, keep1, recv_grad1)

    def to_partners(values, group):
        shift, ways = group
        return (values[0],) + tuple(
            lax.ppermute(values[offset], "dp", [(i, i ^ (offset << shift)) for i in range(dp)])
            for offset in range(1, ways)
        )

    scattered = to_partners(coded, groups[0])

    stem_grad = pl.pallas_call(
        back_stem_kernel,
        in_specs=[held()] * 4,
        out_specs=held(),
        out_shape=struct((27, LANE)),
        compiler_params=PARAMS,
        cost_estimate=pl.CostEstimate(flops=8_000_000_000, bytes_accessed=16_000_000, transcendentals=0),
        name="back_stem",
    )(frame, moved, dmix, back_weight_one)

    for group in groups[1:]:
        coded = pl.pallas_call(
            functools.partial(combine_kernel, share_rows, group[0]),
            out_shape=code_shapes(group),
            scratch_shapes=[piece_scratch(dp >> group[0])],
            compiler_params=PARAMS,
            name="combine",
        )(scattered)
        scattered = to_partners(coded, group)
    parts = pl.pallas_call(
        functools.partial(middle_kernel, share_rows),
        out_shape=struct((1, 2 * piece + SIDE, LANE), jnp.int16),
        compiler_params=PARAMS,
        name="middle",
    )(scattered, stem_grad)
    own = gather_parts(parts, groups[::-1])
    other_grads = tuple(swap_view(part) for part in own)

    conv_block = pl.BlockSpec((None, CH, WIDE), lambda i: (i, 0, 0))
    stem_block, norm_block = whole((27, CH)), norm_spec
    last_ways = groups[0][1]
    codes_shape = (dp // last_ways, 2 * piece + SIDE, LANE)
    code_spec = (whole(codes_shape),) * last_ways
    facts_spec = pl.BlockSpec((32, LANE), lambda i: (GRAD_ROWS // 32, 0))
    grads_scratch = pltpu.VMEM((2, max(dp * share_rows, GRAD_ROWS), LANE), F32)
    outs = pl.pallas_call(
        functools.partial(update_kernel, share_rows),
        grid=(4,),
        in_specs=[code_spec] * 2 + [facts_spec] * 2
        + [conv_block] * 4 + [stem_block] * 4 + [head_spec] * 4 + [norm_block] * 4,
        out_specs=[conv_block] * 5 + [stem_block] * 5 + [head_spec] * 5 + [norm_block] * 4 + [whole((1, 1))] * 4,
        out_shape=[struct((4, CH, WIDE))] * 4 + [struct((4, CH, WIDE), BF16)]
        + [struct((27, CH))] * 4 + [struct((27, CH), BF16)]
        + [struct((CLASSES, CH))] * 4 + [struct((CLASSES, CH), BF16)]
        + [struct((2, 4, CH))] * 4 + [struct((1, 1))] * 4,
        scratch_shapes=[pltpu.VMEM((8, LANE), F32), grads_scratch, grads_scratch,
            pltpu.VMEM((last_ways,) + codes_shape, jnp.int16)],
        compiler_params=PARAMS,
        name="update",
    )(
        own, other_grads, keep1, recv_grad1,
        conv, conv_f, conv_s, conv_t, stem_weight, first_stem, second_stem, teacher_stem,
        head, head_f, head_s, head_t, norm_param, first_norm, second_norm, teacher_norm,
    )
    convs = [jnp.transpose(v, (0, 2, 1)) for v in outs[:5]]
    stems = outs[5:10]
    heads = [v.T for v in outs[10:15]]
    norms = outs[15:19]
    return (
        *(v.reshape(()) for v in outs[19:23]),
        *stems[:4], *convs[:4], *heads[:4], *norms, stems[4], convs[4], heads[4],
    )


def solution(mesh):
    in_specs = (
        (P("view", "dp", None, None, None), P("view", "dp"), P("dp"), P("dp")) + (P(),) * 17
    )
    return jax.shard_map(shards, mesh=mesh, in_specs=in_specs, out_specs=(P(),) * 23, check_vma=False)
```

```python
import functools

import jax
import jax.numpy as jnp
from jax import lax
from jax.experimental import pallas as pl
from jax.experimental.pallas import tpu as pltpu
from jax.sharding import PartitionSpec as P

CLASSES = 10
STEP = 5
EPS_NORM = 1e-05
LEARN_RATE = 0.03
BETA_FIRST = 0.5
BETA_SECOND = 0.5
WEIGHT_DECAY = 0.0001
ADAM_EPS = 1e-08
CLIP_LIMIT = 0.02
TEACHER_KEEP = 0.9
CONS_WEIGHT = 10.0

F32 = jnp.float32
BF16 = jnp.bfloat16
LANE = 128
CH = 96
SIDE = 32
CELLS = SIDE * SIDE
IMAGES = 4
QUARTERS = 4
ACROSS = SIDE // QUARTERS
TILE = IMAGES * QUARTERS
LINE = ACROSS * TILE
STEPS = 4
DEEP = SIDE // STEPS
CHUNK = DEEP * LINE
ALL = SIDE * LINE
BLOCK = 64
TAPS = 9
WIDE = TAPS * CH
BLOCKS = -(-WIDE // LANE)
GRAD_ROWS = BLOCKS * CH
SHARE = GRAD_ROWS // QUARTERS
PIECE = -(-(SHARE + 1) // 16) * 16
CODE_ROWS = 2 * PIECE + SIDE
STEM_ROWS = 80
CODE_TOP = 32000.0
FRAME = (SIDE + 2, ACROSS + 2, TILE)
PARAMS = pltpu.CompilerParams(vmem_limit_bytes=24 * 1024 * 1024)


def dot(a, b):
    return jnp.dot(a, b, preferred_element_type=F32)


def dot_rows(a, b):
    return lax.dot_general(a, b, (((0,), (0,)), ((), ())), preferred_element_type=F32)


def dot_lanes(a, b):
    return lax.dot_general(a, b, (((1,), (1,)), ((), ())), preferred_element_type=F32)


def frame_line(frame, first_line, values):
    lines = values.shape[0] // LINE
    width = values.shape[1]
    tiles = values.reshape(lines, ACROSS, TILE, width)
    row = lax.broadcasted_iota(jnp.int32, (1, TILE, 1), 1)
    before = jnp.where(row >= IMAGES, pltpu.roll(tiles[:, ACROSS - 1], IMAGES, 1), 0.0)
    after = jnp.where(row < TILE - IMAGES, pltpu.roll(tiles[:, 0], TILE - IMAGES, 1), 0.0)
    place = slice(first_line + 1, first_line + 1 + lines)
    frame[place, 1 : ACROSS + 1] = tiles.astype(BF16)
    frame[place, 0] = before.astype(BF16)
    frame[place, ACROSS + 1] = after.astype(BF16)


def clear_frame(frame):
    blank = jnp.zeros(frame.shape[1:], BF16)
    frame[0] = blank
    frame[SIDE + 1] = blank


def taps(frame, step, rows):
    parts = []
    for dy in rows:
        for kx in range(3):
            place = step * DEEP + 1 + dy
            lines = frame[place : place + DEEP, kx : kx + ACROSS]
            parts.append(lines.reshape(CHUNK, lines.shape[-1]))
    return jnp.concatenate(parts, axis=1)


def fold_lines(both, carry):
    upper = jnp.concatenate([carry, both[: CHUNK - LINE, LANE:]], axis=0)
    return both[:, :LANE] + upper, both[CHUNK - LINE :, LANE:]


def blank_line():
    return jnp.zeros((LINE, LANE), F32)


def new_lines(step):
    first = 0 if step == 0 else step * DEEP + 1
    return first, min((step + 1) * DEEP + 1, SIDE)


def chunk_rows(step):
    return slice(step * CHUNK, (step + 1) * CHUNK)


def eight(values):
    parts = values.reshape(values.shape[0] // 8, 8, values.shape[1])
    while parts.shape[0] > 1:
        middle = parts.shape[0] // 2
        rest = parts[2 * middle :]
        parts = parts[:middle] + parts[middle : 2 * middle]
        if rest.shape[0]:
            parts = jnp.concatenate([parts[:-1], parts[-1:] + rest], axis=0) if middle > 1 else parts + rest
    return parts[0]


def both_halves(sums):
    return sums + pltpu.roll(sums, IMAGES, 0)


def tap_block(raw, tap):
    return raw[:, tap * CH : (tap + 1) * CH]


def image_lines(image_ref, plain, moved):
    plain[...] = jnp.zeros(plain.shape, F32)
    for channel in range(3):
        side_by_side = jnp.concatenate([image_ref[i, channel].astype(F32) for i in range(IMAGES)], axis=1)
        plain[pl.ds(8 + channel, SIDE, stride=8), :] = side_by_side
    source = lax.broadcasted_iota(jnp.int32, (LANE, LANE), 0)
    target = lax.broadcasted_iota(jnp.int32, (LANE, LANE), 1)
    same = source // SIDE == (target & (IMAGES - 1))
    across = ((target // IMAGES) & (QUARTERS - 1)) * ACROSS + target // TILE
    for kx in range(3):
        picks = jnp.where(same & ((source & (SIDE - 1)) == across + (kx - 1)), 1.0, 0.0).astype(BF16)
        moved[kx] = dot(plain[...].astype(BF16), picks)


def image_taps(moved, first_line, lines):
    columns = []
    for line in range(lines):
        place = (first_line + line) * 8
        parts = [moved[kx, place : place + 24, :] for kx in range(3)]
        columns.append(jnp.concatenate(parts + [jnp.zeros((8, LANE), F32)], axis=0))
    return jnp.concatenate(columns, axis=1).astype(BF16)


def stem_row(tap):
    return (tap % 3) * 24 + (tap // 3) * 8


def pad_lanes(row):
    return jnp.concatenate([row, jnp.zeros((row.shape[0], LANE - row.shape[1]), row.dtype)], axis=1)


def norm_terms(sums, squares, cell_count):
    average = sums / cell_count
    inverse = lax.rsqrt(squares / cell_count - average * average + EPS_NORM)
    return average, inverse


def column_sum(values):
    return jnp.sum(values, axis=0, keepdims=True)


def slope_rest(half, tanh, product):
    return (tanh + half) - product * tanh


def first_kernel(
    image_hbm, stem_s_hbm, stem_t_hbm, raw_s, raw_t,
    first_s, first_t, frame_s, moved_ref, pooled_ref, msg_ref,
    plain, wst32, wst, wf, frame_t, image_ref, stem_s, stem_t, raw, sems,
):
    coming = [
        pltpu.make_async_copy(source, target, sems.at[k])
        for k, (source, target) in enumerate((
            (image_hbm, image_ref), (stem_s_hbm, stem_s), (stem_t_hbm, stem_t),
            (raw_s.at[0], raw.at[0]), (raw_s.at[2], raw.at[1]), (raw_t.at[0], raw.at[2]), (raw_t.at[2], raw.at[3]),
        ))
    ]
    for copy in coming:
        copy.start()
    wf[...] = jnp.zeros(wf.shape, BF16)
    wst32[...] = jnp.zeros(wst32.shape, F32)
    clear_frame(frame_s)
    clear_frame(frame_t)
    for copy in coming[:3]:
        copy.wait()
    image_lines(image_ref, plain, moved_ref)
    for n, stem in enumerate((stem_s, stem_t)):
        for tap in range(TAPS):
            row = stem_row(tap)
            wst32[row : row + 3, n * LANE : n * LANE + CH] = stem[3 * tap : 3 * tap + 3, :]
    wst[...] = wst32[...].astype(BF16)
    for copy in coming[3:]:
        copy.wait()
    for n in range(2):
        for b in range(2):
            for tap in range(TAPS):
                wf[n, tap * LANE : tap * LANE + CH, b * LANE : b * LANE + CH] = jnp.transpose(
                    tap_block(raw.at[2 * n + b], tap)
                ).astype(BF16)
    pooled = [0.0, 0.0]
    sums = [0.0] * 8
    for step in range(STEPS):
        first_line, end = new_lines(step)
        stems = dot_rows(image_taps(moved_ref, first_line, end - first_line), wst[...])
        for n, (frame, out_ref) in enumerate(((frame_s, first_s), (frame_t, first_t))):
            stem = stems[:, n * LANE : (n + 1) * LANE]
            pooled[n] += eight(stem)
            frame_line(frame, first_line, stem)
            out = dot(taps(frame, step, (-1, 0, 1)), wf[n])
            out_ref[chunk_rows(step), :] = out
            for b in range(2):
                part = out[:, b * LANE : (b + 1) * LANE]
                sums[4 * n + 2 * b] += eight(part)
                sums[4 * n + 2 * b + 1] += eight(part * part)
    for n in range(2):
        pooled_ref[n] = both_halves(pooled[n])
    spread_sums(msg_ref, sums)


def total_of(refs):
    total = refs[0][...]
    for ref in refs[1:]:
        total = total + ref[...]
    return total


def spread_sums(msg_ref, sums):
    sums = [column_sum(part) for part in sums]
    if len(sums) < 8:
        sums.append(jnp.zeros((8 - len(sums), LANE), F32))
    msg_ref[...] = jnp.concatenate(sums, axis=0)


def forward_weight_kernel(raw_ref, w_ref):
    w_ref[...] = jnp.zeros(w_ref.shape, BF16)
    for ky in range(3):
        for kx in range(3):
            row = (ky // 2) * 3 * LANE + kx * LANE
            lane = LANE if ky == 0 else 0
            w_ref[row : row + CH, lane : lane + CH] = jnp.transpose(tap_block(raw_ref, ky * 3 + kx)).astype(BF16)


def backward_weight_kernel(cw0, cw1, cw2, cw3, two_ref, one_ref):
    two_ref[...] = jnp.zeros(two_ref.shape, BF16)
    one_ref[...] = jnp.zeros(one_ref.shape, BF16)
    for ky in range(3):
        for kx in range(3):
            tap = (2 - ky) * 3 + 2 - kx
            lane = LANE if ky == 0 else 0
            for b, (inner, outer) in enumerate(((cw0, cw1), (cw2, cw3))):
                row = (ky // 2) * 3 * LANE + kx * LANE
                two_ref[b, row : row + CH, lane : lane + CH] = (0.5 * tap_block(outer, tap)).astype(BF16)
                one_ref[b, row : row + CH, lane : lane + CH] = tap_block(inner, tap).astype(BF16)


def norm_rows(sums, norm, terms, first_row, norm_index, cell_count):
    for b in range(2):
        row = first_row + 2 * b
        average, inverse = norm_terms(sums[row : row + 1], sums[row + 1 : row + 2], cell_count)
        gain = pad_lanes(norm[0, 2 * b + norm_index : 2 * b + norm_index + 1, :])
        shift = pad_lanes(norm[1, 2 * b + norm_index : 2 * b + norm_index + 1, :])
        scale = inverse * gain
        terms[8 * b : 8 * b + 1, :] = 0.5 * scale
        terms[8 * b + 1 : 8 * b + 2, :] = 0.5 * (shift - average * scale)
        terms[8 * b + 2 : 8 * b + 3, :] = inverse
        terms[8 * b + 3 : 8 * b + 4, :] = -average * inverse
        terms[8 * b + 4 : 8 * b + 5, :] = scale


def term(terms, b, k):
    return terms[8 * b + k : 8 * b + k + 1, :]


def second_kernel(
    cell_count, first_s, first_t, recv_ref, norm_s, norm_t, ws_ref, wt_ref,
    second_s, second_t, frame_s, bent_ref, msg_ref,
    frame_t, terms_s, terms_t,
):
    received = total_of(recv_ref)
    norm_rows(received, norm_s, terms_s, 0, 0, cell_count)
    norm_rows(received, norm_t, terms_t, 4, 0, cell_count)
    nets = ((first_s, terms_s, frame_s, ws_ref, second_s), (first_t, terms_t, frame_t, wt_ref, second_t))
    sums = [0.0] * 8
    carry = [blank_line()] * 4
    for _, _, frames, _, _ in nets:
        for b in range(2):
            clear_frame(frames.at[b])
    for step in range(STEPS):
        first_line, end = new_lines(step)
        for n, (source, terms, frames, w, target) in enumerate(nets):
            for b in range(2):
                k = 2 * n + b
                lanes = slice(b * LANE, (b + 1) * LANE)
                half = source[first_line * LINE : end * LINE, lanes] * term(terms, b, 0) + term(terms, b, 1)
                tanh = jnp.tanh(half)
                product = half * tanh
                frame_line(frames.at[b], first_line, half + product)
                if n == 0:
                    bent_ref[first_line * LINE : end * LINE, lanes] = slope_rest(half, tanh, product)
                out, carry[k] = fold_lines(dot(taps(frames.at[b], step, (0, 1)), w[b]), carry[k])
                target[chunk_rows(step), lanes] = out
                sums[2 * k] += eight(out)
                sums[2 * k + 1] += eight(out * out)
    spread_sums(msg_ref, sums)


def head_rows(head_ref):
    padded = jnp.concatenate([head_ref[...], jnp.zeros((LANE - CLASSES, CH), F32)], axis=0)
    return pad_lanes(padded).astype(BF16)


def alpha_of(ratio_ref, image):
    return (ratio_ref[0, image].astype(F32) + 1.0) / 18.0


def alpha_rows(ratio_ref):
    row = lax.broadcasted_iota(jnp.int32, (2 * IMAGES, LANE), 0) & (IMAGES - 1)
    alpha = jnp.zeros((2 * IMAGES, LANE), F32)
    for k in range(IMAGES):
        alpha = jnp.where(row == k, alpha_of(ratio_ref, k), alpha)
    return alpha


def class_lanes(rows):
    return lax.broadcasted_iota(jnp.int32, (rows, LANE), 1) < CLASSES


def log_softmax(logits, valid):
    top = jnp.max(jnp.where(valid, logits, -3e38), axis=1, keepdims=True)
    moved = logits - top
    total = jnp.sum(jnp.where(valid, jnp.exp(moved), 0.0), axis=1, keepdims=True)
    return moved - jnp.log(total)


def pooled_low(ratio_ref, sums, stem_sums):
    alpha = alpha_rows(ratio_ref)
    total = alpha * both_halves(sums[0]) + (1.0 - alpha) * both_halves(sums[1])
    return ((total + stem_sums) / CELLS).astype(BF16)


def teacher_kernel(
    cell_count, ratio_ref, second_ref, recv_ref, norm, head_ref, stem_sum_ref,
    prob_ref,
    terms,
):
    norm_rows(total_of(recv_ref), norm, terms, 4, 1, cell_count)
    plain, curved = [0.0] * 2, [0.0] * 2
    for block in range(ALL // BLOCK):
        for b in range(2):
            values = second_ref[block * BLOCK : (block + 1) * BLOCK, b * LANE : (b + 1) * LANE]
            half = values * term(terms, b, 0) + term(terms, b, 1)
            plain[b] += eight(values)
            curved[b] += eight(half * jnp.tanh(half))
    sums = [plain[b] * term(terms, b, 0) + (CELLS // 2) * term(terms, b, 1) + curved[b] for b in range(2)]
    low = pooled_low(ratio_ref, sums, stem_sum_ref[1])
    logits = dot_lanes(low, head_rows(head_ref))
    valid = class_lanes(2 * IMAGES)
    first_rows = lax.broadcasted_iota(jnp.int32, (2 * IMAGES, LANE), 0) < IMAGES
    prob = jnp.where(valid & first_rows, jnp.exp(log_softmax(logits, valid)), 0.0)
    prob_ref[...] = pltpu.roll(prob.astype(BF16).astype(F32), 16, 1)


def student_kernel(
    cell_count, ratio_ref, labels_ref, labelled_ref, order_ref,
    second_ref, recv_ref, norm, head_ref, stem_sum_ref, prob_ref,
    msg_ref, bent_ref,
    terms,
):
    norm_rows(total_of(recv_ref), norm, terms, 0, 1, cell_count)
    plain, curved, bent, bent_values = ([0.0] * 2 for _ in range(4))
    for block in range(ALL // BLOCK):
        for b in range(2):
            values = second_ref[block * BLOCK : (block + 1) * BLOCK, b * LANE : (b + 1) * LANE]
            half = values * term(terms, b, 0) + term(terms, b, 1)
            tanh = jnp.tanh(half)
            product = half * tanh
            slope = slope_rest(half, tanh, product)
            bent_ref[block * BLOCK : (block + 1) * BLOCK, b * LANE : (b + 1) * LANE] = slope
            plain[b] += eight(values)
            curved[b] += eight(product)
            bent[b] += eight(slope)
            bent_values[b] += eight(slope * values)
    cells = CELLS // 2
    sums = [plain[b] * term(terms, b, 0) + cells * term(terms, b, 1) + curved[b] for b in range(2)]
    slopes = [0.5 * (cells + bent[b]) for b in range(2)]
    sums += slopes
    sums += [
        term(terms, b, 2) * (0.5 * (plain[b] + bent_values[b])) + term(terms, b, 3) * slopes[b] for b in range(2)
    ]
    dp_index = lax.axis_index("dp")
    low = pooled_low(ratio_ref, sums, stem_sum_ref[0])
    logits = dot_lanes(low, head_rows(head_ref))
    rows = 2 * IMAGES
    info = jnp.where(class_lanes(rows), logits, 0.0)
    lane = lax.broadcasted_iota(jnp.int32, (rows, LANE), 1)
    row = lax.broadcasted_iota(jnp.int32, (rows, LANE), 0)
    for k in range(IMAGES):
        facts = (
            alpha_of(ratio_ref, k),
            labels_ref[k].astype(F32),
            labelled_ref[k].astype(F32),
            order_ref[dp_index * IMAGES + k].astype(F32),
        )
        for place, fact in enumerate(facts):
            info = jnp.where((row == k) & (lane == 32 + place), fact, info)
    for b in range(2):
        msg_ref[:, b * LANE : (b + 1) * LANE] = jnp.where(
            row < IMAGES, both_halves(sums[2 + b]), both_halves(sums[4 + b])
        )
    msg_ref[:, 2 * LANE :] = jnp.where(row < IMAGES, info + prob_ref[...], low.astype(F32))


def loss_part(images, all_images, cell_count, recv_refs, head_ref, rows_ref, means, small_ref):
    view = lax.axis_index("view")
    received = jnp.concatenate([ref[...] for ref in recv_refs], axis=0)
    count = received.shape[0] * 2 * images
    received = received.reshape(count, 3 * LANE)
    raw = received[:, 2 * LANE :]
    row = lax.broadcasted_iota(jnp.int32, (count, 1), 0)
    part = row & (2 * images - 1)
    once = part < images
    facts = jnp.where(once, raw, pltpu.roll(raw, images, 0))
    group, inner = row // (2 * images), received.shape[0] // (2 * images * len(recv_refs))
    offset = (group % inner) * len(recv_refs) + group // inner
    image = ((offset ^ lax.axis_index("dp")) * images + (part & (images - 1))).astype(F32)
    alpha = facts[:, 32:33]
    label = facts[:, 33:34]
    labelled = facts[:, 34:35]
    order = facts[:, 35:36]
    eye = row == lax.broadcasted_iota(jnp.int32, (count, count), 1)
    image_lane = jnp.sum(jnp.where(eye, image, 0.0), axis=0, keepdims=True)
    order_lane = jnp.sum(jnp.where(eye, order, 0.0), axis=0, keepdims=True)
    first_lane = jnp.sum(jnp.where(eye & once, 1.0, 0.0), axis=0, keepdims=True)
    is_one = jnp.where(view == 0, 1.0, 0.0)
    ours = is_one * image + (1.0 - is_one) * order
    theirs = is_one * order_lane + (1.0 - is_one) * image_lane
    match = jnp.where((ours == theirs) & (first_lane > 0.5), 1.0, 0.0).astype(BF16)
    valid = class_lanes(count)
    other = pltpu.roll(facts, LANE - 16, 1)
    target = dot(match, jnp.where(valid, other, 0.0).astype(BF16))
    log_prob = jnp.where(valid, log_softmax(jnp.where(valid, facts, 0.0), valid), 0.0)
    probs = jnp.where(valid, jnp.exp(log_prob), 0.0)
    lane = lax.broadcasted_iota(jnp.int32, (count, LANE), 1)
    onehot = jnp.where(lane.astype(F32) == label, 1.0, 0.0)
    total = jnp.sum(jnp.where(once, labelled, 0.0), axis=0, keepdims=True)
    mask = labelled * is_one
    away = probs - target
    grad_prob = CONS_WEIGHT / all_images * away
    grad = mask * (probs - onehot) / total + probs * (
        grad_prob - jnp.sum(probs * grad_prob, axis=1, keepdims=True)
    )
    grad_low = grad.astype(BF16)
    dmix = dot(grad_low, head_rows(head_ref)) / CELLS
    weights = (dmix * alpha, dmix * (1.0 - alpha))
    for b in range(2):
        product = weights[b] * received[:, b * LANE : (b + 1) * LANE]
        plain = column_sum(jnp.where(once, product, 0.0))
        normal = column_sum(jnp.where(once, 0.0, product))
        means[2 * b : 2 * b + 1, :] = plain / cell_count
        means[2 * b + 1 : 2 * b + 2, :] = normal / cell_count
        rows_ref[b] = weights[b]
        small_ref[16 + 2 * b : 16 + 2 * b + 1, :] = plain
        small_ref[16 + 2 * b + 1 : 16 + 2 * b + 2, :] = normal
    rows_ref[2] = dmix
    cross = -jnp.sum(
        jnp.where(once, mask * jnp.sum(onehot * log_prob, axis=1, keepdims=True), 0.0), axis=0, keepdims=True
    )
    consistency = jnp.sum(
        jnp.where(once, jnp.sum(away * away, axis=1, keepdims=True), 0.0), axis=0, keepdims=True
    )
    lane_row = lax.broadcasted_iota(jnp.int32, (1, LANE), 1)
    small_ref[20:21, :] = jnp.where(
        lane_row == 0, cross, jnp.where(lane_row == 1, consistency, jnp.where(lane_row == 2, total, 0.0))
    )
    small_ref[21:24, :] = jnp.zeros((3, LANE), F32)
    pooled = jnp.where(once, 0.0, raw).astype(BF16)
    small_ref[0:16, :] = dot_rows(grad_low, pooled)[0:16, :]


def pack_grad(ref, blocks):
    side_by_side = jnp.concatenate(blocks + [jnp.zeros((CH, BLOCKS * LANE - WIDE), F32)], axis=1)
    for k in range(BLOCKS):
        ref[k * CH : (k + 1) * CH, :] = side_by_side[:, k * LANE : (k + 1) * LANE]


def keep_and_send(keep_ref, send_ref, blocks):
    view = lax.axis_index("view")
    for own, ref in ((0, keep_ref), (1, send_ref)):
        @pl.when(view == own)
        def _():
            pack_grad(ref, blocks[0])

        @pl.when(view != own)
        def _():
            pack_grad(ref, blocks[1])


def back_second_kernel(
    cell_count, all_images,
    second_ref, first_ref, bent_two, bent_one, recv1_ref, recv2_ref, recv3_ref, norm, head_ref, w_ref,
    du_ref, frames, msg_ref, small_ref, dmix_ref,
    terms1, terms2, rows_ref, means,
):
    rows = 2 * IMAGES
    norm_rows(total_of(recv1_ref), norm, terms1, 0, 0, cell_count)
    norm_rows(total_of(recv2_ref), norm, terms2, 0, 1, cell_count)
    loss_part(IMAGES, all_images, cell_count, recv3_ref, head_ref, rows_ref, means, small_ref)
    dmix_ref[...] = rows_ref[2, 0:rows, :]
    scales, linears, offsets = [], [], []
    for b in range(2):
        gain = term(terms2, b, 4)
        mean, slant = means[2 * b : 2 * b + 1, :], means[2 * b + 1 : 2 * b + 2, :]
        scales.append(0.5 * gain * rows_ref[b, 0:rows, :])
        linears.append(-gain * slant * term(terms2, b, 2))
        offsets.append(scales[b] - gain * (mean + slant * term(terms2, b, 3)))
    sums = [0.0] * 4
    carry = [blank_line()] * 2
    for b in range(2):
        clear_frame(frames.at[b])
    for step in range(STEPS):
        first_line, end = new_lines(step)
        for b in range(2):
            lanes = slice(b * LANE, (b + 1) * LANE)
            values = second_ref[first_line * LINE : end * LINE, lanes]
            bent = bent_two[first_line * LINE : end * LINE, lanes]
            shape = (values.shape[0] // 8, 8, LANE)
            dy = (bent.reshape(shape) * scales[b][None] + offsets[b][None]).reshape(values.shape) + values * linears[b]
            frame_line(frames.at[b], first_line, dy)
            dh, carry[b] = fold_lines(dot(taps(frames.at[b], step, (0, 1)), w_ref[b]), carry[b])
            before = first_ref[chunk_rows(step), lanes]
            du = dh + dh * bent_one[chunk_rows(step), lanes]
            du_ref[chunk_rows(step), lanes] = du
            sums[2 * b] += eight(du)
            sums[2 * b + 1] += eight(du * before)
    for b in range(2):
        plain, product = column_sum(sums[2 * b]), column_sum(sums[2 * b + 1])
        sums[2 * b] = plain
        sums[2 * b + 1] = term(terms1, b, 2) * product + term(terms1, b, 3) * plain
    spread_sums(msg_ref, sums)


def middle_lines(frame, first_line):
    return frame[first_line + 1 : first_line + 1 + DEEP, 1 : ACROSS + 1].reshape(CHUNK, frame.shape[-1])


def second_weight_kernel(frame_ref, dy_ref, keep_ref, send_ref, gacc):
    for b in range(2):
        for step in range(STEPS):
            pair = jnp.concatenate(
                [middle_lines(dy_ref.at[b], step * DEEP), middle_lines(dy_ref.at[b], step * DEEP + 1)], axis=1
            )
            product = dot_rows(pair, taps(frame_ref.at[b], step, (0, 1)))
            gacc[b] = product if step == 0 else gacc[b] + product
    blocks = []
    for b in range(2):
        blocks.append([])
        for tap in range(TAPS):
            ky, kx = tap // 3, tap % 3
            row = LANE if ky == 0 else 0
            lane = (ky // 2) * 3 * LANE + kx * LANE
            blocks[b].append(gacc[b, row : row + CH, lane : lane + CH])
    keep_and_send(keep_ref, send_ref, blocks)


def back_weight_kernel(
    cell_count,
    du_ref, first_ref, low_ref, recv1_ref, recv5_ref, norm, small_ref,
    frame_ref, keep_ref, send_ref,
    terms1, gacc,
):
    norm_rows(total_of(recv1_ref), norm, terms1, 0, 0, cell_count)
    sums = total_of(recv5_ref)
    for ref in (keep_ref, send_ref):
        ref[GRAD_ROWS : GRAD_ROWS + 24, :] = small_ref[...]
        ref[GRAD_ROWS + 24 :, :] = sums
    means = sums / cell_count
    for b in range(2):
        clear_frame(frame_ref.at[b])
    for step in range(STEPS):
        parts = []
        for b in range(2):
            lanes = slice(b * LANE, (b + 1) * LANE)
            normal = first_ref[chunk_rows(step), lanes] * term(terms1, b, 2) + term(terms1, b, 3)
            parts.append(term(terms1, b, 4) * (
                du_ref[chunk_rows(step), lanes] - means[2 * b : 2 * b + 1, :] - normal * means[2 * b + 1 : 2 * b + 2, :]
            ))
        pair = jnp.concatenate(parts, axis=1)
        for b in range(2):
            frame_line(frame_ref.at[b], step * DEEP, parts[b])
        product = dot_rows(pair.astype(BF16), taps(low_ref, step, (-1, 0, 1)))
        gacc[...] = product if step == 0 else gacc[...] + product
    keep_and_send(
        keep_ref, send_ref,
        [[gacc[b * LANE : b * LANE + CH, tap * LANE : tap * LANE + CH] for tap in range(TAPS)] for b in range(2)],
    )


def back_stem_kernel(frame_ref, moved_ref, dmix_ref, w_ref, stem_ref):
    carry = blank_line()
    total = 0.0
    products = []
    for step in range(STEPS):
        if step % 2 == 0:
            products = [[dot(taps(frame_ref.at[b], step + k, (0, 1)), w_ref[b]) for k in range(2)] for b in range(2)]
        both = products[0][step % 2] + products[1][step % 2]
        dstem, carry = fold_lines(both, carry)
        dstem = (dstem.reshape(CHUNK // 8, 8, LANE) + dmix_ref[...][None]).reshape(CHUNK, LANE)
        total += dot(image_taps(moved_ref, step * DEEP, DEEP), dstem.astype(BF16))
    rows = [total[stem_row(tap) : stem_row(tap) + 3, :] for tap in range(TAPS)]
    stem_ref[...] = jnp.concatenate(rows, axis=0)


def code(values):
    top = jnp.max(jnp.abs(values), axis=0, keepdims=True)
    power = jnp.clip(jnp.ceil(jnp.log2(jnp.maximum(top, 1e-30)) + 0.01), -100.0, 100.0)
    counted = jnp.round(values * (jnp.exp2(-power) * CODE_TOP))
    return counted, power


def unit(power):
    return jnp.exp2(power) * (1.0 / CODE_TOP)


def coded_rows(values, rows):
    counted, power = code(values)
    parts = [counted, power]
    if rows - values.shape[0] - 1:
        parts.append(jnp.zeros((rows - values.shape[0] - 1, LANE), F32))
    return jnp.concatenate(parts, axis=0).astype(jnp.int32).astype(jnp.int16)


def decoded(values, count):
    whole_part = values.astype(jnp.int32).astype(F32)
    return whole_part[:count] * unit(whole_part[count : count + 1])


def encode_kernel(keep2, recv2, keep1, recv1, *refs):
    outs, total = refs[:-1], refs[-1]
    for k, (keep, recv) in enumerate(((keep1, recv1), (keep2, recv2))):
        total[k] = keep[0:GRAD_ROWS, :] + recv[0:GRAD_ROWS, :]
    mine = lax.axis_index("dp") & (QUARTERS - 1)
    for offset, out in enumerate(outs):
        place = pl.multiple_of((mine ^ offset) * SHARE, 8)
        for k in range(2):
            out[k * PIECE : (k + 1) * PIECE, :] = coded_rows(total[k, pl.ds(place, SHARE), :], PIECE)


def summed(refs, first, count, rows):
    total = decoded(refs[0][first : first + rows, :], count)
    for ref in refs[1:]:
        total += decoded(ref[first : first + rows, :], count)
    return total


def combine_kernel(recv_refs, stem_ref, out_ref):
    for k in range(2):
        out_ref[k * PIECE : (k + 1) * PIECE, :] = coded_rows(summed(recv_refs, k * PIECE, SHARE, PIECE), PIECE)
    out_ref[2 * PIECE :, :] = coded_rows(stem_ref[...], SIDE)


def recode_kernel(recv_refs, out_ref):
    for k in range(2):
        out_ref[k * PIECE : (k + 1) * PIECE, :] = coded_rows(summed(recv_refs, k * PIECE, SHARE, PIECE), PIECE)
    out_ref[2 * PIECE :, :] = coded_rows(summed(recv_refs, 2 * PIECE, 27, SIDE), SIDE)


def stack_kernel(inner, parts, out_ref):
    count = parts[0].shape[0]
    for k, part in enumerate(parts):
        if inner:
            for entry in range(count):
                out_ref[entry * len(parts) + k] = part[entry]
        else:
            out_ref[k * count : (k + 1) * count] = part[...]


def adam_terms(gradient, factor, weight, first, second, teacher):
    clipped = gradient * factor
    first_new = BETA_FIRST * first + (1.0 - BETA_FIRST) * clipped
    second_new = BETA_SECOND * second + (1.0 - BETA_SECOND) * (clipped * clipped)
    second_hat = second_new * (1.0 / (1.0 - BETA_SECOND**STEP))
    weight_new = weight * (1.0 - LEARN_RATE * WEIGHT_DECAY) - (
        first_new * (LEARN_RATE / (1.0 - BETA_FIRST**STEP)) / (jnp.sqrt(second_hat) + ADAM_EPS)
    )
    return weight_new, first_new, second_new, TEACHER_KEEP * teacher + (1.0 - TEACHER_KEEP) * weight_new


def update_kernel(
    own_codes, other_codes, own_facts, other_facts,
    cw, cf, cs, ct, sw, sf, ss, st, hw, hf, hs, ht, nw, nf, ns, nt,
    cw_o, cf_o, cs_o, ct_o, cb_o, sw_o, sf_o, ss_o, st_o, sb_o, hw_o, hf_o, hs_o, ht_o, hb_o,
    nw_o, nf_o, ns_o, nt_o, norm_o, cross_o, count_o, consistency_o,
    factor_ref, own_ref, other_ref,
):
    conv = pl.program_id(0)
    view = lax.axis_index("view")

    @pl.when(conv == 0)
    def _():
        facts = own_facts[...] + other_facts[...]
        small, sums = facts[:24], facts[24:]
        mine = lax.axis_index("dp") & (QUARTERS - 1)
        stem = jnp.zeros((27, LANE), F32)
        for codes, ref in ((own_codes, own_ref), (other_codes, other_ref)):
            for offset, source in enumerate(codes):
                place = pl.multiple_of((mine ^ offset) * SHARE, 8)
                for k in range(2):
                    ref[k, pl.ds(place, SHARE), :] = decoded(source[k * PIECE : (k + 1) * PIECE, :], SHARE)
            stem += summed(codes, 2 * PIECE, 27, SIDE)
        stem = stem[:, :CH]
        head = small[:CLASSES, :CH]
        gains = jnp.concatenate([sums[1:2], small[17:18], sums[3:4], small[19:20]], axis=0)[:, :CH]
        shifts = jnp.concatenate([sums[0:1], small[16:17], sums[2:3], small[18:19]], axis=0)[:, :CH]
        total = jnp.zeros((1, 1), F32)
        for part in (stem, head, gains, shifts):
            total += jnp.sum(jnp.sum(part * part, axis=1, keepdims=True), axis=0, keepdims=True)
        for ref in (own_ref, other_ref):
            for k in range(2):
                values = ref[k, 0:GRAD_ROWS, :]
                column = jnp.sum(values * values, axis=0, keepdims=True)
                total += jnp.sum(column, axis=1, keepdims=True)
        norm = jnp.sqrt(total)
        factor = CLIP_LIMIT / jnp.maximum(norm, CLIP_LIMIT)
        factor_ref[...] = jnp.broadcast_to(factor, factor_ref.shape)
        norm_o[...] = norm
        cross_o[...] = small[20:21, 0:1]
        consistency_o[...] = small[20:21, 1:2]
        count_o[...] = own_facts[20:21, 2:3]
        sw_o[...], sf_o[...], ss_o[...], st_o[...] = adam_terms(stem, factor, sw[...], sf[...], ss[...], st[...])
        sb_o[...] = sw_o[...].astype(BF16)
        hw_o[...], hf_o[...], hs_o[...], ht_o[...] = adam_terms(head, factor, hw[...], hf[...], hs[...], ht[...])
        hb_o[...] = hw_o[...].astype(BF16)
        for k, part in enumerate((gains, shifts)):
            nw_o[k], nf_o[k], ns_o[k], nt_o[k] = adam_terms(part, factor, nw[k], nf[k], ns[k], nt[k])

    def update(ref, second):
        factor = factor_ref[0:1, 0:1]
        for k in range(BLOCKS):
            lanes = slice(k * LANE, min((k + 1) * LANE, WIDE))
            gradient = ref[second, k * CH : (k + 1) * CH, 0 : lanes.stop - lanes.start]
            weight, first, second_moment, teacher = adam_terms(
                gradient, factor, cw[:, lanes], cf[:, lanes], cs[:, lanes], ct[:, lanes]
            )
            cw_o[:, lanes] = weight
            cf_o[:, lanes] = first
            cs_o[:, lanes] = second_moment
            ct_o[:, lanes] = teacher
            cb_o[:, lanes] = weight.astype(BF16)

    mine = conv // 2 == view

    @pl.when(mine)
    def _():
        update(own_ref, conv & 1)

    @pl.when(jnp.logical_not(mine))
    def _():
        update(other_ref, conv & 1)


def whole(shape):
    return pl.BlockSpec(shape, lambda i: (0,) * len(shape))


def scalars():
    return pl.BlockSpec(memory_space=pltpu.SMEM)


def conv_part(k):
    return pl.BlockSpec((None, CH, WIDE), lambda i: (k, 0, 0))


def held():
    return pl.BlockSpec(memory_space=pltpu.VMEM)


def hold(values):
    return pltpu.with_memory_space_constraint(values, pltpu.VMEM)


def struct(shape, kind=F32):
    return jax.ShapeDtypeStruct(shape, kind)


def from_partners(values, shift, ways):
    size = lax.axis_size("dp")
    return [values] + [
        lax.ppermute(values, "dp", [(i, i ^ (offset << shift)) for i in range(size)]) for offset in range(1, ways)
    ]


def stages():
    size = lax.axis_size("dp")
    groups = []
    shift = 0
    while (1 << shift) < size:
        ways = min(4, size >> shift)
        groups.append((shift, ways))
        shift += 2
    return groups


def sum_parts(values, beside=None):
    groups = stages()
    for shift, ways in groups[:-1]:
        parts = from_partners(values, shift, ways)
        if beside is not None:
            parts, beside = lax.optimization_barrier((parts, beside))
        values = sum(parts)
    return tuple(from_partners(values, *groups[-1])), beside


def stack(parts, inner):
    shape = (len(parts) * parts[0].shape[0],) + parts[0].shape[1:]
    return pl.pallas_call(
        functools.partial(stack_kernel, inner), out_shape=struct(shape, parts[0].dtype), compiler_params=PARAMS, name="stack"
    )(tuple(parts))


def gather_parts(values, groups):
    inner = groups[0][0] > 0
    for shift, ways in groups[:-1]:
        values = stack(from_partners(values, shift, ways), inner)
    return tuple(from_partners(values, *groups[-1]))


def swap_view(values):
    return lax.ppermute(values, "view", [(0, 1), (1, 0)])


def forward_weights(conv):
    shape = (2, 6 * LANE, 2 * LANE)
    return pl.pallas_call(
        forward_weight_kernel,
        grid=(2,),
        in_specs=[pl.BlockSpec((None, CH, WIDE), lambda i: (2 * i + 1, 0, 0))],
        out_specs=pl.BlockSpec((None,) + shape[1:], lambda i: (i, 0, 0)),
        out_shape=struct(shape, BF16),
        compiler_params=PARAMS,
        cost_estimate=pl.CostEstimate(flops=2_000_000_000, bytes_accessed=4_000_000, transcendentals=0),
        name="forward_weight",
    )(conv)


def backward_weights(conv):
    return pl.pallas_call(
        backward_weight_kernel,
        grid=(1,),
        in_specs=[conv_part(k) for k in range(4)],
        out_specs=[whole((2, 6 * LANE, 2 * LANE))] * 2,
        out_shape=[struct((2, 6 * LANE, 2 * LANE), BF16)] * 2,
        compiler_params=PARAMS,
        cost_estimate=pl.CostEstimate(flops=4_000_000_000, bytes_accessed=8_000_000, transcendentals=0),
        name="backward_weight",
    )(conv, conv, conv, conv)


def shards(
    augmented, shake_ratio, labels, labelled, view_order,
    stem_weight, conv_weight, head_weight, norm_param,
    teacher_stem, teacher_conv, teacher_head, teacher_norm,
    first_stem, first_conv, first_head, first_norm,
    second_stem, second_conv, second_head, second_norm,
):
    dp = lax.axis_size("dp")
    all_images = IMAGES * dp
    cell_count = float(all_images * CELLS)
    rows = dp * 2 * IMAGES
    conv, conv_t, conv_f, conv_s = (
        jnp.transpose(v, (0, 2, 1)) for v in (conv_weight, teacher_conv, first_conv, second_conv)
    )
    head, head_t, head_f, head_s = (v.T for v in (head_weight, teacher_head, first_head, second_head))
    pixels = jnp.transpose(augmented[0], (0, 3, 1, 2))
    msg = struct((8, LANE))
    groups = stages()
    last_ways = groups[-1][1]
    recv_spec = (held(),) * last_ways
    norm_spec = whole((2, 4, CH))
    head_spec = whole((CLASSES, CH))
    moved_shape = (3, (SIDE + 4) * 8, LANE)
    frame_one, frame_two = FRAME + (LANE,), (2,) + FRAME + (LANE,)
    values_shape, grad_shape = (ALL, 2 * LANE), struct((GRAD_ROWS, LANE))
    terms_scratch = pltpu.VMEM((16, LANE), F32)

    first_s, first_t, low, moved, stem_sums, message = pl.pallas_call(
        first_kernel,
        in_specs=[pl.BlockSpec(memory_space=pltpu.HBM)] * 5,
        out_specs=[held()] * 6,
        out_shape=[
            pltpu.VMEM(values_shape, F32), pltpu.VMEM(values_shape, F32), pltpu.VMEM(frame_one, BF16),
            pltpu.VMEM(moved_shape, F32), struct((2, 8, LANE)), msg,
        ],
        scratch_shapes=[
            pltpu.VMEM(moved_shape[1:], F32), pltpu.VMEM((STEM_ROWS, 2 * LANE), F32),
            pltpu.VMEM((STEM_ROWS, 2 * LANE), BF16), pltpu.VMEM((2, 9 * LANE, 2 * LANE), BF16),
            pltpu.VMEM(frame_one, BF16), pltpu.VMEM((IMAGES, 3, SIDE, SIDE), BF16), pltpu.VMEM((27, CH), F32),
            pltpu.VMEM((27, CH), F32), pltpu.VMEM((4, CH, WIDE), F32), pltpu.SemaphoreType.DMA((7,)),
        ],
        compiler_params=PARAMS,
        name="first_conv",
    )(*(pltpu.with_memory_space_constraint(v, pltpu.HBM) for v in (pixels, stem_weight, teacher_stem, conv, conv_t)))
    first_s, first_t, low, moved = (hold(v) for v in (first_s, first_t, low, moved))
    recv1, (weight_s, weight_t) = sum_parts(message, (forward_weights(conv), forward_weights(conv_t)))

    second_s, second_t, hidden, bent_one, message = pl.pallas_call(
        functools.partial(second_kernel, cell_count),
        in_specs=[held()] * 2 + [recv_spec] + [held()] * 4,
        out_specs=[held()] * 5,
        out_shape=[pltpu.VMEM(values_shape, F32)] * 2 + [pltpu.VMEM(frame_two, BF16), pltpu.VMEM(values_shape, F32), msg],
        scratch_shapes=[pltpu.VMEM(frame_two, BF16), terms_scratch, terms_scratch],
        compiler_params=PARAMS,
        name="second_conv",
    )(first_s, first_t, recv1, norm_param, teacher_norm, weight_s, weight_t)
    second_s, second_t, hidden, bent_one = (hold(v) for v in (second_s, second_t, hidden, bent_one))
    recv2, _ = sum_parts(message)

    prob = pl.pallas_call(
        functools.partial(teacher_kernel, cell_count),
        in_specs=[scalars(), held(), recv_spec] + [held()] * 3,
        out_specs=held(),
        out_shape=struct((8, LANE)),
        scratch_shapes=[terms_scratch],
        compiler_params=PARAMS,
        name="teacher_logits",
    )(shake_ratio, second_t, recv2, teacher_norm, head_t, stem_sums)
    prob, conv_later = lax.optimization_barrier((prob, conv))
    other = swap_view(prob)
    back_weight_two, back_weight_one = backward_weights(conv_later)
    other, back_weight_two = lax.optimization_barrier((other, back_weight_two))
    facts, bent_two = pl.pallas_call(
        functools.partial(student_kernel, cell_count),
        in_specs=[scalars()] * 4 + [held(), recv_spec] + [held()] * 4,
        out_specs=[held()] * 2,
        out_shape=[struct((8, 3 * LANE)), pltpu.VMEM(values_shape, F32)],
        scratch_shapes=[terms_scratch],
        compiler_params=PARAMS,
        cost_estimate=pl.CostEstimate(flops=4_000_000_000, bytes_accessed=8_000_000, transcendentals=0),
        name="student_logits",
    )(shake_ratio, labels, labelled, view_order, second_s, recv2, norm_param, head, stem_sums, other)
    bent_two = hold(bent_two)
    recv3 = gather_parts(facts.reshape(1, 8, 3 * LANE), groups[::-1])

    du, dy, message, small, dmix = pl.pallas_call(
        functools.partial(back_second_kernel, cell_count, float(all_images)),
        in_specs=[held()] * 4 + [recv_spec] * 2 + [(held(),) * groups[0][1]] + [held()] * 3,
        out_specs=[held()] * 5,
        out_shape=[
            pltpu.VMEM(values_shape, F32), pltpu.VMEM(frame_two, BF16), msg, struct((24, LANE)), struct((8, LANE)),
        ],
        scratch_shapes=[
            terms_scratch, terms_scratch, pltpu.VMEM((3, rows, LANE), F32), pltpu.VMEM((8, LANE), F32),
        ],
        compiler_params=PARAMS,
        name="back_second",
    )(second_s, first_s, bent_two, bent_one, recv1, recv2, recv3, norm_param, head, back_weight_two)
    du, dy = hold(du), hold(dy)
    keep2, send2 = pl.pallas_call(
        second_weight_kernel,
        in_specs=[held()] * 2,
        out_specs=[held()] * 2,
        out_shape=[grad_shape] * 2,
        scratch_shapes=[pltpu.VMEM((2, 2 * LANE, 6 * LANE), F32)],
        compiler_params=PARAMS,
        cost_estimate=pl.CostEstimate(flops=8_000_000_000, bytes_accessed=16_000_000, transcendentals=0),
        name="second_weight",
    )(hidden, dy)
    recv5, (keep2, send2) = sum_parts(message, (keep2, send2))
    recv_grad2 = swap_view(send2)

    frame, keep1, send1 = pl.pallas_call(
        functools.partial(back_weight_kernel, cell_count),
        in_specs=[held()] * 3 + [recv_spec] * 2 + [held()] * 2,
        out_specs=[held()] * 3,
        out_shape=[pltpu.VMEM(frame_two, BF16)] + [struct((GRAD_ROWS + 32, LANE))] * 2,
        scratch_shapes=[terms_scratch, pltpu.VMEM((2 * LANE, 9 * LANE), F32)],
        compiler_params=PARAMS,
        cost_estimate=pl.CostEstimate(flops=8_000_000_000, bytes_accessed=16_000_000, transcendentals=0),
        name="back_weight",
    )(du, first_s, low, recv1, recv5, norm_param, small)
    frame = hold(frame)
    recv_grad1 = swap_view(send1)
    coded = pl.pallas_call(
        encode_kernel,
        out_shape=[struct((2 * PIECE, LANE), jnp.int16)] * QUARTERS,
        scratch_shapes=[pltpu.VMEM((2, GRAD_ROWS, LANE), F32)],
        compiler_params=PARAMS,
        name="encode",
    )(keep2, recv_grad2, keep1, recv_grad1)
    scattered = (coded[0],) + tuple(
        lax.ppermute(coded[offset], "dp", [(i, i ^ offset) for i in range(dp)]) for offset in range(1, QUARTERS)
    )

    stem_grad = pl.pallas_call(
        back_stem_kernel,
        in_specs=[held()] * 4,
        out_specs=held(),
        out_shape=struct((27, LANE)),
        compiler_params=PARAMS,
        cost_estimate=pl.CostEstimate(flops=8_000_000_000, bytes_accessed=16_000_000, transcendentals=0),
        name="back_stem",
    )(frame, moved, dmix, back_weight_one)

    stem_grad, scattered = lax.optimization_barrier((stem_grad, scattered))
    code_shape = struct((CODE_ROWS, LANE), jnp.int16)
    codes = pl.pallas_call(combine_kernel, out_shape=code_shape, compiler_params=PARAMS, name="combine")(
        scattered, stem_grad
    )
    for group in groups[1:]:
        codes = pl.pallas_call(recode_kernel, out_shape=code_shape, compiler_params=PARAMS, name="recode")(
            tuple(from_partners(codes, *group))
        )
    own = tuple(from_partners(codes, *groups[0]))
    other_grads = tuple(swap_view(part) for part in own)

    conv_block = pl.BlockSpec((None, CH, WIDE), lambda i: (i, 0, 0))
    stem_block, norm_block = whole((27, CH)), norm_spec
    code_spec = (whole((CODE_ROWS, LANE)),) * QUARTERS
    facts_spec = pl.BlockSpec((32, LANE), lambda i: (GRAD_ROWS // 32, 0))
    grads_scratch = pltpu.VMEM((2, GRAD_ROWS, LANE), F32)
    outs = pl.pallas_call(
        update_kernel,
        grid=(4,),
        in_specs=[code_spec] * 2 + [facts_spec] * 2
        + [conv_block] * 4 + [stem_block] * 4 + [head_spec] * 4 + [norm_block] * 4,
        out_specs=[conv_block] * 5 + [stem_block] * 5 + [head_spec] * 5 + [norm_block] * 4 + [whole((1, 1))] * 4,
        out_shape=[struct((4, CH, WIDE))] * 4 + [struct((4, CH, WIDE), BF16)]
        + [struct((27, CH))] * 4 + [struct((27, CH), BF16)]
        + [struct((CLASSES, CH))] * 4 + [struct((CLASSES, CH), BF16)]
        + [struct((2, 4, CH))] * 4 + [struct((1, 1))] * 4,
        scratch_shapes=[pltpu.VMEM((8, LANE), F32), grads_scratch, grads_scratch],
        compiler_params=PARAMS,
        name="update",
    )(
        own, other_grads, keep1, recv_grad1,
        conv, conv_f, conv_s, conv_t, stem_weight, first_stem, second_stem, teacher_stem,
        head, head_f, head_s, head_t, norm_param, first_norm, second_norm, teacher_norm,
    )
    convs = [jnp.transpose(v, (0, 2, 1)) for v in outs[:5]]
    stems = outs[5:10]
    heads = [v.T for v in outs[10:15]]
    norms = outs[15:19]
    return (
        *(v.reshape(()) for v in outs[19:23]),
        *stems[:4], *convs[:4], *heads[:4], *norms, stems[4], convs[4], heads[4],
    )


def solution(mesh):
    in_specs = (
        (P("view", "dp", None, None, None), P("view", "dp"), P("dp"), P("dp")) + (P(),) * 17
    )
    return jax.shard_map(shards, mesh=mesh, in_specs=in_specs, out_specs=(P(),) * 23, check_vma=False)
```

```python
import functools

import jax
import jax.numpy as jnp
from jax import lax
from jax.experimental import pallas as pl
from jax.experimental.pallas import tpu as pltpu
from jax.sharding import PartitionSpec as P

CLASSES = 10
STEP = 5
EPS_NORM = 1e-05
LEARN_RATE = 0.03
BETA_FIRST = 0.5
BETA_SECOND = 0.5
WEIGHT_DECAY = 0.0001
ADAM_EPS = 1e-08
CLIP_LIMIT = 0.02
TEACHER_KEEP = 0.9
CONS_WEIGHT = 10.0

F32 = jnp.float32
BF16 = jnp.bfloat16
LANE = 128
CH = 96
SIDE = 32
CELLS = SIDE * SIDE
IMAGES = 4
QUARTERS = 4
ACROSS = SIDE // QUARTERS
TILE = IMAGES * QUARTERS
LINE = ACROSS * TILE
STEPS = 4
DEEP = SIDE // STEPS
CHUNK = DEEP * LINE
ALL = SIDE * LINE
BLOCK = 64
TAPS = 9
WIDE = TAPS * CH
BLOCKS = -(-WIDE // LANE)
GRAD_ROWS = BLOCKS * CH
SHARE = GRAD_ROWS // QUARTERS
PIECE = -(-(SHARE + 1) // 16) * 16
CODE_ROWS = 2 * PIECE + SIDE
STEM_ROWS = 80
CODE_TOP = 32000.0
FRAME = (SIDE + 2, ACROSS + 2, TILE)
PARAMS = pltpu.CompilerParams(vmem_limit_bytes=24 * 1024 * 1024)


def dot(a, b):
    return jnp.dot(a, b, preferred_element_type=F32)


def dot_rows(a, b):
    return lax.dot_general(a, b, (((0,), (0,)), ((), ())), preferred_element_type=F32)


def dot_lanes(a, b):
    return lax.dot_general(a, b, (((1,), (1,)), ((), ())), preferred_element_type=F32)


def frame_line(frame, first_line, values):
    lines = values.shape[0] // LINE
    width = values.shape[1]
    tiles = values.reshape(lines, ACROSS, TILE, width)
    row = lax.broadcasted_iota(jnp.int32, (1, TILE, 1), 1)
    before = jnp.where(row >= IMAGES, pltpu.roll(tiles[:, ACROSS - 1], IMAGES, 1), 0.0)
    after = jnp.where(row < TILE - IMAGES, pltpu.roll(tiles[:, 0], TILE - IMAGES, 1), 0.0)
    place = slice(first_line + 1, first_line + 1 + lines)
    frame[place, 1 : ACROSS + 1] = tiles.astype(BF16)
    frame[place, 0] = before.astype(BF16)
    frame[place, ACROSS + 1] = after.astype(BF16)


def clear_frame(frame):
    blank = jnp.zeros(frame.shape[1:], BF16)
    frame[0] = blank
    frame[SIDE + 1] = blank


def taps(frame, step, rows):
    parts = []
    for dy in rows:
        for kx in range(3):
            place = step * DEEP + 1 + dy
            lines = frame[place : place + DEEP, kx : kx + ACROSS]
            parts.append(lines.reshape(CHUNK, lines.shape[-1]))
    return jnp.concatenate(parts, axis=1)


def fold_lines(both, carry):
    upper = jnp.concatenate([carry, both[: CHUNK - LINE, LANE:]], axis=0)
    return both[:, :LANE] + upper, both[CHUNK - LINE :, LANE:]


def blank_line():
    return jnp.zeros((LINE, LANE), F32)


def new_lines(step):
    first = 0 if step == 0 else step * DEEP + 1
    return first, min((step + 1) * DEEP + 1, SIDE)


def chunk_rows(step):
    return slice(step * CHUNK, (step + 1) * CHUNK)


def eight(values):
    parts = values.reshape(values.shape[0] // 8, 8, values.shape[1])
    while parts.shape[0] > 1:
        middle = parts.shape[0] // 2
        rest = parts[2 * middle :]
        parts = parts[:middle] + parts[middle : 2 * middle]
        if rest.shape[0]:
            parts = jnp.concatenate([parts[:-1], parts[-1:] + rest], axis=0) if middle > 1 else parts + rest
    return parts[0]


def both_halves(sums):
    return sums + pltpu.roll(sums, IMAGES, 0)


def tap_block(raw, tap):
    return raw[:, tap * CH : (tap + 1) * CH]


def image_lines(image_ref, plain, moved):
    plain[...] = jnp.zeros(plain.shape, F32)
    for channel in range(3):
        side_by_side = jnp.concatenate([image_ref[i, channel].astype(F32) for i in range(IMAGES)], axis=1)
        plain[pl.ds(8 + channel, SIDE, stride=8), :] = side_by_side
    source = lax.broadcasted_iota(jnp.int32, (LANE, LANE), 0)
    target = lax.broadcasted_iota(jnp.int32, (LANE, LANE), 1)
    same = source // SIDE == (target & (IMAGES - 1))
    across = ((target // IMAGES) & (QUARTERS - 1)) * ACROSS + target // TILE
    for kx in range(3):
        picks = jnp.where(same & ((source & (SIDE - 1)) == across + (kx - 1)), 1.0, 0.0).astype(BF16)
        moved[kx] = dot(plain[...].astype(BF16), picks)


def image_taps(moved, first_line, lines):
    columns = []
    for line in range(lines):
        place = (first_line + line) * 8
        parts = [moved[kx, place : place + 24, :] for kx in range(3)]
        columns.append(jnp.concatenate(parts + [jnp.zeros((8, LANE), F32)], axis=0))
    return jnp.concatenate(columns, axis=1).astype(BF16)


def stem_row(tap):
    return (tap % 3) * 24 + (tap // 3) * 8


def pad_lanes(row):
    return jnp.concatenate([row, jnp.zeros((row.shape[0], LANE - row.shape[1]), row.dtype)], axis=1)


def norm_terms(sums, squares, cell_count):
    average = sums / cell_count
    inverse = lax.rsqrt(squares / cell_count - average * average + EPS_NORM)
    return average, inverse


def column_sum(values):
    return jnp.sum(values, axis=0, keepdims=True)


def slope_rest(half, tanh, product):
    return (tanh + half) - product * tanh


def first_kernel(
    image_hbm, stem_s_hbm, stem_t_hbm, raw_s, raw_t,
    first_s, first_t, frame_s, moved_ref, pooled_ref, msg_ref,
    plain, wst32, wst, wf, frame_t, image_ref, stem_s, stem_t, raw, sems,
):
    coming = [
        pltpu.make_async_copy(source, target, sems.at[k])
        for k, (source, target) in enumerate((
            (image_hbm, image_ref), (stem_s_hbm, stem_s), (stem_t_hbm, stem_t),
            (raw_s.at[0], raw.at[0]), (raw_s.at[2], raw.at[1]), (raw_t.at[0], raw.at[2]), (raw_t.at[2], raw.at[3]),
        ))
    ]
    for copy in coming:
        copy.start()
    wf[...] = jnp.zeros(wf.shape, BF16)
    wst32[...] = jnp.zeros(wst32.shape, F32)
    clear_frame(frame_s)
    clear_frame(frame_t)
    for copy in coming[:3]:
        copy.wait()
    image_lines(image_ref, plain, moved_ref)
    for n, stem in enumerate((stem_s, stem_t)):
        for tap in range(TAPS):
            row = stem_row(tap)
            wst32[row : row + 3, n * LANE : n * LANE + CH] = stem[3 * tap : 3 * tap + 3, :]
    wst[...] = wst32[...].astype(BF16)
    for copy in coming[3:]:
        copy.wait()
    for n in range(2):
        for b in range(2):
            for tap in range(TAPS):
                wf[n, tap * LANE : tap * LANE + CH, b * LANE : b * LANE + CH] = jnp.transpose(
                    tap_block(raw.at[2 * n + b], tap)
                ).astype(BF16)
    pooled = [0.0, 0.0]
    sums = [0.0] * 8
    for step in range(STEPS):
        first_line, end = new_lines(step)
        stems = dot_rows(image_taps(moved_ref, first_line, end - first_line), wst[...])
        for n, (frame, out_ref) in enumerate(((frame_s, first_s), (frame_t, first_t))):
            stem = stems[:, n * LANE : (n + 1) * LANE]
            pooled[n] += eight(stem)
            frame_line(frame, first_line, stem)
            out = dot(taps(frame, step, (-1, 0, 1)), wf[n])
            out_ref[chunk_rows(step), :] = out
            for b in range(2):
                part = out[:, b * LANE : (b + 1) * LANE]
                sums[4 * n + 2 * b] += eight(part)
                sums[4 * n + 2 * b + 1] += eight(part * part)
    for n in range(2):
        pooled_ref[n] = both_halves(pooled[n])
    spread_sums(msg_ref, sums)


def total_of(refs):
    total = refs[0][...]
    for ref in refs[1:]:
        total = total + ref[...]
    return total


def spread_sums(msg_ref, sums):
    sums = [column_sum(part) for part in sums]
    if len(sums) < 8:
        sums.append(jnp.zeros((8 - len(sums), LANE), F32))
    msg_ref[...] = jnp.concatenate(sums, axis=0)


def forward_weight_kernel(raw_ref, w_ref):
    w_ref[...] = jnp.zeros(w_ref.shape, BF16)
    for ky in range(3):
        for kx in range(3):
            row = (ky // 2) * 3 * LANE + kx * LANE
            lane = LANE if ky == 0 else 0
            w_ref[row : row + CH, lane : lane + CH] = jnp.transpose(tap_block(raw_ref, ky * 3 + kx)).astype(BF16)


def backward_weight_kernel(cw0, cw1, cw2, cw3, two_ref, one_ref):
    two_ref[...] = jnp.zeros(two_ref.shape, BF16)
    one_ref[...] = jnp.zeros(one_ref.shape, BF16)
    for ky in range(3):
        for kx in range(3):
            tap = (2 - ky) * 3 + 2 - kx
            lane = LANE if ky == 0 else 0
            for b, (inner, outer) in enumerate(((cw0, cw1), (cw2, cw3))):
                row = (ky // 2) * 3 * LANE + kx * LANE
                two_ref[b, row : row + CH, lane : lane + CH] = (0.5 * tap_block(outer, tap)).astype(BF16)
                one_ref[b, row : row + CH, lane : lane + CH] = tap_block(inner, tap).astype(BF16)


def norm_rows(sums, norm, terms, first_row, norm_index, cell_count):
    for b in range(2):
        row = first_row + 2 * b
        average, inverse = norm_terms(sums[row : row + 1], sums[row + 1 : row + 2], cell_count)
        gain = pad_lanes(norm[0, 2 * b + norm_index : 2 * b + norm_index + 1, :])
        shift = pad_lanes(norm[1, 2 * b + norm_index : 2 * b + norm_index + 1, :])
        scale = inverse * gain
        terms[8 * b : 8 * b + 1, :] = 0.5 * scale
        terms[8 * b + 1 : 8 * b + 2, :] = 0.5 * (shift - average * scale)
        terms[8 * b + 2 : 8 * b + 3, :] = inverse
        terms[8 * b + 3 : 8 * b + 4, :] = -average * inverse
        terms[8 * b + 4 : 8 * b + 5, :] = scale


def term(terms, b, k):
    return terms[8 * b + k : 8 * b + k + 1, :]


def second_kernel(
    cell_count, first_s, first_t, recv_ref, norm_s, norm_t, ws_ref, wt_ref,
    second_s, second_t, frame_s, bent_ref, msg_ref,
    frame_t, terms_s, terms_t,
):
    received = total_of(recv_ref)
    norm_rows(received, norm_s, terms_s, 0, 0, cell_count)
    norm_rows(received, norm_t, terms_t, 4, 0, cell_count)
    nets = ((first_s, terms_s, frame_s, ws_ref, second_s), (first_t, terms_t, frame_t, wt_ref, second_t))
    sums = [0.0] * 8
    carry = [blank_line()] * 4
    for _, _, frames, _, _ in nets:
        for b in range(2):
            clear_frame(frames.at[b])
    for step in range(STEPS):
        first_line, end = new_lines(step)
        for n, (source, terms, frames, w, target) in enumerate(nets):
            for b in range(2):
                k = 2 * n + b
                lanes = slice(b * LANE, (b + 1) * LANE)
                half = source[first_line * LINE : end * LINE, lanes] * term(terms, b, 0) + term(terms, b, 1)
                tanh = jnp.tanh(half)
                product = half * tanh
                frame_line(frames.at[b], first_line, half + product)
                if n == 0:
                    bent_ref[first_line * LINE : end * LINE, lanes] = slope_rest(half, tanh, product)
                out, carry[k] = fold_lines(dot(taps(frames.at[b], step, (0, 1)), w[b]), carry[k])
                target[chunk_rows(step), lanes] = out
                sums[2 * k] += eight(out)
                sums[2 * k + 1] += eight(out * out)
    spread_sums(msg_ref, sums)


def head_rows(head_ref):
    padded = jnp.concatenate([head_ref[...], jnp.zeros((LANE - CLASSES, CH), F32)], axis=0)
    return pad_lanes(padded).astype(BF16)


def alpha_of(ratio_ref, image):
    return (ratio_ref[0, image].astype(F32) + 1.0) / 18.0


def alpha_rows(ratio_ref):
    row = lax.broadcasted_iota(jnp.int32, (2 * IMAGES, LANE), 0) & (IMAGES - 1)
    alpha = jnp.zeros((2 * IMAGES, LANE), F32)
    for k in range(IMAGES):
        alpha = jnp.where(row == k, alpha_of(ratio_ref, k), alpha)
    return alpha


def class_lanes(rows):
    return lax.broadcasted_iota(jnp.int32, (rows, LANE), 1) < CLASSES


def log_softmax(logits, valid):
    top = jnp.max(jnp.where(valid, logits, -3e38), axis=1, keepdims=True)
    moved = logits - top
    total = jnp.sum(jnp.where(valid, jnp.exp(moved), 0.0), axis=1, keepdims=True)
    return moved - jnp.log(total)


def pooled_low(ratio_ref, sums, stem_sums):
    alpha = alpha_rows(ratio_ref)
    total = alpha * both_halves(sums[0]) + (1.0 - alpha) * both_halves(sums[1])
    return ((total + stem_sums) / CELLS).astype(BF16)


def teacher_kernel(
    cell_count, ratio_ref, second_ref, recv_ref, norm, head_ref, stem_sum_ref,
    prob_ref,
    terms,
):
    norm_rows(total_of(recv_ref), norm, terms, 4, 1, cell_count)
    plain, curved = [0.0] * 2, [0.0] * 2
    for block in range(ALL // BLOCK):
        for b in range(2):
            values = second_ref[block * BLOCK : (block + 1) * BLOCK, b * LANE : (b + 1) * LANE]
            half = values * term(terms, b, 0) + term(terms, b, 1)
            plain[b] += eight(values)
            curved[b] += eight(half * jnp.tanh(half))
    sums = [plain[b] * term(terms, b, 0) + (CELLS // 2) * term(terms, b, 1) + curved[b] for b in range(2)]
    low = pooled_low(ratio_ref, sums, stem_sum_ref[1])
    logits = dot_lanes(low, head_rows(head_ref))
    valid = class_lanes(2 * IMAGES)
    first_rows = lax.broadcasted_iota(jnp.int32, (2 * IMAGES, LANE), 0) < IMAGES
    prob = jnp.where(valid & first_rows, jnp.exp(log_softmax(logits, valid)), 0.0)
    prob_ref[...] = pltpu.roll(prob.astype(BF16).astype(F32), 16, 1)


def student_kernel(
    cell_count, ratio_ref, labels_ref, labelled_ref, order_ref,
    second_ref, recv_ref, norm, head_ref, stem_sum_ref,
    msg_ref, bent_ref,
    terms,
):
    norm_rows(total_of(recv_ref), norm, terms, 0, 1, cell_count)
    plain, curved, bent, bent_values = ([0.0] * 2 for _ in range(4))
    for block in range(ALL // BLOCK):
        for b in range(2):
            values = second_ref[block * BLOCK : (block + 1) * BLOCK, b * LANE : (b + 1) * LANE]
            half = values * term(terms, b, 0) + term(terms, b, 1)
            tanh = jnp.tanh(half)
            product = half * tanh
            slope = slope_rest(half, tanh, product)
            bent_ref[block * BLOCK : (block + 1) * BLOCK, b * LANE : (b + 1) * LANE] = slope
            plain[b] += eight(values)
            curved[b] += eight(product)
            bent[b] += eight(slope)
            bent_values[b] += eight(slope * values)
    cells = CELLS // 2
    sums = [plain[b] * term(terms, b, 0) + cells * term(terms, b, 1) + curved[b] for b in range(2)]
    slopes = [0.5 * (cells + bent[b]) for b in range(2)]
    sums += slopes
    sums += [
        term(terms, b, 2) * (0.5 * (plain[b] + bent_values[b])) + term(terms, b, 3) * slopes[b] for b in range(2)
    ]
    dp_index = lax.axis_index("dp")
    low = pooled_low(ratio_ref, sums, stem_sum_ref[0])
    logits = dot_lanes(low, head_rows(head_ref))
    rows = 2 * IMAGES
    info = jnp.where(class_lanes(rows), logits, 0.0)
    lane = lax.broadcasted_iota(jnp.int32, (rows, LANE), 1)
    row = lax.broadcasted_iota(jnp.int32, (rows, LANE), 0)
    for k in range(IMAGES):
        facts = (
            alpha_of(ratio_ref, k),
            labels_ref[k].astype(F32),
            labelled_ref[k].astype(F32),
            order_ref[dp_index * IMAGES + k].astype(F32),
        )
        for place, fact in enumerate(facts):
            info = jnp.where((row == k) & (lane == 32 + place), fact, info)
    for b in range(2):
        msg_ref[:, b * LANE : (b + 1) * LANE] = jnp.where(
            row < IMAGES, both_halves(sums[2 + b]), both_halves(sums[4 + b])
        )
    msg_ref[:, 2 * LANE :] = jnp.where(row < IMAGES, info, low.astype(F32))


def assemble_kernel(facts_ref, prob_ref, out_ref):
    out_ref[0, :, 0 : 2 * LANE] = facts_ref[:, 0 : 2 * LANE]
    out_ref[0, :, 2 * LANE :] = facts_ref[:, 2 * LANE :] + prob_ref[...]


def loss_part(images, all_images, cell_count, recv_refs, head_ref, rows_ref, means, small_ref):
    view = lax.axis_index("view")
    received = jnp.concatenate([ref[...] for ref in recv_refs], axis=0)
    count = received.shape[0] * 2 * images
    received = received.reshape(count, 3 * LANE)
    raw = received[:, 2 * LANE :]
    row = lax.broadcasted_iota(jnp.int32, (count, 1), 0)
    part = row & (2 * images - 1)
    once = part < images
    facts = jnp.where(once, raw, pltpu.roll(raw, images, 0))
    group, inner = row // (2 * images), received.shape[0] // (2 * images * len(recv_refs))
    offset = (group % inner) * len(recv_refs) + group // inner
    image = ((offset ^ lax.axis_index("dp")) * images + (part & (images - 1))).astype(F32)
    alpha = facts[:, 32:33]
    label = facts[:, 33:34]
    labelled = facts[:, 34:35]
    order = facts[:, 35:36]
    eye = row == lax.broadcasted_iota(jnp.int32, (count, count), 1)
    image_lane = jnp.sum(jnp.where(eye, image, 0.0), axis=0, keepdims=True)
    order_lane = jnp.sum(jnp.where(eye, order, 0.0), axis=0, keepdims=True)
    first_lane = jnp.sum(jnp.where(eye & once, 1.0, 0.0), axis=0, keepdims=True)
    is_one = jnp.where(view == 0, 1.0, 0.0)
    ours = is_one * image + (1.0 - is_one) * order
    theirs = is_one * order_lane + (1.0 - is_one) * image_lane
    match = jnp.where((ours == theirs) & (first_lane > 0.5), 1.0, 0.0).astype(BF16)
    valid = class_lanes(count)
    other = pltpu.roll(facts, LANE - 16, 1)
    target = dot(match, jnp.where(valid, other, 0.0).astype(BF16))
    log_prob = jnp.where(valid, log_softmax(jnp.where(valid, facts, 0.0), valid), 0.0)
    probs = jnp.where(valid, jnp.exp(log_prob), 0.0)
    lane = lax.broadcasted_iota(jnp.int32, (count, LANE), 1)
    onehot = jnp.where(lane.astype(F32) == label, 1.0, 0.0)
    total = jnp.sum(jnp.where(once, labelled, 0.0), axis=0, keepdims=True)
    mask = labelled * is_one
    away = probs - target
    grad_prob = CONS_WEIGHT / all_images * away
    grad = mask * (probs - onehot) / total + probs * (
        grad_prob - jnp.sum(probs * grad_prob, axis=1, keepdims=True)
    )
    grad_low = grad.astype(BF16)
    dmix = dot(grad_low, head_rows(head_ref)) / CELLS
    weights = (dmix * alpha, dmix * (1.0 - alpha))
    for b in range(2):
        product = weights[b] * received[:, b * LANE : (b + 1) * LANE]
        plain = column_sum(jnp.where(once, product, 0.0))
        normal = column_sum(jnp.where(once, 0.0, product))
        means[2 * b : 2 * b + 1, :] = plain / cell_count
        means[2 * b + 1 : 2 * b + 2, :] = normal / cell_count
        rows_ref[b] = weights[b]
        small_ref[16 + 2 * b : 16 + 2 * b + 1, :] = plain
        small_ref[16 + 2 * b + 1 : 16 + 2 * b + 2, :] = normal
    rows_ref[2] = dmix
    cross = -jnp.sum(
        jnp.where(once, mask * jnp.sum(onehot * log_prob, axis=1, keepdims=True), 0.0), axis=0, keepdims=True
    )
    consistency = jnp.sum(
        jnp.where(once, jnp.sum(away * away, axis=1, keepdims=True), 0.0), axis=0, keepdims=True
    )
    lane_row = lax.broadcasted_iota(jnp.int32, (1, LANE), 1)
    small_ref[20:21, :] = jnp.where(
        lane_row == 0, cross, jnp.where(lane_row == 1, consistency, jnp.where(lane_row == 2, total, 0.0))
    )
    small_ref[21:24, :] = jnp.zeros((3, LANE), F32)
    pooled = jnp.where(once, 0.0, raw).astype(BF16)
    small_ref[0:16, :] = dot_rows(grad_low, pooled)[0:16, :]


def pack_grad(ref, blocks):
    side_by_side = jnp.concatenate(blocks + [jnp.zeros((CH, BLOCKS * LANE - WIDE), F32)], axis=1)
    for k in range(BLOCKS):
        ref[k * CH : (k + 1) * CH, :] = side_by_side[:, k * LANE : (k + 1) * LANE]


def keep_and_send(keep_ref, send_ref, blocks):
    view = lax.axis_index("view")
    for own, ref in ((0, keep_ref), (1, send_ref)):
        @pl.when(view == own)
        def _():
            pack_grad(ref, blocks[0])

        @pl.when(view != own)
        def _():
            pack_grad(ref, blocks[1])


def back_second_kernel(
    cell_count, all_images,
    second_ref, first_ref, bent_two, bent_one, recv1_ref, recv2_ref, recv3_ref, norm, head_ref, w_ref,
    du_ref, frames, msg_ref, small_ref, dmix_ref,
    terms1, terms2, rows_ref, means,
):
    rows = 2 * IMAGES
    norm_rows(total_of(recv1_ref), norm, terms1, 0, 0, cell_count)
    norm_rows(total_of(recv2_ref), norm, terms2, 0, 1, cell_count)
    loss_part(IMAGES, all_images, cell_count, recv3_ref, head_ref, rows_ref, means, small_ref)
    dmix_ref[...] = rows_ref[2, 0:rows, :]
    scales, linears, offsets = [], [], []
    for b in range(2):
        gain = term(terms2, b, 4)
        mean, slant = means[2 * b : 2 * b + 1, :], means[2 * b + 1 : 2 * b + 2, :]
        scales.append(0.5 * gain * rows_ref[b, 0:rows, :])
        linears.append(-gain * slant * term(terms2, b, 2))
        offsets.append(scales[b] - gain * (mean + slant * term(terms2, b, 3)))
    sums = [0.0] * 4
    carry = [blank_line()] * 2
    for b in range(2):
        clear_frame(frames.at[b])
    for step in range(STEPS):
        first_line, end = new_lines(step)
        for b in range(2):
            lanes = slice(b * LANE, (b + 1) * LANE)
            values = second_ref[first_line * LINE : end * LINE, lanes]
            bent = bent_two[first_line * LINE : end * LINE, lanes]
            shape = (values.shape[0] // 8, 8, LANE)
            dy = (bent.reshape(shape) * scales[b][None] + offsets[b][None]).reshape(values.shape) + values * linears[b]
            frame_line(frames.at[b], first_line, dy)
            dh, carry[b] = fold_lines(dot(taps(frames.at[b], step, (0, 1)), w_ref[b]), carry[b])
            before = first_ref[chunk_rows(step), lanes]
            du = dh + dh * bent_one[chunk_rows(step), lanes]
            du_ref[chunk_rows(step), lanes] = du
            sums[2 * b] += eight(du)
            sums[2 * b + 1] += eight(du * before)
    for b in range(2):
        plain, product = column_sum(sums[2 * b]), column_sum(sums[2 * b + 1])
        sums[2 * b] = plain
        sums[2 * b + 1] = term(terms1, b, 2) * product + term(terms1, b, 3) * plain
    spread_sums(msg_ref, sums)


def middle_lines(frame, first_line):
    return frame[first_line + 1 : first_line + 1 + DEEP, 1 : ACROSS + 1].reshape(CHUNK, frame.shape[-1])


def second_weight_kernel(other, frame_ref, dy_ref, grad_ref, gacc):
    view = lax.axis_index("view")
    branch = 1 - view if other else view
    for step in range(STEPS):
        pair = jnp.concatenate(
            [middle_lines(dy_ref.at[branch], step * DEEP), middle_lines(dy_ref.at[branch], step * DEEP + 1)], axis=1
        )
        product = dot_rows(pair, taps(frame_ref.at[branch], step, (0, 1)))
        gacc[...] = product if step == 0 else gacc[...] + product
    blocks = []
    for tap in range(TAPS):
        ky, kx = tap // 3, tap % 3
        row = LANE if ky == 0 else 0
        lane = (ky // 2) * 3 * LANE + kx * LANE
        blocks.append(gacc[row : row + CH, lane : lane + CH])
    pack_grad(grad_ref, blocks)


def back_weight_kernel(
    cell_count,
    du_ref, first_ref, low_ref, recv1_ref, recv5_ref, norm, small_ref,
    frame_ref, keep_ref, send_ref,
    terms1, gacc,
):
    norm_rows(total_of(recv1_ref), norm, terms1, 0, 0, cell_count)
    sums = total_of(recv5_ref)
    for ref in (keep_ref, send_ref):
        ref[GRAD_ROWS : GRAD_ROWS + 24, :] = small_ref[...]
        ref[GRAD_ROWS + 24 :, :] = sums
    means = sums / cell_count
    for b in range(2):
        clear_frame(frame_ref.at[b])
    for step in range(STEPS):
        parts = []
        for b in range(2):
            lanes = slice(b * LANE, (b + 1) * LANE)
            normal = first_ref[chunk_rows(step), lanes] * term(terms1, b, 2) + term(terms1, b, 3)
            parts.append(term(terms1, b, 4) * (
                du_ref[chunk_rows(step), lanes] - means[2 * b : 2 * b + 1, :] - normal * means[2 * b + 1 : 2 * b + 2, :]
            ))
        pair = jnp.concatenate(parts, axis=1)
        for b in range(2):
            frame_line(frame_ref.at[b], step * DEEP, parts[b])
        product = dot_rows(pair.astype(BF16), taps(low_ref, step, (-1, 0, 1)))
        gacc[...] = product if step == 0 else gacc[...] + product
    keep_and_send(
        keep_ref, send_ref,
        [[gacc[b * LANE : b * LANE + CH, tap * LANE : tap * LANE + CH] for tap in range(TAPS)] for b in range(2)],
    )


def back_stem_kernel(frame_ref, moved_ref, dmix_ref, w_ref, stem_ref):
    carry = blank_line()
    total = 0.0
    products = []
    for step in range(STEPS):
        if step % 2 == 0:
            products = [[dot(taps(frame_ref.at[b], step + k, (0, 1)), w_ref[b]) for k in range(2)] for b in range(2)]
        both = products[0][step % 2] + products[1][step % 2]
        dstem, carry = fold_lines(both, carry)
        dstem = (dstem.reshape(CHUNK // 8, 8, LANE) + dmix_ref[...][None]).reshape(CHUNK, LANE)
        total += dot(image_taps(moved_ref, step * DEEP, DEEP), dstem.astype(BF16))
    rows = [total[stem_row(tap) : stem_row(tap) + 3, :] for tap in range(TAPS)]
    stem_ref[...] = jnp.concatenate(rows, axis=0)


def code(values):
    top = jnp.max(jnp.abs(values), axis=0, keepdims=True)
    power = jnp.clip(jnp.ceil(jnp.log2(jnp.maximum(top, 1e-30)) + 0.01), -100.0, 100.0)
    counted = jnp.round(values * (jnp.exp2(-power) * CODE_TOP))
    return counted, power


def unit(power):
    return jnp.exp2(power) * (1.0 / CODE_TOP)


def coded_rows(values, rows):
    counted, power = code(values)
    parts = [counted, power]
    if rows - values.shape[0] - 1:
        parts.append(jnp.zeros((rows - values.shape[0] - 1, LANE), F32))
    return jnp.concatenate(parts, axis=0).astype(jnp.int32).astype(jnp.int16)


def decoded(values, count):
    whole_part = values.astype(jnp.int32).astype(F32)
    return whole_part[:count] * unit(whole_part[count : count + 1])


def encode_kernel(keep2, recv2, keep1, recv1, *refs):
    outs, total = refs[:-1], refs[-1]
    for k, (keep, recv) in enumerate(((keep1, recv1), (keep2, recv2))):
        total[k] = keep[0:GRAD_ROWS, :] + recv[0:GRAD_ROWS, :]
    mine = lax.axis_index("dp") & (QUARTERS - 1)
    for offset, out in enumerate(outs):
        place = pl.multiple_of((mine ^ offset) * SHARE, 8)
        for k in range(2):
            out[k * PIECE : (k + 1) * PIECE, :] = coded_rows(total[k, pl.ds(place, SHARE), :], PIECE)


def summed(refs, first, count, rows):
    total = decoded(refs[0][first : first + rows, :], count)
    for ref in refs[1:]:
        total += decoded(ref[first : first + rows, :], count)
    return total


def combine_kernel(recv_refs, stem_ref, out_ref):
    for k in range(2):
        out_ref[k * PIECE : (k + 1) * PIECE, :] = coded_rows(summed(recv_refs, k * PIECE, SHARE, PIECE), PIECE)
    out_ref[2 * PIECE :, :] = coded_rows(stem_ref[...], SIDE)


def recode_kernel(recv_refs, out_ref):
    for k in range(2):
        out_ref[k * PIECE : (k + 1) * PIECE, :] = coded_rows(summed(recv_refs, k * PIECE, SHARE, PIECE), PIECE)
    out_ref[2 * PIECE :, :] = coded_rows(summed(recv_refs, 2 * PIECE, 27, SIDE), SIDE)


def stack_kernel(inner, parts, out_ref):
    count = parts[0].shape[0]
    for k, part in enumerate(parts):
        if inner:
            for entry in range(count):
                out_ref[entry * len(parts) + k] = part[entry]
        else:
            out_ref[k * count : (k + 1) * count] = part[...]


def adam_terms(gradient, factor, weight, first, second, teacher):
    clipped = gradient * factor
    first_new = BETA_FIRST * first + (1.0 - BETA_FIRST) * clipped
    second_new = BETA_SECOND * second + (1.0 - BETA_SECOND) * (clipped * clipped)
    second_hat = second_new * (1.0 / (1.0 - BETA_SECOND**STEP))
    weight_new = weight * (1.0 - LEARN_RATE * WEIGHT_DECAY) - (
        first_new * (LEARN_RATE / (1.0 - BETA_FIRST**STEP)) / (jnp.sqrt(second_hat) + ADAM_EPS)
    )
    return weight_new, first_new, second_new, TEACHER_KEEP * teacher + (1.0 - TEACHER_KEEP) * weight_new


def update_kernel(
    own_codes, other_codes, own_facts, other_facts,
    cw, cf, cs, ct, sw, sf, ss, st, hw, hf, hs, ht, nw, nf, ns, nt,
    cw_o, cf_o, cs_o, ct_o, cb_o, sw_o, sf_o, ss_o, st_o, sb_o, hw_o, hf_o, hs_o, ht_o, hb_o,
    nw_o, nf_o, ns_o, nt_o, norm_o, cross_o, count_o, consistency_o,
    factor_ref, own_ref, other_ref,
):
    conv = pl.program_id(0)
    view = lax.axis_index("view")

    @pl.when(conv == 0)
    def _():
        facts = own_facts[GRAD_ROWS:, :] + other_facts[GRAD_ROWS:, :]
        small, sums = facts[:24], facts[24:]
        mine = lax.axis_index("dp") & (QUARTERS - 1)
        stem = jnp.zeros((27, LANE), F32)
        for codes, ref in ((own_codes, own_ref), (other_codes, other_ref)):
            for offset, source in enumerate(codes):
                place = pl.multiple_of((mine ^ offset) * SHARE, 8)
                for k in range(2):
                    ref[k, pl.ds(place, SHARE), :] = decoded(source[k * PIECE : (k + 1) * PIECE, :], SHARE)
            stem += summed(codes, 2 * PIECE, 27, SIDE)
        stem = stem[:, :CH]
        head = small[:CLASSES, :CH]
        gains = jnp.concatenate([sums[1:2], small[17:18], sums[3:4], small[19:20]], axis=0)[:, :CH]
        shifts = jnp.concatenate([sums[0:1], small[16:17], sums[2:3], small[18:19]], axis=0)[:, :CH]
        total = jnp.zeros((1, 1), F32)
        for part in (stem, head, gains, shifts):
            total += jnp.sum(jnp.sum(part * part, axis=1, keepdims=True), axis=0, keepdims=True)
        for ref in (own_ref, other_ref):
            for k in range(2):
                values = ref[k, 0:GRAD_ROWS, :]
                column = jnp.sum(values * values, axis=0, keepdims=True)
                total += jnp.sum(column, axis=1, keepdims=True)
        norm = jnp.sqrt(total)
        factor = CLIP_LIMIT / jnp.maximum(norm, CLIP_LIMIT)
        factor_ref[...] = jnp.broadcast_to(factor, factor_ref.shape)
        norm_o[...] = norm
        cross_o[...] = small[20:21, 0:1]
        consistency_o[...] = small[20:21, 1:2]
        count_o[...] = own_facts[GRAD_ROWS + 20 : GRAD_ROWS + 21, 2:3]
        sw_o[...], sf_o[...], ss_o[...], st_o[...] = adam_terms(stem, factor, sw[...], sf[...], ss[...], st[...])
        sb_o[...] = sw_o[...].astype(BF16)
        hw_o[...], hf_o[...], hs_o[...], ht_o[...] = adam_terms(head, factor, hw[...], hf[...], hs[...], ht[...])
        hb_o[...] = hw_o[...].astype(BF16)
        for k, part in enumerate((gains, shifts)):
            nw_o[k], nf_o[k], ns_o[k], nt_o[k] = adam_terms(part, factor, nw[k], nf[k], ns[k], nt[k])

    def update(ref, second):
        factor = factor_ref[0:1, 0:1]
        for k in range(BLOCKS):
            lanes = slice(k * LANE, min((k + 1) * LANE, WIDE))
            gradient = ref[second, k * CH : (k + 1) * CH, 0 : lanes.stop - lanes.start]
            weight, first, second_moment, teacher = adam_terms(
                gradient, factor, cw[conv, :, lanes], cf[conv, :, lanes], cs[conv, :, lanes], ct[conv, :, lanes]
            )
            cw_o[:, lanes] = weight
            cf_o[:, lanes] = first
            cs_o[:, lanes] = second_moment
            ct_o[:, lanes] = teacher
            cb_o[:, lanes] = weight.astype(BF16)

    mine = conv // 2 == view

    @pl.when(mine)
    def _():
        update(own_ref, conv & 1)

    @pl.when(jnp.logical_not(mine))
    def _():
        update(other_ref, conv & 1)


def whole(shape):
    return pl.BlockSpec(shape, lambda i: (0,) * len(shape))


def scalars():
    return pl.BlockSpec(memory_space=pltpu.SMEM)


def conv_part(k):
    return pl.BlockSpec((None, CH, WIDE), lambda i: (k, 0, 0))


def held():
    return pl.BlockSpec(memory_space=pltpu.VMEM)


def hold(values):
    return pltpu.with_memory_space_constraint(values, pltpu.VMEM)


def struct(shape, kind=F32):
    return jax.ShapeDtypeStruct(shape, kind)


def to_partner(values, difference):
    size = lax.axis_size("dp")
    return lax.ppermute(values, ("view", "dp"), [(i, i ^ (difference + size)) for i in range(2 * size)])


def far_last(ways):
    return (1, 3, 2) if ways == 4 else range(1, ways)


def from_partners(values, shift, ways):
    parts = [to_partner(values, 0)] + [None] * (ways - 1)
    for offset in far_last(ways):
        parts[offset] = to_partner(values, offset << shift)
    return parts


def stages():
    size = lax.axis_size("dp")
    groups = []
    shift = 0
    while (1 << shift) < size:
        ways = min(4, size >> shift)
        groups.append((shift, ways))
        shift += 2
    assert len(groups) % 2 == 0
    return groups


def sum_parts(values, beside=None):
    groups = stages()
    for shift, ways in groups[:-1]:
        parts = from_partners(values, shift, ways)
        if beside is not None:
            parts, beside = lax.optimization_barrier((parts, beside))
        values = sum(parts)
    return tuple(from_partners(values, *groups[-1])), beside


def stack(parts, inner):
    shape = (len(parts) * parts[0].shape[0],) + parts[0].shape[1:]
    return pl.pallas_call(
        functools.partial(stack_kernel, inner), out_shape=struct(shape, parts[0].dtype), compiler_params=PARAMS, name="stack"
    )(tuple(parts))


def gather_parts(values, groups):
    inner = groups[0][0] > 0
    for shift, ways in groups[:-1]:
        values = stack(from_partners(values, shift, ways), inner)
    return tuple(from_partners(values, *groups[-1]))


def swap_view(values):
    return lax.ppermute(values, "view", [(0, 1), (1, 0)])


def forward_weights(conv):
    shape = (2, 6 * LANE, 2 * LANE)
    return pl.pallas_call(
        forward_weight_kernel,
        grid=(2,),
        in_specs=[pl.BlockSpec((None, CH, WIDE), lambda i: (2 * i + 1, 0, 0))],
        out_specs=pl.BlockSpec((None,) + shape[1:], lambda i: (i, 0, 0)),
        out_shape=struct(shape, BF16),
        compiler_params=PARAMS,
        cost_estimate=pl.CostEstimate(flops=2_000_000_000, bytes_accessed=4_000_000, transcendentals=0),
        name="forward_weight",
    )(conv)


def backward_weights(conv):
    return pl.pallas_call(
        backward_weight_kernel,
        grid=(1,),
        in_specs=[conv_part(k) for k in range(4)],
        out_specs=[whole((2, 6 * LANE, 2 * LANE))] * 2,
        out_shape=[struct((2, 6 * LANE, 2 * LANE), BF16)] * 2,
        compiler_params=PARAMS,
        cost_estimate=pl.CostEstimate(flops=4_000_000_000, bytes_accessed=8_000_000, transcendentals=0),
        name="backward_weight",
    )(conv, conv, conv, conv)


def shards(
    augmented, shake_ratio, labels, labelled, view_order,
    stem_weight, conv_weight, head_weight, norm_param,
    teacher_stem, teacher_conv, teacher_head, teacher_norm,
    first_stem, first_conv, first_head, first_norm,
    second_stem, second_conv, second_head, second_norm,
):
    dp = lax.axis_size("dp")
    all_images = IMAGES * dp
    cell_count = float(all_images * CELLS)
    rows = dp * 2 * IMAGES
    conv, conv_t, conv_f, conv_s = (
        jnp.transpose(v, (0, 2, 1)) for v in (conv_weight, teacher_conv, first_conv, second_conv)
    )
    head, head_t, head_f, head_s = (v.T for v in (head_weight, teacher_head, first_head, second_head))
    pixels = jnp.transpose(augmented[0], (0, 3, 1, 2))
    msg = struct((8, LANE))
    groups = stages()
    last_ways = groups[-1][1]
    recv_spec = (held(),) * last_ways
    norm_spec = whole((2, 4, CH))
    head_spec = whole((CLASSES, CH))
    moved_shape = (3, (SIDE + 4) * 8, LANE)
    frame_one, frame_two = FRAME + (LANE,), (2,) + FRAME + (LANE,)
    values_shape, grad_shape = (ALL, 2 * LANE), struct((GRAD_ROWS, LANE))
    terms_scratch = pltpu.VMEM((16, LANE), F32)

    first_s, first_t, low, moved, stem_sums, message = pl.pallas_call(
        first_kernel,
        in_specs=[pl.BlockSpec(memory_space=pltpu.HBM)] * 5,
        out_specs=[held()] * 6,
        out_shape=[
            pltpu.VMEM(values_shape, F32), pltpu.VMEM(values_shape, F32), pltpu.VMEM(frame_one, BF16),
            pltpu.VMEM(moved_shape, F32), struct((2, 8, LANE)), msg,
        ],
        scratch_shapes=[
            pltpu.VMEM(moved_shape[1:], F32), pltpu.VMEM((STEM_ROWS, 2 * LANE), F32),
            pltpu.VMEM((STEM_ROWS, 2 * LANE), BF16), pltpu.VMEM((2, 9 * LANE, 2 * LANE), BF16),
            pltpu.VMEM(frame_one, BF16), pltpu.VMEM((IMAGES, 3, SIDE, SIDE), BF16), pltpu.VMEM((27, CH), F32),
            pltpu.VMEM((27, CH), F32), pltpu.VMEM((4, CH, WIDE), F32), pltpu.SemaphoreType.DMA((7,)),
        ],
        compiler_params=PARAMS,
        name="first_conv",
    )(*(pltpu.with_memory_space_constraint(v, pltpu.HBM) for v in (pixels, stem_weight, teacher_stem, conv, conv_t)))
    first_s, first_t, low, moved = (hold(v) for v in (first_s, first_t, low, moved))
    recv1, (weight_s, weight_t, (back_weight_two, back_weight_one)) = sum_parts(
        message, (forward_weights(conv), forward_weights(conv_t), backward_weights(conv))
    )

    second_s, second_t, hidden, bent_one, message = pl.pallas_call(
        functools.partial(second_kernel, cell_count),
        in_specs=[held()] * 2 + [recv_spec] + [held()] * 4,
        out_specs=[held()] * 5,
        out_shape=[pltpu.VMEM(values_shape, F32)] * 2 + [pltpu.VMEM(frame_two, BF16), pltpu.VMEM(values_shape, F32), msg],
        scratch_shapes=[pltpu.VMEM(frame_two, BF16), terms_scratch, terms_scratch],
        compiler_params=PARAMS,
        name="second_conv",
    )(first_s, first_t, recv1, norm_param, teacher_norm, weight_s, weight_t)
    second_s, second_t, hidden, bent_one = (hold(v) for v in (second_s, second_t, hidden, bent_one))
    recv2, _ = sum_parts(message)

    prob = pl.pallas_call(
        functools.partial(teacher_kernel, cell_count),
        in_specs=[scalars(), held(), recv_spec] + [held()] * 3,
        out_specs=held(),
        out_shape=struct((8, LANE)),
        scratch_shapes=[terms_scratch],
        compiler_params=PARAMS,
        name="teacher_logits",
    )(shake_ratio, second_t, recv2, teacher_norm, head_t, stem_sums)
    other = swap_view(prob)
    facts, bent_two = pl.pallas_call(
        functools.partial(student_kernel, cell_count),
        in_specs=[scalars()] * 4 + [held(), recv_spec] + [held()] * 3,
        out_specs=[held()] * 2,
        out_shape=[struct((8, 3 * LANE)), pltpu.VMEM(values_shape, F32)],
        scratch_shapes=[terms_scratch],
        compiler_params=PARAMS,
        cost_estimate=pl.CostEstimate(flops=4_000_000_000, bytes_accessed=8_000_000, transcendentals=0),
        name="student_logits",
    )(shake_ratio, labels, labelled, view_order, second_s, recv2, norm_param, head, stem_sums)
    bent_two = hold(bent_two)
    facts, other = lax.optimization_barrier((facts, other))
    facts = pl.pallas_call(
        assemble_kernel, out_shape=struct((1, 8, 3 * LANE)), compiler_params=PARAMS, name="assemble"
    )(facts, other)
    recv3 = gather_parts(facts, groups[::-1])

    du, dy, message, small, dmix = pl.pallas_call(
        functools.partial(back_second_kernel, cell_count, float(all_images)),
        in_specs=[held()] * 4 + [recv_spec] * 2 + [(held(),) * groups[0][1]] + [held()] * 3,
        out_specs=[held()] * 5,
        out_shape=[
            pltpu.VMEM(values_shape, F32), pltpu.VMEM(frame_two, BF16), msg, struct((24, LANE)), struct((8, LANE)),
        ],
        scratch_shapes=[
            terms_scratch, terms_scratch, pltpu.VMEM((3, rows, LANE), F32), pltpu.VMEM((8, LANE), F32),
        ],
        compiler_params=PARAMS,
        name="back_second",
    )(second_s, first_s, bent_two, bent_one, recv1, recv2, recv3, norm_param, head, back_weight_two)
    du, dy = hold(du), hold(dy)

    def second_weight(other):
        return pl.pallas_call(
            functools.partial(second_weight_kernel, other),
            in_specs=[held()] * 2,
            out_specs=held(),
            out_shape=grad_shape,
            scratch_shapes=[pltpu.VMEM((2 * LANE, 6 * LANE), F32)],
            compiler_params=PARAMS,
            cost_estimate=pl.CostEstimate(flops=4_000_000_000, bytes_accessed=8_000_000, transcendentals=0),
            name="second_weight",
        )(hidden, dy)

    send2, keep2 = second_weight(True), second_weight(False)
    recv5, send2 = sum_parts(message, send2)
    recv_grad2 = swap_view(send2)
    recv5, keep2, recv_grad2 = lax.optimization_barrier((recv5, keep2, recv_grad2))

    frame, keep1, send1 = pl.pallas_call(
        functools.partial(back_weight_kernel, cell_count),
        in_specs=[held()] * 3 + [recv_spec] * 2 + [held()] * 2,
        out_specs=[held()] * 3,
        out_shape=[pltpu.VMEM(frame_two, BF16)] + [struct((GRAD_ROWS + 32, LANE))] * 2,
        scratch_shapes=[terms_scratch, pltpu.VMEM((2 * LANE, 9 * LANE), F32)],
        compiler_params=PARAMS,
        cost_estimate=pl.CostEstimate(flops=8_000_000_000, bytes_accessed=16_000_000, transcendentals=0),
        name="back_weight",
    )(du, first_s, low, recv1, recv5, norm_param, small)
    frame = hold(frame)
    recv_grad1 = swap_view(send1)
    coded = pl.pallas_call(
        encode_kernel,
        out_shape=[struct((2 * PIECE, LANE), jnp.int16)] * QUARTERS,
        scratch_shapes=[pltpu.VMEM((2, GRAD_ROWS, LANE), F32)],
        compiler_params=PARAMS,
        name="encode",
    )(keep2, recv_grad2, keep1, recv_grad1)
    scattered = [to_partner(coded[0], 0)] + [None] * (QUARTERS - 1)
    for offset in far_last(QUARTERS):
        scattered[offset] = to_partner(coded[offset], offset)
    scattered = tuple(scattered)

    stem_grad = pl.pallas_call(
        back_stem_kernel,
        in_specs=[held()] * 4,
        out_specs=held(),
        out_shape=struct((27, LANE)),
        compiler_params=PARAMS,
        cost_estimate=pl.CostEstimate(flops=8_000_000_000, bytes_accessed=16_000_000, transcendentals=0),
        name="back_stem",
    )(frame, moved, dmix, back_weight_one)

    stem_grad, scattered = lax.optimization_barrier((stem_grad, scattered))
    code_shape = struct((CODE_ROWS, LANE), jnp.int16)
    codes = pl.pallas_call(combine_kernel, out_shape=code_shape, compiler_params=PARAMS, name="combine")(
        scattered, stem_grad
    )
    for group in groups[1:]:
        codes = pl.pallas_call(recode_kernel, out_shape=code_shape, compiler_params=PARAMS, name="recode")(
            tuple(from_partners(codes, *group))
        )
    other_grads = tuple(from_partners(codes, *groups[0]))
    own = tuple(swap_view(part) for part in other_grads)

    conv_block = pl.BlockSpec((None, CH, WIDE), lambda i: (i, 0, 0))
    stem_block, norm_block = whole((27, CH)), norm_spec
    code_spec = (held(),) * QUARTERS
    grads_scratch = pltpu.VMEM((2, GRAD_ROWS, LANE), F32)
    outs = pl.pallas_call(
        update_kernel,
        grid=(4,),
        in_specs=[code_spec] * 2 + [held()] * 18,
        out_specs=[conv_block] * 5 + [stem_block] * 5 + [head_spec] * 5 + [norm_block] * 4 + [whole((1, 1))] * 4,
        out_shape=[struct((4, CH, WIDE))] * 4 + [struct((4, CH, WIDE), BF16)]
        + [struct((27, CH))] * 4 + [struct((27, CH), BF16)]
        + [struct((CLASSES, CH))] * 4 + [struct((CLASSES, CH), BF16)]
        + [struct((2, 4, CH))] * 4 + [struct((1, 1))] * 4,
        scratch_shapes=[pltpu.VMEM((8, LANE), F32), grads_scratch, grads_scratch],
        compiler_params=PARAMS,
        name="update",
    )(
        own, other_grads, keep1, recv_grad1,
        conv, conv_f, conv_s, conv_t, stem_weight, first_stem, second_stem, teacher_stem,
        head, head_f, head_s, head_t, norm_param, first_norm, second_norm, teacher_norm,
    )
    convs = [jnp.transpose(v, (0, 2, 1)) for v in outs[:5]]
    stems = outs[5:10]
    heads = [v.T for v in outs[10:15]]
    norms = outs[15:19]
    return (
        *(v.reshape(()) for v in outs[19:23]),
        *stems[:4], *convs[:4], *heads[:4], *norms, stems[4], convs[4], heads[4],
    )


def solution(mesh):
    in_specs = (
        (P("view", "dp", None, None, None), P("view", "dp"), P("dp"), P("dp")) + (P(),) * 17
    )
    return jax.shard_map(shards, mesh=mesh, in_specs=in_specs, out_specs=(P(),) * 23, check_vma=False)
```

```python
import functools

import jax
import jax.numpy as jnp
from jax import lax
from jax.experimental import pallas as pl
from jax.experimental.pallas import tpu as pltpu
from jax.sharding import PartitionSpec as P

CLASSES = 10
STEP = 5
EPS_NORM = 1e-05
LEARN_RATE = 0.03
BETA_FIRST = 0.5
BETA_SECOND = 0.5
WEIGHT_DECAY = 0.0001
ADAM_EPS = 1e-08
CLIP_LIMIT = 0.02
TEACHER_KEEP = 0.9
CONS_WEIGHT = 10.0

F32 = jnp.float32
BF16 = jnp.bfloat16
LANE = 128
CH = 96
SIDE = 32
CELLS = SIDE * SIDE
IMAGES = 4
QUARTERS = 4
ACROSS = SIDE // QUARTERS
TILE = IMAGES * QUARTERS
LINE = ACROSS * TILE
STEPS = 4
DEEP = SIDE // STEPS
CHUNK = DEEP * LINE
ALL = SIDE * LINE
BLOCK = 64
TAPS = 9
WIDE = TAPS * CH
BLOCKS = -(-WIDE // LANE)
GRAD_ROWS = BLOCKS * CH
SHARE = GRAD_ROWS // QUARTERS
PIECE = -(-(SHARE + 1) // 16) * 16
CODE_ROWS = 2 * PIECE + SIDE
STEM_ROWS = 80
CODE_TOP = 32000.0
FRAME = (SIDE + 2, ACROSS + 2, TILE)
PARAMS = pltpu.CompilerParams(vmem_limit_bytes=14 * 1024 * 1024)


def dot(a, b):
    return jnp.dot(a, b, preferred_element_type=F32)


def dot_rows(a, b):
    return lax.dot_general(a, b, (((0,), (0,)), ((), ())), preferred_element_type=F32)


def dot_lanes(a, b):
    return lax.dot_general(a, b, (((1,), (1,)), ((), ())), preferred_element_type=F32)


def frame_line(frame, first_line, values):
    lines = values.shape[0] // LINE
    width = values.shape[1]
    tiles = values.reshape(lines, ACROSS, TILE, width)
    row = lax.broadcasted_iota(jnp.int32, (1, TILE, 1), 1)
    before = jnp.where(row >= IMAGES, pltpu.roll(tiles[:, ACROSS - 1], IMAGES, 1), 0.0)
    after = jnp.where(row < TILE - IMAGES, pltpu.roll(tiles[:, 0], TILE - IMAGES, 1), 0.0)
    place = slice(first_line + 1, first_line + 1 + lines)
    frame[place, 1 : ACROSS + 1] = tiles.astype(BF16)
    frame[place, 0] = before.astype(BF16)
    frame[place, ACROSS + 1] = after.astype(BF16)


def clear_frame(frame):
    blank = jnp.zeros(frame.shape[1:], BF16)
    frame[0] = blank
    frame[SIDE + 1] = blank


def taps(frame, step, rows):
    parts = []
    for dy in rows:
        for kx in range(3):
            place = step * DEEP + 1 + dy
            lines = frame[place : place + DEEP, kx : kx + ACROSS]
            parts.append(lines.reshape(CHUNK, lines.shape[-1]))
    return jnp.concatenate(parts, axis=1)


def fold_lines(both, carry):
    upper = jnp.concatenate([carry, both[: CHUNK - LINE, LANE:]], axis=0)
    return both[:, :LANE] + upper, both[CHUNK - LINE :, LANE:]


def blank_line():
    return jnp.zeros((LINE, LANE), F32)


def new_lines(step):
    first = 0 if step == 0 else step * DEEP + 1
    return first, min((step + 1) * DEEP + 1, SIDE)


def chunk_rows(step):
    return slice(step * CHUNK, (step + 1) * CHUNK)


def eight(values):
    parts = values.reshape(values.shape[0] // 8, 8, values.shape[1])
    while parts.shape[0] > 1:
        middle = parts.shape[0] // 2
        rest = parts[2 * middle :]
        parts = parts[:middle] + parts[middle : 2 * middle]
        if rest.shape[0]:
            parts = jnp.concatenate([parts[:-1], parts[-1:] + rest], axis=0) if middle > 1 else parts + rest
    return parts[0]


def both_halves(sums):
    return sums + pltpu.roll(sums, IMAGES, 0)


def tap_block(raw, tap):
    return raw[:, tap * CH : (tap + 1) * CH]


def image_lines(image_ref, plain, moved):
    plain[...] = jnp.zeros(plain.shape, F32)
    for channel in range(3):
        side_by_side = jnp.concatenate([image_ref[i, channel].astype(F32) for i in range(IMAGES)], axis=1)
        plain[pl.ds(8 + channel, SIDE, stride=8), :] = side_by_side
    source = lax.broadcasted_iota(jnp.int32, (LANE, LANE), 0)
    target = lax.broadcasted_iota(jnp.int32, (LANE, LANE), 1)
    same = source // SIDE == (target & (IMAGES - 1))
    across = ((target // IMAGES) & (QUARTERS - 1)) * ACROSS + target // TILE
    for kx in range(3):
        picks = jnp.where(same & ((source & (SIDE - 1)) == across + (kx - 1)), 1.0, 0.0).astype(BF16)
        moved[kx] = dot(plain[...].astype(BF16), picks)


def image_taps(moved, first_line, lines):
    columns = []
    for line in range(lines):
        place = (first_line + line) * 8
        parts = [moved[kx, place : place + 24, :] for kx in range(3)]
        columns.append(jnp.concatenate(parts + [jnp.zeros((8, LANE), F32)], axis=0))
    return jnp.concatenate(columns, axis=1).astype(BF16)


def stem_row(tap):
    return (tap % 3) * 24 + (tap // 3) * 8


def pad_lanes(row):
    return jnp.concatenate([row, jnp.zeros((row.shape[0], LANE - row.shape[1]), row.dtype)], axis=1)


def norm_terms(sums, squares, cell_count):
    average = sums / cell_count
    inverse = lax.rsqrt(squares / cell_count - average * average + EPS_NORM)
    return average, inverse


def column_sum(values):
    return jnp.sum(values, axis=0, keepdims=True)


def slope_rest(half, tanh, product):
    return (tanh + half) - product * tanh


def first_kernel(
    image_hbm, stem_s_hbm, stem_t_hbm, raw_s, raw_t,
    first_s, first_t, frame_s, moved_ref, pooled_ref, msg_ref,
    plain, wst32, wst, wf, frame_t, image_ref, stem_s, stem_t, raw, sems,
):
    coming = [
        pltpu.make_async_copy(source, target, sems.at[k])
        for k, (source, target) in enumerate((
            (image_hbm, image_ref), (stem_s_hbm, stem_s), (stem_t_hbm, stem_t),
            (raw_s.at[0], raw.at[0]), (raw_s.at[2], raw.at[1]), (raw_t.at[0], raw.at[2]), (raw_t.at[2], raw.at[3]),
        ))
    ]
    for copy in coming:
        copy.start()
    wf[...] = jnp.zeros(wf.shape, BF16)
    wst32[...] = jnp.zeros(wst32.shape, F32)
    clear_frame(frame_s)
    clear_frame(frame_t)
    for copy in coming[:3]:
        copy.wait()
    image_lines(image_ref, plain, moved_ref)
    for n, stem in enumerate((stem_s, stem_t)):
        for tap in range(TAPS):
            row = stem_row(tap)
            wst32[row : row + 3, n * LANE : n * LANE + CH] = stem[3 * tap : 3 * tap + 3, :]
    wst[...] = wst32[...].astype(BF16)
    for copy in coming[3:]:
        copy.wait()
    for n in range(2):
        for b in range(2):
            for tap in range(TAPS):
                wf[n, tap * LANE : tap * LANE + CH, b * LANE : b * LANE + CH] = jnp.transpose(
                    tap_block(raw.at[2 * n + b], tap)
                ).astype(BF16)
    pooled = [0.0, 0.0]
    sums = [0.0] * 8
    for step in range(STEPS):
        first_line, end = new_lines(step)
        stems = dot_rows(image_taps(moved_ref, first_line, end - first_line), wst[...])
        for n, (frame, out_ref) in enumerate(((frame_s, first_s), (frame_t, first_t))):
            stem = stems[:, n * LANE : (n + 1) * LANE]
            pooled[n] += eight(stem)
            frame_line(frame, first_line, stem)
            out = dot(taps(frame, step, (-1, 0, 1)), wf[n])
            out_ref[chunk_rows(step), :] = out
            for b in range(2):
                part = out[:, b * LANE : (b + 1) * LANE]
                sums[4 * n + 2 * b] += eight(part)
                sums[4 * n + 2 * b + 1] += eight(part * part)
    for n in range(2):
        pooled_ref[n] = both_halves(pooled[n])
    spread_sums(msg_ref, sums)


def total_of(refs):
    total = refs[0][...]
    for ref in refs[1:]:
        total = total + ref[...]
    return total


def spread_sums(msg_ref, sums):
    sums = [column_sum(part) for part in sums]
    if len(sums) < 8:
        sums.append(jnp.zeros((8 - len(sums), LANE), F32))
    msg_ref[...] = jnp.concatenate(sums, axis=0)


def forward_weight_kernel(raw_ref, w_ref):
    w_ref[...] = jnp.zeros(w_ref.shape, BF16)
    for ky in range(3):
        for kx in range(3):
            row = (ky // 2) * 3 * LANE + kx * LANE
            lane = LANE if ky == 0 else 0
            w_ref[row : row + CH, lane : lane + CH] = jnp.transpose(tap_block(raw_ref, ky * 3 + kx)).astype(BF16)


def backward_weight_kernel(cw0, cw1, cw2, cw3, two_ref, one_ref):
    two_ref[...] = jnp.zeros(two_ref.shape, BF16)
    one_ref[...] = jnp.zeros(one_ref.shape, BF16)
    for ky in range(3):
        for kx in range(3):
            tap = (2 - ky) * 3 + 2 - kx
            lane = LANE if ky == 0 else 0
            for b, (inner, outer) in enumerate(((cw0, cw1), (cw2, cw3))):
                row = (ky // 2) * 3 * LANE + kx * LANE
                two_ref[b, row : row + CH, lane : lane + CH] = (0.5 * tap_block(outer, tap)).astype(BF16)
                one_ref[b, row : row + CH, lane : lane + CH] = tap_block(inner, tap).astype(BF16)


def norm_rows(sums, norm, terms, first_row, norm_index, cell_count):
    for b in range(2):
        row = first_row + 2 * b
        average, inverse = norm_terms(sums[row : row + 1], sums[row + 1 : row + 2], cell_count)
        gain = pad_lanes(norm[0, 2 * b + norm_index : 2 * b + norm_index + 1, :])
        shift = pad_lanes(norm[1, 2 * b + norm_index : 2 * b + norm_index + 1, :])
        scale = inverse * gain
        terms[8 * b : 8 * b + 1, :] = 0.5 * scale
        terms[8 * b + 1 : 8 * b + 2, :] = 0.5 * (shift - average * scale)
        terms[8 * b + 2 : 8 * b + 3, :] = inverse
        terms[8 * b + 3 : 8 * b + 4, :] = -average * inverse
        terms[8 * b + 4 : 8 * b + 5, :] = scale


def term(terms, b, k):
    return terms[8 * b + k : 8 * b + k + 1, :]


def second_kernel(
    cell_count, first_s, first_t, recv_ref, norm_s, norm_t, ws_ref, wt_ref,
    second_s, second_t, frame_s, bent_ref, plain_ref, msg_ref,
    frame_t, terms_s, terms_t,
):
    received = total_of(recv_ref)
    norm_rows(received, norm_s, terms_s, 0, 0, cell_count)
    norm_rows(received, norm_t, terms_t, 4, 0, cell_count)
    nets = ((first_s, terms_s, frame_s, ws_ref, second_s), (first_t, terms_t, frame_t, wt_ref, second_t))
    sums = [0.0] * 8
    carry = [blank_line()] * 4
    for _, _, frames, _, _ in nets:
        for b in range(2):
            clear_frame(frames.at[b])
    for step in range(STEPS):
        first_line, end = new_lines(step)
        for n, (source, terms, frames, w, target) in enumerate(nets):
            for b in range(2):
                k = 2 * n + b
                lanes = slice(b * LANE, (b + 1) * LANE)
                half = source[first_line * LINE : end * LINE, lanes] * term(terms, b, 0) + term(terms, b, 1)
                tanh = jnp.tanh(half)
                product = half * tanh
                frame_line(frames.at[b], first_line, half + product)
                if n == 0:
                    bent_ref[first_line * LINE : end * LINE, lanes] = slope_rest(half, tanh, product)
                out, carry[k] = fold_lines(dot(taps(frames.at[b], step, (0, 1)), w[b]), carry[k])
                target[chunk_rows(step), lanes] = out
                sums[2 * k] += eight(out)
                sums[2 * k + 1] += eight(out * out)
    for k in range(4):
        plain_ref[k] = sums[2 * k]
    spread_sums(msg_ref, sums)


def head_rows(head_ref):
    padded = jnp.concatenate([head_ref[...], jnp.zeros((LANE - CLASSES, CH), F32)], axis=0)
    return pad_lanes(padded).astype(BF16)


def alpha_of(ratio_ref, image):
    return (ratio_ref[0, image].astype(F32) + 1.0) / 18.0


def alpha_rows(ratio_ref):
    row = lax.broadcasted_iota(jnp.int32, (2 * IMAGES, LANE), 0) & (IMAGES - 1)
    alpha = jnp.zeros((2 * IMAGES, LANE), F32)
    for k in range(IMAGES):
        alpha = jnp.where(row == k, alpha_of(ratio_ref, k), alpha)
    return alpha


def class_lanes(rows):
    return lax.broadcasted_iota(jnp.int32, (rows, LANE), 1) < CLASSES


def log_softmax(logits, valid):
    top = jnp.max(jnp.where(valid, logits, -3e38), axis=1, keepdims=True)
    moved = logits - top
    total = jnp.sum(jnp.where(valid, jnp.exp(moved), 0.0), axis=1, keepdims=True)
    return moved - jnp.log(total)


def facts_kernel(ratio_ref, labels_ref, labelled_ref, order_ref, facts_ref):
    dp_index = lax.axis_index("dp")
    facts_ref[0] = alpha_rows(ratio_ref)
    lane = lax.broadcasted_iota(jnp.int32, (2 * IMAGES, LANE), 1)
    row = lax.broadcasted_iota(jnp.int32, (2 * IMAGES, LANE), 0)
    info = jnp.zeros((2 * IMAGES, LANE), F32)
    for k in range(IMAGES):
        facts = (
            alpha_of(ratio_ref, k),
            labels_ref[k].astype(F32),
            labelled_ref[k].astype(F32),
            order_ref[dp_index * IMAGES + k].astype(F32),
        )
        for place, fact in enumerate(facts):
            info = jnp.where((row == k) & (lane == 32 + place), fact, info)
    facts_ref[1] = info


def pooled_low(alpha, sums, stem_sums):
    total = alpha * both_halves(sums[0]) + (1.0 - alpha) * both_halves(sums[1])
    return ((total + stem_sums) / CELLS).astype(BF16)


def teacher_kernel(
    cell_count, facts_ref, second_ref, recv_ref, norm, head_ref, stem_sum_ref, image_sum_ref,
    prob_ref,
    terms,
):
    norm_rows(total_of(recv_ref), norm, terms, 4, 1, cell_count)
    plain, curved = [image_sum_ref[2 + b] for b in range(2)], [0.0] * 2
    for block in range(ALL // BLOCK):
        for b in range(2):
            values = second_ref[block * BLOCK : (block + 1) * BLOCK, b * LANE : (b + 1) * LANE]
            half = values * term(terms, b, 0) + term(terms, b, 1)
            curved[b] += eight(half * jnp.tanh(half))
    sums = [plain[b] * term(terms, b, 0) + (CELLS // 2) * term(terms, b, 1) + curved[b] for b in range(2)]
    low = pooled_low(facts_ref[0], sums, stem_sum_ref[1])
    logits = dot_lanes(low, head_rows(head_ref))
    valid = class_lanes(2 * IMAGES)
    first_rows = lax.broadcasted_iota(jnp.int32, (2 * IMAGES, LANE), 0) < IMAGES
    prob = jnp.where(valid & first_rows, jnp.exp(log_softmax(logits, valid)), 0.0)
    prob_ref[...] = pltpu.roll(prob.astype(BF16).astype(F32), 16, 1)


def student_kernel(
    cell_count, facts_ref, second_ref, recv_ref, norm, head_ref, stem_sum_ref, image_sum_ref,
    msg_ref, bent_ref,
    terms,
):
    norm_rows(total_of(recv_ref), norm, terms, 0, 1, cell_count)
    plain = [image_sum_ref[b] for b in range(2)]
    curved, bent, bent_values = ([0.0] * 2 for _ in range(3))
    for block in range(ALL // BLOCK):
        for b in range(2):
            values = second_ref[block * BLOCK : (block + 1) * BLOCK, b * LANE : (b + 1) * LANE]
            half = values * term(terms, b, 0) + term(terms, b, 1)
            tanh = jnp.tanh(half)
            product = half * tanh
            slope = slope_rest(half, tanh, product)
            bent_ref[block * BLOCK : (block + 1) * BLOCK, b * LANE : (b + 1) * LANE] = slope
            curved[b] += eight(product)
            bent[b] += eight(slope)
            bent_values[b] += eight(slope * values)
    cells = CELLS // 2
    sums = [plain[b] * term(terms, b, 0) + cells * term(terms, b, 1) + curved[b] for b in range(2)]
    slopes = [0.5 * (cells + bent[b]) for b in range(2)]
    sums += slopes
    sums += [
        term(terms, b, 2) * (0.5 * (plain[b] + bent_values[b])) + term(terms, b, 3) * slopes[b] for b in range(2)
    ]
    low = pooled_low(facts_ref[0], sums, stem_sum_ref[0])
    logits = dot_lanes(low, head_rows(head_ref))
    rows = 2 * IMAGES
    info = jnp.where(class_lanes(rows), logits, facts_ref[1])
    row = lax.broadcasted_iota(jnp.int32, (rows, LANE), 0)
    for b in range(2):
        msg_ref[:, b * LANE : (b + 1) * LANE] = jnp.where(
            row < IMAGES, both_halves(sums[2 + b]), both_halves(sums[4 + b])
        )
    msg_ref[:, 2 * LANE :] = jnp.where(row < IMAGES, info, low.astype(F32))


def assemble_kernel(facts_ref, prob_ref, out_ref):
    out_ref[0, :, 0 : 2 * LANE] = facts_ref[:, 0 : 2 * LANE]
    out_ref[0, :, 2 * LANE :] = facts_ref[:, 2 * LANE :] + prob_ref[...]


def loss_part(images, all_images, cell_count, recv_refs, head_ref, rows_ref, means, small_ref):
    view = lax.axis_index("view")
    received = jnp.concatenate([ref[...] for ref in recv_refs], axis=0)
    count = received.shape[0] * 2 * images
    received = received.reshape(count, 3 * LANE)
    raw = received[:, 2 * LANE :]
    row = lax.broadcasted_iota(jnp.int32, (count, 1), 0)
    part = row & (2 * images - 1)
    once = part < images
    facts = jnp.where(once, raw, pltpu.roll(raw, images, 0))
    group, inner = row // (2 * images), received.shape[0] // (2 * images * len(recv_refs))
    offset = (group % inner) * len(recv_refs) + group // inner
    image = ((offset ^ lax.axis_index("dp")) * images + (part & (images - 1))).astype(F32)
    alpha = facts[:, 32:33]
    label = facts[:, 33:34]
    labelled = facts[:, 34:35]
    order = facts[:, 35:36]
    eye = row == lax.broadcasted_iota(jnp.int32, (count, count), 1)
    image_lane = jnp.sum(jnp.where(eye, image, 0.0), axis=0, keepdims=True)
    order_lane = jnp.sum(jnp.where(eye, order, 0.0), axis=0, keepdims=True)
    first_lane = jnp.sum(jnp.where(eye & once, 1.0, 0.0), axis=0, keepdims=True)
    is_one = jnp.where(view == 0, 1.0, 0.0)
    ours = is_one * image + (1.0 - is_one) * order
    theirs = is_one * order_lane + (1.0 - is_one) * image_lane
    match = jnp.where((ours == theirs) & (first_lane > 0.5), 1.0, 0.0).astype(BF16)
    valid = class_lanes(count)
    other = pltpu.roll(facts, LANE - 16, 1)
    target = dot(match, jnp.where(valid, other, 0.0).astype(BF16))
    log_prob = jnp.where(valid, log_softmax(jnp.where(valid, facts, 0.0), valid), 0.0)
    probs = jnp.where(valid, jnp.exp(log_prob), 0.0)
    lane = lax.broadcasted_iota(jnp.int32, (count, LANE), 1)
    onehot = jnp.where(lane.astype(F32) == label, 1.0, 0.0)
    total = jnp.sum(jnp.where(once, labelled, 0.0), axis=0, keepdims=True)
    mask = labelled * is_one
    away = probs - target
    grad_prob = CONS_WEIGHT / all_images * away
    grad = mask * (probs - onehot) / total + probs * (
        grad_prob - jnp.sum(probs * grad_prob, axis=1, keepdims=True)
    )
    grad_low = grad.astype(BF16)
    dmix = dot(grad_low, head_rows(head_ref)) / CELLS
    weights = (dmix * alpha, dmix * (1.0 - alpha))
    for b in range(2):
        product = weights[b] * received[:, b * LANE : (b + 1) * LANE]
        plain = column_sum(jnp.where(once, product, 0.0))
        normal = column_sum(jnp.where(once, 0.0, product))
        means[2 * b : 2 * b + 1, :] = plain / cell_count
        means[2 * b + 1 : 2 * b + 2, :] = normal / cell_count
        rows_ref[b] = weights[b]
        small_ref[16 + 2 * b : 16 + 2 * b + 1, :] = plain
        small_ref[16 + 2 * b + 1 : 16 + 2 * b + 2, :] = normal
    rows_ref[2] = dmix
    cross = -jnp.sum(
        jnp.where(once, mask * jnp.sum(onehot * log_prob, axis=1, keepdims=True), 0.0), axis=0, keepdims=True
    )
    consistency = jnp.sum(
        jnp.where(once, jnp.sum(away * away, axis=1, keepdims=True), 0.0), axis=0, keepdims=True
    )
    lane_row = lax.broadcasted_iota(jnp.int32, (1, LANE), 1)
    small_ref[20:21, :] = jnp.where(
        lane_row == 0, cross, jnp.where(lane_row == 1, consistency, jnp.where(lane_row == 2, total, 0.0))
    )
    small_ref[21:24, :] = jnp.zeros((3, LANE), F32)
    pooled = jnp.where(once, 0.0, raw).astype(BF16)
    small_ref[0:16, :] = dot_rows(grad_low, pooled)[0:16, :]


def pack_grad(ref, blocks):
    side_by_side = jnp.concatenate(blocks + [jnp.zeros((CH, BLOCKS * LANE - WIDE), F32)], axis=1)
    for k in range(BLOCKS):
        ref[k * CH : (k + 1) * CH, :] = side_by_side[:, k * LANE : (k + 1) * LANE]


def keep_and_send(keep_ref, send_ref, blocks):
    view = lax.axis_index("view")
    for own, ref in ((0, keep_ref), (1, send_ref)):
        @pl.when(view == own)
        def _():
            pack_grad(ref, blocks[0])

        @pl.when(view != own)
        def _():
            pack_grad(ref, blocks[1])


def back_second_kernel(
    cell_count, all_images,
    second_ref, first_ref, bent_two, bent_one, recv1_ref, recv2_ref, recv3_ref, norm, head_ref, w_ref,
    du_ref, frames, msg_ref, small_ref, dmix_ref,
    terms1, terms2, rows_ref, means,
):
    rows = 2 * IMAGES
    norm_rows(total_of(recv1_ref), norm, terms1, 0, 0, cell_count)
    norm_rows(total_of(recv2_ref), norm, terms2, 0, 1, cell_count)
    loss_part(IMAGES, all_images, cell_count, recv3_ref, head_ref, rows_ref, means, small_ref)
    dmix_ref[...] = rows_ref[2, 0:rows, :]
    scales, linears, offsets = [], [], []
    for b in range(2):
        gain = term(terms2, b, 4)
        mean, slant = means[2 * b : 2 * b + 1, :], means[2 * b + 1 : 2 * b + 2, :]
        scales.append(0.5 * gain * rows_ref[b, 0:rows, :])
        linears.append(-gain * slant * term(terms2, b, 2))
        offsets.append(scales[b] - gain * (mean + slant * term(terms2, b, 3)))
    sums = [0.0] * 4
    carry = [blank_line()] * 2
    for b in range(2):
        clear_frame(frames.at[b])
    for step in range(STEPS):
        first_line, end = new_lines(step)
        for b in range(2):
            lanes = slice(b * LANE, (b + 1) * LANE)
            values = second_ref[first_line * LINE : end * LINE, lanes]
            bent = bent_two[first_line * LINE : end * LINE, lanes]
            shape = (values.shape[0] // 8, 8, LANE)
            dy = (bent.reshape(shape) * scales[b][None] + offsets[b][None]).reshape(values.shape) + values * linears[b]
            frame_line(frames.at[b], first_line, dy)
            dh, carry[b] = fold_lines(dot(taps(frames.at[b], step, (0, 1)), w_ref[b]), carry[b])
            before = first_ref[chunk_rows(step), lanes]
            du = dh + dh * bent_one[chunk_rows(step), lanes]
            du_ref[chunk_rows(step), lanes] = du
            sums[2 * b] += eight(du)
            sums[2 * b + 1] += eight(du * before)
    for b in range(2):
        plain, product = column_sum(sums[2 * b]), column_sum(sums[2 * b + 1])
        sums[2 * b] = plain
        sums[2 * b + 1] = term(terms1, b, 2) * product + term(terms1, b, 3) * plain
    spread_sums(msg_ref, sums)


def middle_lines(frame, first_line):
    return frame[first_line + 1 : first_line + 1 + DEEP, 1 : ACROSS + 1].reshape(CHUNK, frame.shape[-1])


def second_weight_kernel(other, frame_ref, dy_ref, grad_ref, gacc):
    view = lax.axis_index("view")
    branch = 1 - view if other else view
    for step in range(STEPS):
        pair = jnp.concatenate(
            [middle_lines(dy_ref.at[branch], step * DEEP), middle_lines(dy_ref.at[branch], step * DEEP + 1)], axis=1
        )
        product = dot_rows(pair, taps(frame_ref.at[branch], step, (0, 1)))
        gacc[...] = product if step == 0 else gacc[...] + product
    blocks = []
    for tap in range(TAPS):
        ky, kx = tap // 3, tap % 3
        row = LANE if ky == 0 else 0
        lane = (ky // 2) * 3 * LANE + kx * LANE
        blocks.append(gacc[row : row + CH, lane : lane + CH])
    pack_grad(grad_ref, blocks)


def back_weight_kernel(
    cell_count,
    du_ref, first_ref, low_ref, recv1_ref, recv5_ref, norm, small_ref,
    frame_ref, keep_ref, send_ref,
    terms1, gacc,
):
    norm_rows(total_of(recv1_ref), norm, terms1, 0, 0, cell_count)
    sums = total_of(recv5_ref)
    for ref in (keep_ref, send_ref):
        ref[GRAD_ROWS : GRAD_ROWS + 24, :] = small_ref[...]
        ref[GRAD_ROWS + 24 :, :] = sums
    means = sums / cell_count
    linears, offsets = [], []
    for b in range(2):
        mean, slant = means[2 * b : 2 * b + 1, :], means[2 * b + 1 : 2 * b + 2, :]
        linears.append(-term(terms1, b, 4) * slant * term(terms1, b, 2))
        offsets.append(-term(terms1, b, 4) * (mean + slant * term(terms1, b, 3)))
    for b in range(2):
        clear_frame(frame_ref.at[b])
    for step in range(STEPS):
        parts = []
        for b in range(2):
            lanes = slice(b * LANE, (b + 1) * LANE)
            parts.append(
                du_ref[chunk_rows(step), lanes] * term(terms1, b, 4)
                + (first_ref[chunk_rows(step), lanes] * linears[b] + offsets[b])
            )
        pair = jnp.concatenate(parts, axis=1)
        for b in range(2):
            frame_line(frame_ref.at[b], step * DEEP, parts[b])
        product = dot_rows(pair.astype(BF16), taps(low_ref, step, (-1, 0, 1)))
        gacc[...] = product if step == 0 else gacc[...] + product
    keep_and_send(
        keep_ref, send_ref,
        [[gacc[b * LANE : b * LANE + CH, tap * LANE : tap * LANE + CH] for tap in range(TAPS)] for b in range(2)],
    )


def back_stem_kernel(frame_ref, moved_ref, dmix_ref, w_ref, stem_ref):
    carry = blank_line()
    total = 0.0
    products = []
    for step in range(STEPS):
        if step % 2 == 0:
            products = [[dot(taps(frame_ref.at[b], step + k, (0, 1)), w_ref[b]) for k in range(2)] for b in range(2)]
        both = products[0][step % 2] + products[1][step % 2]
        dstem, carry = fold_lines(both, carry)
        dstem = (dstem.reshape(CHUNK // 8, 8, LANE) + dmix_ref[...][None]).reshape(CHUNK, LANE)
        total += dot(image_taps(moved_ref, step * DEEP, DEEP), dstem.astype(BF16))
    rows = [total[stem_row(tap) : stem_row(tap) + 3, :] for tap in range(TAPS)]
    stem_ref[...] = jnp.concatenate(rows, axis=0)


def code(values):
    top = jnp.max(jnp.abs(values), axis=0, keepdims=True)
    power = jnp.clip(jnp.ceil(jnp.log2(jnp.maximum(top, 1e-30)) + 0.01), -100.0, 100.0)
    counted = jnp.round(values * (jnp.exp2(-power) * CODE_TOP))
    return counted, power


def unit(power):
    return jnp.exp2(power) * (1.0 / CODE_TOP)


def coded_rows(values, rows):
    counted, power = code(values)
    parts = [counted, power]
    if rows - values.shape[0] - 1:
        parts.append(jnp.zeros((rows - values.shape[0] - 1, LANE), F32))
    return jnp.concatenate(parts, axis=0).astype(jnp.int32).astype(jnp.int16)


def decoded(values, count):
    whole_part = values.astype(jnp.int32).astype(F32)
    return whole_part[:count] * unit(whole_part[count : count + 1])


def encode_kernel(keep2, recv2, keep1, recv1, *refs):
    outs, total = refs[:-1], refs[-1]
    for k, (keep, recv) in enumerate(((keep1, recv1), (keep2, recv2))):
        total[k] = keep[0:GRAD_ROWS, :] + recv[0:GRAD_ROWS, :]
    mine = lax.axis_index("dp") & (QUARTERS - 1)
    for offset, out in enumerate(outs):
        place = pl.multiple_of((mine ^ offset) * SHARE, 8)
        for k in range(2):
            out[k * PIECE : (k + 1) * PIECE, :] = coded_rows(total[k, pl.ds(place, SHARE), :], PIECE)


def summed(refs, first, count, rows):
    total = decoded(refs[0][first : first + rows, :], count)
    for ref in refs[1:]:
        total += decoded(ref[first : first + rows, :], count)
    return total


def combine_kernel(recv_refs, stem_ref, out_ref):
    for k in range(2):
        out_ref[k * PIECE : (k + 1) * PIECE, :] = coded_rows(summed(recv_refs, k * PIECE, SHARE, PIECE), PIECE)
    out_ref[2 * PIECE :, :] = coded_rows(stem_ref[...], SIDE)


def recode_kernel(recv_refs, out_ref):
    for k in range(2):
        out_ref[k * PIECE : (k + 1) * PIECE, :] = coded_rows(summed(recv_refs, k * PIECE, SHARE, PIECE), PIECE)
    out_ref[2 * PIECE :, :] = coded_rows(summed(recv_refs, 2 * PIECE, 27, SIDE), SIDE)


def stack_kernel(inner, parts, out_ref):
    count = parts[0].shape[0]
    for k, part in enumerate(parts):
        if inner:
            for entry in range(count):
                out_ref[entry * len(parts) + k] = part[entry]
        else:
            out_ref[k * count : (k + 1) * count] = part[...]


def adam_terms(gradient, factor, weight, first, second, teacher):
    clipped = gradient * factor
    first_new = BETA_FIRST * first + (1.0 - BETA_FIRST) * clipped
    second_new = BETA_SECOND * second + (1.0 - BETA_SECOND) * (clipped * clipped)
    second_hat = second_new * (1.0 / (1.0 - BETA_SECOND**STEP))
    weight_new = weight * (1.0 - LEARN_RATE * WEIGHT_DECAY) - (
        first_new * (LEARN_RATE / (1.0 - BETA_FIRST**STEP)) / (jnp.sqrt(second_hat) + ADAM_EPS)
    )
    return weight_new, first_new, second_new, TEACHER_KEEP * teacher + (1.0 - TEACHER_KEEP) * weight_new


def update_kernel(
    own_codes, other_codes, own_facts, other_facts,
    cw, cf, cs, ct, sw, sf, ss, st, hw, hf, hs, ht, nw, nf, ns, nt,
    cw_o, cf_o, cs_o, ct_o, cb_o, sw_o, sf_o, ss_o, st_o, sb_o, hw_o, hf_o, hs_o, ht_o, hb_o,
    nw_o, nf_o, ns_o, nt_o, norm_o, cross_o, count_o, consistency_o,
    factor_ref, own_ref, other_ref,
):
    conv = pl.program_id(0)
    view = lax.axis_index("view")

    @pl.when(conv == 0)
    def _():
        facts = own_facts[GRAD_ROWS:, :] + other_facts[GRAD_ROWS:, :]
        small, sums = facts[:24], facts[24:]
        mine = lax.axis_index("dp") & (QUARTERS - 1)
        stem = jnp.zeros((27, LANE), F32)
        for codes, ref in ((own_codes, own_ref), (other_codes, other_ref)):
            for offset, source in enumerate(codes):
                place = pl.multiple_of((mine ^ offset) * SHARE, 8)
                for k in range(2):
                    ref[k, pl.ds(place, SHARE), :] = decoded(source[k * PIECE : (k + 1) * PIECE, :], SHARE)
            stem += summed(codes, 2 * PIECE, 27, SIDE)
        stem = stem[:, :CH]
        head = small[:CLASSES, :CH]
        gains = jnp.concatenate([sums[1:2], small[17:18], sums[3:4], small[19:20]], axis=0)[:, :CH]
        shifts = jnp.concatenate([sums[0:1], small[16:17], sums[2:3], small[18:19]], axis=0)[:, :CH]
        total = jnp.zeros((1, 1), F32)
        for part in (stem, head, gains, shifts):
            total += jnp.sum(jnp.sum(part * part, axis=1, keepdims=True), axis=0, keepdims=True)
        for ref in (own_ref, other_ref):
            for k in range(2):
                values = ref[k, 0:GRAD_ROWS, :]
                column = jnp.sum(values * values, axis=0, keepdims=True)
                total += jnp.sum(column, axis=1, keepdims=True)
        norm = jnp.sqrt(total)
        factor = CLIP_LIMIT / jnp.maximum(norm, CLIP_LIMIT)
        factor_ref[...] = jnp.broadcast_to(factor, factor_ref.shape)
        norm_o[...] = norm
        cross_o[...] = small[20:21, 0:1]
        consistency_o[...] = small[20:21, 1:2]
        count_o[...] = own_facts[GRAD_ROWS + 20 : GRAD_ROWS + 21, 2:3]
        sw_o[...], sf_o[...], ss_o[...], st_o[...] = adam_terms(stem, factor, sw[...], sf[...], ss[...], st[...])
        sb_o[...] = sw_o[...].astype(BF16)
        hw_o[...], hf_o[...], hs_o[...], ht_o[...] = adam_terms(head, factor, hw[...], hf[...], hs[...], ht[...])
        hb_o[...] = hw_o[...].astype(BF16)
        for k, part in enumerate((gains, shifts)):
            nw_o[k], nf_o[k], ns_o[k], nt_o[k] = adam_terms(part, factor, nw[k], nf[k], ns[k], nt[k])

    def update(ref, second):
        factor = factor_ref[0:1, 0:1]
        for k in range(BLOCKS):
            lanes = slice(k * LANE, min((k + 1) * LANE, WIDE))
            gradient = ref[second, k * CH : (k + 1) * CH, 0 : lanes.stop - lanes.start]
            weight, first, second_moment, teacher = adam_terms(
                gradient, factor, cw[conv, :, lanes], cf[conv, :, lanes], cs[conv, :, lanes], ct[conv, :, lanes]
            )
            cw_o[:, lanes] = weight
            cf_o[:, lanes] = first
            cs_o[:, lanes] = second_moment
            ct_o[:, lanes] = teacher
            cb_o[:, lanes] = weight.astype(BF16)

    mine = conv // 2 == view

    @pl.when(mine)
    def _():
        update(own_ref, conv & 1)

    @pl.when(jnp.logical_not(mine))
    def _():
        update(other_ref, conv & 1)


def whole(shape):
    return pl.BlockSpec(shape, lambda i: (0,) * len(shape))


def scalars():
    return pl.BlockSpec(memory_space=pltpu.SMEM)


def conv_part(k):
    return pl.BlockSpec((None, CH, WIDE), lambda i: (k, 0, 0))


def held():
    return pl.BlockSpec(memory_space=pltpu.VMEM)


def hold(values):
    return pltpu.with_memory_space_constraint(values, pltpu.VMEM)


def struct(shape, kind=F32):
    return jax.ShapeDtypeStruct(shape, kind)


def to_partner(values, difference):
    return lax.ppermute(values, "dp", [(i, i ^ difference) for i in range(lax.axis_size("dp"))])


def to_other_core(values, difference):
    size = lax.axis_size("dp")
    return lax.ppermute(values, ("view", "dp"), [(i, i ^ (difference + size)) for i in range(2 * size)])


def far_last(ways):
    return (1, 3, 2) if ways == 4 else range(1, ways)


def from_partners(values, shift, ways, crossing=True):
    send = to_other_core if crossing else to_partner
    parts = [to_other_core(values, 0) if crossing else values] + [None] * (ways - 1)
    for offset in far_last(ways):
        parts[offset] = send(values, offset << shift)
    return parts


def stages():
    size = lax.axis_size("dp")
    groups = []
    shift = 0
    while (1 << shift) < size:
        ways = min(4, size >> shift)
        groups.append((shift, ways))
        shift += 2
    assert len(groups) % 2 == 0
    return groups


def sum_parts(values, beside=None):
    groups = stages()
    for shift, ways in groups[:-1]:
        parts = from_partners(values, shift, ways)
        if beside is not None:
            parts, beside = lax.optimization_barrier((parts, beside))
        values = sum(parts)
    return tuple(from_partners(values, *groups[-1])), beside


def stack(parts, inner):
    shape = (len(parts) * parts[0].shape[0],) + parts[0].shape[1:]
    return pl.pallas_call(
        functools.partial(stack_kernel, inner), out_shape=struct(shape, parts[0].dtype), compiler_params=PARAMS, name="stack"
    )(tuple(parts))


def gather_parts(values, groups):
    inner = groups[0][0] > 0
    for shift, ways in groups[:-1]:
        values = stack(from_partners(values, shift, ways), inner)
    return tuple(from_partners(values, *groups[-1]))


def swap_view(values):
    return lax.ppermute(values, "view", [(0, 1), (1, 0)])


def forward_weights(conv):
    shape = (2, 6 * LANE, 2 * LANE)
    return pl.pallas_call(
        forward_weight_kernel,
        grid=(2,),
        in_specs=[pl.BlockSpec((None, CH, WIDE), lambda i: (2 * i + 1, 0, 0))],
        out_specs=pl.BlockSpec((None,) + shape[1:], lambda i: (i, 0, 0)),
        out_shape=struct(shape, BF16),
        compiler_params=PARAMS,
        cost_estimate=pl.CostEstimate(flops=2_000_000_000, bytes_accessed=4_000_000, transcendentals=0),
        name="forward_weight",
    )(conv)


def backward_weights(conv):
    return pl.pallas_call(
        backward_weight_kernel,
        grid=(1,),
        in_specs=[conv_part(k) for k in range(4)],
        out_specs=[whole((2, 6 * LANE, 2 * LANE))] * 2,
        out_shape=[struct((2, 6 * LANE, 2 * LANE), BF16)] * 2,
        compiler_params=PARAMS,
        cost_estimate=pl.CostEstimate(flops=4_000_000_000, bytes_accessed=8_000_000, transcendentals=0),
        name="backward_weight",
    )(conv, conv, conv, conv)


def shards(
    augmented, shake_ratio, labels, labelled, view_order,
    stem_weight, conv_weight, head_weight, norm_param,
    teacher_stem, teacher_conv, teacher_head, teacher_norm,
    first_stem, first_conv, first_head, first_norm,
    second_stem, second_conv, second_head, second_norm,
):
    dp = lax.axis_size("dp")
    all_images = IMAGES * dp
    cell_count = float(all_images * CELLS)
    rows = dp * 2 * IMAGES
    conv, conv_t, conv_f, conv_s = (
        jnp.transpose(v, (0, 2, 1)) for v in (conv_weight, teacher_conv, first_conv, second_conv)
    )
    head, head_t, head_f, head_s = (v.T for v in (head_weight, teacher_head, first_head, second_head))
    pixels = jnp.transpose(augmented[0], (0, 3, 1, 2))
    msg = struct((8, LANE))
    groups = stages()
    last_ways = groups[-1][1]
    recv_spec = (held(),) * last_ways
    norm_spec = whole((2, 4, CH))
    head_spec = whole((CLASSES, CH))
    moved_shape = (3, (SIDE + 4) * 8, LANE)
    frame_one, frame_two = FRAME + (LANE,), (2,) + FRAME + (LANE,)
    values_shape, grad_shape = (ALL, 2 * LANE), struct((GRAD_ROWS, LANE))
    terms_scratch = pltpu.VMEM((16, LANE), F32)

    first_s, first_t, low, moved, stem_sums, message = pl.pallas_call(
        first_kernel,
        in_specs=[pl.BlockSpec(memory_space=pltpu.HBM)] * 5,
        out_specs=[held()] * 6,
        out_shape=[
            pltpu.VMEM(values_shape, F32), pltpu.VMEM(values_shape, F32), pltpu.VMEM(frame_one, BF16),
            pltpu.VMEM(moved_shape, F32), struct((2, 8, LANE)), msg,
        ],
        scratch_shapes=[
            pltpu.VMEM(moved_shape[1:], F32), pltpu.VMEM((STEM_ROWS, 2 * LANE), F32),
            pltpu.VMEM((STEM_ROWS, 2 * LANE), BF16), pltpu.VMEM((2, 9 * LANE, 2 * LANE), BF16),
            pltpu.VMEM(frame_one, BF16), pltpu.VMEM((IMAGES, 3, SIDE, SIDE), BF16), pltpu.VMEM((27, CH), F32),
            pltpu.VMEM((27, CH), F32), pltpu.VMEM((4, CH, WIDE), F32), pltpu.SemaphoreType.DMA((7,)),
        ],
        compiler_params=PARAMS,
        name="first_conv",
    )(*(pltpu.with_memory_space_constraint(v, pltpu.HBM) for v in (pixels, stem_weight, teacher_stem, conv, conv_t)))
    first_s, first_t, low, moved = (hold(v) for v in (first_s, first_t, low, moved))
    recv1, weight_s = sum_parts(message, forward_weights(conv))
    known = pl.pallas_call(
        facts_kernel,
        in_specs=[scalars()] * 4,
        out_specs=held(),
        out_shape=struct((2, 8, LANE)),
        compiler_params=PARAMS,
        name="facts",
    )(shake_ratio, labels, labelled, view_order)
    recv1, weight_t, known = lax.optimization_barrier((recv1, forward_weights(conv_t), known))

    second_s, second_t, hidden, bent_one, image_sums, message = pl.pallas_call(
        functools.partial(second_kernel, cell_count),
        in_specs=[held()] * 2 + [recv_spec] + [held()] * 4,
        out_specs=[held()] * 6,
        out_shape=[pltpu.VMEM(values_shape, F32)] * 2
        + [pltpu.VMEM(frame_two, BF16), pltpu.VMEM(values_shape, F32), struct((4, 8, LANE)), msg],
        scratch_shapes=[pltpu.VMEM(frame_two, BF16), terms_scratch, terms_scratch],
        compiler_params=PARAMS,
        name="second_conv",
    )(first_s, first_t, recv1, norm_param, teacher_norm, weight_s, weight_t)
    second_s, second_t, hidden, bent_one = (hold(v) for v in (second_s, second_t, hidden, bent_one))
    recv2, (back_weight_two, back_weight_one) = sum_parts(message, backward_weights(conv))

    prob = pl.pallas_call(
        functools.partial(teacher_kernel, cell_count),
        in_specs=[held()] * 2 + [recv_spec] + [held()] * 4,
        out_specs=held(),
        out_shape=struct((8, LANE)),
        scratch_shapes=[terms_scratch],
        compiler_params=PARAMS,
        name="teacher_logits",
    )(known, second_t, recv2, teacher_norm, head_t, stem_sums, image_sums)
    other = swap_view(prob)
    facts, bent_two = pl.pallas_call(
        functools.partial(student_kernel, cell_count),
        in_specs=[held()] * 2 + [recv_spec] + [held()] * 4,
        out_specs=[held()] * 2,
        out_shape=[struct((8, 3 * LANE)), pltpu.VMEM(values_shape, F32)],
        scratch_shapes=[terms_scratch],
        compiler_params=PARAMS,
        cost_estimate=pl.CostEstimate(flops=4_000_000_000, bytes_accessed=8_000_000, transcendentals=0),
        name="student_logits",
    )(known, second_s, recv2, norm_param, head, stem_sums, image_sums)
    bent_two = hold(bent_two)
    facts, other = lax.optimization_barrier((facts, other))
    facts = pl.pallas_call(
        assemble_kernel, out_shape=struct((1, 8, 3 * LANE)), compiler_params=PARAMS, name="assemble"
    )(facts, other)
    recv3 = gather_parts(facts, groups[::-1])

    du, dy, message, small, dmix = pl.pallas_call(
        functools.partial(back_second_kernel, cell_count, float(all_images)),
        in_specs=[held()] * 4 + [recv_spec] * 2 + [(held(),) * groups[0][1]] + [held()] * 3,
        out_specs=[held()] * 5,
        out_shape=[
            pltpu.VMEM(values_shape, F32), pltpu.VMEM(frame_two, BF16), msg, struct((24, LANE)), struct((8, LANE)),
        ],
        scratch_shapes=[
            terms_scratch, terms_scratch, pltpu.VMEM((3, rows, LANE), F32), pltpu.VMEM((8, LANE), F32),
        ],
        compiler_params=PARAMS,
        name="back_second",
    )(second_s, first_s, bent_two, bent_one, recv1, recv2, recv3, norm_param, head, back_weight_two)
    du, dy = hold(du), hold(dy)

    def second_weight(other):
        return pl.pallas_call(
            functools.partial(second_weight_kernel, other),
            in_specs=[held()] * 2,
            out_specs=held(),
            out_shape=grad_shape,
            scratch_shapes=[pltpu.VMEM((2 * LANE, 6 * LANE), F32)],
            compiler_params=PARAMS,
            cost_estimate=pl.CostEstimate(flops=4_000_000_000, bytes_accessed=8_000_000, transcendentals=0),
            name="second_weight",
        )(hidden, dy)

    send2, keep2 = second_weight(True), second_weight(False)
    recv5, send2 = sum_parts(message, send2)
    recv_grad2 = swap_view(send2)
    recv5, keep2, recv_grad2 = lax.optimization_barrier((recv5, keep2, recv_grad2))

    frame, keep1, send1 = pl.pallas_call(
        functools.partial(back_weight_kernel, cell_count),
        in_specs=[held()] * 3 + [recv_spec] * 2 + [held()] * 2,
        out_specs=[held()] * 3,
        out_shape=[pltpu.VMEM(frame_two, BF16)] + [struct((GRAD_ROWS + 32, LANE))] * 2,
        scratch_shapes=[terms_scratch, pltpu.VMEM((2 * LANE, 9 * LANE), F32)],
        compiler_params=PARAMS,
        cost_estimate=pl.CostEstimate(flops=8_000_000_000, bytes_accessed=16_000_000, transcendentals=0),
        name="back_weight",
    )(du, first_s, low, recv1, recv5, norm_param, small)
    frame = hold(frame)
    recv_grad1 = swap_view(send1)
    coded = pl.pallas_call(
        encode_kernel,
        out_shape=[struct((2 * PIECE, LANE), jnp.int16)] * QUARTERS,
        scratch_shapes=[pltpu.VMEM((2, GRAD_ROWS, LANE), F32)],
        compiler_params=PARAMS,
        name="encode",
    )(keep2, recv_grad2, keep1, recv_grad1)
    scattered = [coded[0]] + [None] * (QUARTERS - 1)
    for offset in far_last(QUARTERS):
        scattered[offset] = to_partner(coded[offset], offset)
    scattered = tuple(scattered)

    stem_grad = pl.pallas_call(
        back_stem_kernel,
        in_specs=[held()] * 4,
        out_specs=held(),
        out_shape=struct((27, LANE)),
        compiler_params=PARAMS,
        cost_estimate=pl.CostEstimate(flops=8_000_000_000, bytes_accessed=16_000_000, transcendentals=0),
        name="back_stem",
    )(frame, moved, dmix, back_weight_one)

    stem_grad, scattered = lax.optimization_barrier((stem_grad, scattered))
    code_shape = struct((CODE_ROWS, LANE), jnp.int16)
    codes = pl.pallas_call(combine_kernel, out_shape=code_shape, compiler_params=PARAMS, name="combine")(
        scattered, stem_grad
    )
    for group in groups[1:]:
        codes = pl.pallas_call(recode_kernel, out_shape=code_shape, compiler_params=PARAMS, name="recode")(
            tuple(from_partners(codes, *group, crossing=False))
        )
    own = tuple(from_partners(codes, *groups[0], crossing=False))
    other_grads = tuple(swap_view(part) for part in own)

    conv_block = pl.BlockSpec((None, CH, WIDE), lambda i: (i, 0, 0))
    stem_block, norm_block = whole((27, CH)), norm_spec
    code_spec = (held(),) * QUARTERS
    grads_scratch = pltpu.VMEM((2, GRAD_ROWS, LANE), F32)
    outs = pl.pallas_call(
        update_kernel,
        grid=(4,),
        in_specs=[code_spec] * 2 + [held()] * 18,
        out_specs=[conv_block] * 5 + [stem_block] * 5 + [head_spec] * 5 + [norm_block] * 4 + [whole((1, 1))] * 4,
        out_shape=[struct((4, CH, WIDE))] * 4 + [struct((4, CH, WIDE), BF16)]
        + [struct((27, CH))] * 4 + [struct((27, CH), BF16)]
        + [struct((CLASSES, CH))] * 4 + [struct((CLASSES, CH), BF16)]
        + [struct((2, 4, CH))] * 4 + [struct((1, 1))] * 4,
        scratch_shapes=[pltpu.VMEM((8, LANE), F32), grads_scratch, grads_scratch],
        compiler_params=PARAMS,
        name="update",
    )(
        own, other_grads, keep1, recv_grad1,
        conv, conv_f, conv_s, conv_t, stem_weight, first_stem, second_stem, teacher_stem,
        head, head_f, head_s, head_t, norm_param, first_norm, second_norm, teacher_norm,
    )
    convs = [jnp.transpose(v, (0, 2, 1)) for v in outs[:5]]
    stems = outs[5:10]
    heads = [v.T for v in outs[10:15]]
    norms = outs[15:19]
    return (
        *(v.reshape(()) for v in outs[19:23]),
        *stems[:4], *convs[:4], *heads[:4], *norms, stems[4], convs[4], heads[4],
    )


def solution(mesh):
    in_specs = (
        (P("view", "dp", None, None, None), P("view", "dp"), P("dp"), P("dp")) + (P(),) * 17
    )
    return jax.shard_map(shards, mesh=mesh, in_specs=in_specs, out_specs=(P(),) * 23, check_vma=False)
```

```python
import functools

import jax
import jax.numpy as jnp
from jax import lax
from jax.experimental import pallas as pl
from jax.experimental.pallas import tpu as pltpu
from jax.sharding import PartitionSpec as P

CLASSES = 10
STEP = 5
EPS_NORM = 1e-05
LEARN_RATE = 0.03
BETA_FIRST = 0.5
BETA_SECOND = 0.5
WEIGHT_DECAY = 0.0001
ADAM_EPS = 1e-08
CLIP_LIMIT = 0.02
TEACHER_KEEP = 0.9
CONS_WEIGHT = 10.0

F32 = jnp.float32
BF16 = jnp.bfloat16
LANE = 128
CH = 96
SIDE = 32
CELLS = SIDE * SIDE
IMAGES = 4
QUARTERS = 4
ACROSS = SIDE // QUARTERS
TILE = IMAGES * QUARTERS
LINE = ACROSS * TILE
STEPS = 4
DEEP = SIDE // STEPS
CHUNK = DEEP * LINE
ALL = SIDE * LINE
BLOCK = 64
TAPS = 9
WIDE = TAPS * CH
BLOCKS = -(-WIDE // LANE)
GRAD_ROWS = BLOCKS * CH
SHARE = GRAD_ROWS // QUARTERS
PIECE = -(-(SHARE + 1) // 16) * 16
CODE_ROWS = 2 * PIECE + SIDE
STEM_ROWS = 80
CODE_TOP = 32000.0
FRAME = (SIDE + 2, ACROSS + 2, TILE)
PARAMS = pltpu.CompilerParams(vmem_limit_bytes=14 * 1024 * 1024)


def dot(a, b):
    return jnp.dot(a, b, preferred_element_type=F32)


def dot_rows(a, b):
    return lax.dot_general(a, b, (((0,), (0,)), ((), ())), preferred_element_type=F32)


def dot_lanes(a, b):
    return lax.dot_general(a, b, (((1,), (1,)), ((), ())), preferred_element_type=F32)


def frame_line(frame, first_line, values):
    lines = values.shape[0] // LINE
    width = values.shape[1]
    tiles = values.reshape(lines, ACROSS, TILE, width)
    row = lax.broadcasted_iota(jnp.int32, (1, TILE, 1), 1)
    before = jnp.where(row >= IMAGES, pltpu.roll(tiles[:, ACROSS - 1], IMAGES, 1), 0.0)
    after = jnp.where(row < TILE - IMAGES, pltpu.roll(tiles[:, 0], TILE - IMAGES, 1), 0.0)
    place = slice(first_line + 1, first_line + 1 + lines)
    frame[place, 1 : ACROSS + 1] = tiles.astype(BF16)
    frame[place, 0] = before.astype(BF16)
    frame[place, ACROSS + 1] = after.astype(BF16)


def clear_frame(frame):
    blank = jnp.zeros(frame.shape[1:], BF16)
    frame[0] = blank
    frame[SIDE + 1] = blank


def taps(frame, step, rows):
    parts = []
    for dy in rows:
        for kx in range(3):
            place = step * DEEP + 1 + dy
            lines = frame[place : place + DEEP, kx : kx + ACROSS]
            parts.append(lines.reshape(CHUNK, lines.shape[-1]))
    return jnp.concatenate(parts, axis=1)


def fold_lines(both, carry):
    upper = jnp.concatenate([carry, both[: CHUNK - LINE, LANE:]], axis=0)
    return both[:, :LANE] + upper, both[CHUNK - LINE :, LANE:]


def blank_line():
    return jnp.zeros((LINE, LANE), F32)


def new_lines(step):
    first = 0 if step == 0 else step * DEEP + 1
    return first, min((step + 1) * DEEP + 1, SIDE)


def chunk_rows(step):
    return slice(step * CHUNK, (step + 1) * CHUNK)


def eight(values):
    parts = values.reshape(values.shape[0] // 8, 8, values.shape[1])
    while parts.shape[0] > 1:
        middle = parts.shape[0] // 2
        rest = parts[2 * middle :]
        parts = parts[:middle] + parts[middle : 2 * middle]
        if rest.shape[0]:
            parts = jnp.concatenate([parts[:-1], parts[-1:] + rest], axis=0) if middle > 1 else parts + rest
    return parts[0]


def both_halves(sums):
    return sums + pltpu.roll(sums, IMAGES, 0)


def tap_block(raw, tap):
    return raw[:, tap * CH : (tap + 1) * CH]


def image_lines(image_ref, plain, moved):
    plain[...] = jnp.zeros(plain.shape, F32)
    for channel in range(3):
        side_by_side = jnp.concatenate([image_ref[i, channel].astype(F32) for i in range(IMAGES)], axis=1)
        plain[pl.ds(8 + channel, SIDE, stride=8), :] = side_by_side
    source = lax.broadcasted_iota(jnp.int32, (LANE, LANE), 0)
    target = lax.broadcasted_iota(jnp.int32, (LANE, LANE), 1)
    same = source // SIDE == (target & (IMAGES - 1))
    across = ((target // IMAGES) & (QUARTERS - 1)) * ACROSS + target // TILE
    for kx in range(3):
        picks = jnp.where(same & ((source & (SIDE - 1)) == across + (kx - 1)), 1.0, 0.0).astype(BF16)
        moved[kx] = dot(plain[...].astype(BF16), picks)


def image_taps(moved, first_line, lines):
    columns = []
    for line in range(lines):
        place = (first_line + line) * 8
        parts = [moved[kx, place : place + 24, :] for kx in range(3)]
        columns.append(jnp.concatenate(parts + [jnp.zeros((8, LANE), F32)], axis=0))
    return jnp.concatenate(columns, axis=1).astype(BF16)


def stem_row(tap):
    return (tap % 3) * 24 + (tap // 3) * 8


def pad_lanes(row):
    return jnp.concatenate([row, jnp.zeros((row.shape[0], LANE - row.shape[1]), row.dtype)], axis=1)


def norm_terms(sums, squares, cell_count):
    average = sums / cell_count
    inverse = lax.rsqrt(squares / cell_count - average * average + EPS_NORM)
    return average, inverse


def column_sum(values):
    return jnp.sum(values, axis=0, keepdims=True)


def slope_rest(half, tanh, product):
    return (tanh + half) - product * tanh


def first_kernel(
    image_hbm, stem_s_hbm, stem_t_hbm, raw_s, raw_t,
    first_s, first_t, frame_s, moved_ref, pooled_ref, msg_ref,
    plain, wst32, wst, wf, frame_t, image_ref, stem_s, stem_t, raw, sems,
):
    coming = [
        pltpu.make_async_copy(source, target, sems.at[k])
        for k, (source, target) in enumerate((
            (image_hbm, image_ref), (stem_s_hbm, stem_s), (stem_t_hbm, stem_t),
            (raw_s.at[0], raw.at[0]), (raw_s.at[2], raw.at[1]), (raw_t.at[0], raw.at[2]), (raw_t.at[2], raw.at[3]),
        ))
    ]
    for copy in coming:
        copy.start()
    wf[...] = jnp.zeros(wf.shape, BF16)
    wst32[...] = jnp.zeros(wst32.shape, F32)
    clear_frame(frame_s)
    clear_frame(frame_t)
    for copy in coming[:3]:
        copy.wait()
    image_lines(image_ref, plain, moved_ref)
    for n, stem in enumerate((stem_s, stem_t)):
        for tap in range(TAPS):
            row = stem_row(tap)
            wst32[row : row + 3, n * LANE : n * LANE + CH] = stem[3 * tap : 3 * tap + 3, :]
    wst[...] = wst32[...].astype(BF16)
    for copy in coming[3:]:
        copy.wait()
    for n in range(2):
        for b in range(2):
            for tap in range(TAPS):
                wf[n, tap * LANE : tap * LANE + CH, b * LANE : b * LANE + CH] = jnp.transpose(
                    tap_block(raw.at[2 * n + b], tap)
                ).astype(BF16)
    pooled = [0.0, 0.0]
    sums = [0.0] * 8
    for step in range(STEPS):
        first_line, end = new_lines(step)
        stems = dot_rows(image_taps(moved_ref, first_line, end - first_line), wst[...])
        for n, (frame, out_ref) in enumerate(((frame_s, first_s), (frame_t, first_t))):
            stem = stems[:, n * LANE : (n + 1) * LANE]
            pooled[n] += eight(stem)
            frame_line(frame, first_line, stem)
            out = dot(taps(frame, step, (-1, 0, 1)), wf[n])
            out_ref[chunk_rows(step), :] = out
            for b in range(2):
                part = out[:, b * LANE : (b + 1) * LANE]
                sums[4 * n + 2 * b] += eight(part)
                sums[4 * n + 2 * b + 1] += eight(part * part)
    for n in range(2):
        pooled_ref[n] = both_halves(pooled[n])
    spread_sums(msg_ref, sums)


def total_of(refs):
    total = refs[0][...]
    for ref in refs[1:]:
        total = total + ref[...]
    return total


def spread_sums(msg_ref, sums):
    sums = [column_sum(part) for part in sums]
    if len(sums) < 8:
        sums.append(jnp.zeros((8 - len(sums), LANE), F32))
    msg_ref[...] = jnp.concatenate(sums, axis=0)


def forward_weight_kernel(raw_ref, w_ref):
    w_ref[...] = jnp.zeros(w_ref.shape, BF16)
    for ky in range(3):
        for kx in range(3):
            row = (ky // 2) * 3 * LANE + kx * LANE
            lane = LANE if ky == 0 else 0
            w_ref[row : row + CH, lane : lane + CH] = jnp.transpose(tap_block(raw_ref, ky * 3 + kx)).astype(BF16)


def backward_weight_kernel(cw0, cw1, cw2, cw3, two_ref, one_ref):
    two_ref[...] = jnp.zeros(two_ref.shape, BF16)
    one_ref[...] = jnp.zeros(one_ref.shape, BF16)
    for ky in range(3):
        for kx in range(3):
            tap = (2 - ky) * 3 + 2 - kx
            lane = LANE if ky == 0 else 0
            for b, (inner, outer) in enumerate(((cw0, cw1), (cw2, cw3))):
                row = (ky // 2) * 3 * LANE + kx * LANE
                two_ref[b, row : row + CH, lane : lane + CH] = (0.5 * tap_block(outer, tap)).astype(BF16)
                one_ref[b, row : row + CH, lane : lane + CH] = tap_block(inner, tap).astype(BF16)


def norm_rows(sums, norm, terms, first_row, norm_index, cell_count):
    for b in range(2):
        row = first_row + 2 * b
        average, inverse = norm_terms(sums[row : row + 1], sums[row + 1 : row + 2], cell_count)
        gain = pad_lanes(norm[0, 2 * b + norm_index : 2 * b + norm_index + 1, :])
        shift = pad_lanes(norm[1, 2 * b + norm_index : 2 * b + norm_index + 1, :])
        scale = inverse * gain
        terms[8 * b : 8 * b + 1, :] = 0.5 * scale
        terms[8 * b + 1 : 8 * b + 2, :] = 0.5 * (shift - average * scale)
        terms[8 * b + 2 : 8 * b + 3, :] = inverse
        terms[8 * b + 3 : 8 * b + 4, :] = -average * inverse
        terms[8 * b + 4 : 8 * b + 5, :] = scale


def term(terms, b, k):
    return terms[8 * b + k : 8 * b + k + 1, :]


def second_kernel(
    cell_count, first_s, first_t, recv_ref, norm_s, norm_t, ws_ref, wt_ref,
    second_s, second_t, frame_s, bent_ref, plain_ref, msg_ref,
    frame_t, terms_s, terms_t,
):
    received = total_of(recv_ref)
    norm_rows(received, norm_s, terms_s, 0, 0, cell_count)
    norm_rows(received, norm_t, terms_t, 4, 0, cell_count)
    nets = ((first_s, terms_s, frame_s, ws_ref, second_s), (first_t, terms_t, frame_t, wt_ref, second_t))
    sums = [0.0] * 8
    carry = [blank_line()] * 4
    for _, _, frames, _, _ in nets:
        for b in range(2):
            clear_frame(frames.at[b])
    for step in range(STEPS):
        first_line, end = new_lines(step)
        for n, (source, terms, frames, w, target) in enumerate(nets):
            for b in range(2):
                k = 2 * n + b
                lanes = slice(b * LANE, (b + 1) * LANE)
                half = source[first_line * LINE : end * LINE, lanes] * term(terms, b, 0) + term(terms, b, 1)
                tanh = jnp.tanh(half)
                product = half * tanh
                frame_line(frames.at[b], first_line, half + product)
                if n == 0:
                    bent_ref[first_line * LINE : end * LINE, lanes] = slope_rest(half, tanh, product)
                out, carry[k] = fold_lines(dot(taps(frames.at[b], step, (0, 1)), w[b]), carry[k])
                target[chunk_rows(step), lanes] = out
                sums[2 * k] += eight(out)
                sums[2 * k + 1] += eight(out * out)
    for k in range(4):
        plain_ref[k] = sums[2 * k]
    spread_sums(msg_ref, sums)


def head_rows(head_ref):
    padded = jnp.concatenate([head_ref[...], jnp.zeros((LANE - CLASSES, CH), F32)], axis=0)
    return pad_lanes(padded).astype(BF16)


def alpha_of(ratio_ref, image):
    return (ratio_ref[0, image].astype(F32) + 1.0) / 18.0


def alpha_rows(ratio_ref):
    row = lax.broadcasted_iota(jnp.int32, (2 * IMAGES, LANE), 0) & (IMAGES - 1)
    alpha = jnp.zeros((2 * IMAGES, LANE), F32)
    for k in range(IMAGES):
        alpha = jnp.where(row == k, alpha_of(ratio_ref, k), alpha)
    return alpha


def class_lanes(rows):
    return lax.broadcasted_iota(jnp.int32, (rows, LANE), 1) < CLASSES


def log_softmax(logits, valid):
    top = jnp.max(jnp.where(valid, logits, -3e38), axis=1, keepdims=True)
    moved = logits - top
    total = jnp.sum(jnp.where(valid, jnp.exp(moved), 0.0), axis=1, keepdims=True)
    return moved - jnp.log(total)


def facts_kernel(ratio_ref, labels_ref, labelled_ref, order_ref, facts_ref):
    dp_index = lax.axis_index("dp")
    facts_ref[0] = alpha_rows(ratio_ref)
    lane = lax.broadcasted_iota(jnp.int32, (2 * IMAGES, LANE), 1)
    row = lax.broadcasted_iota(jnp.int32, (2 * IMAGES, LANE), 0)
    info = jnp.zeros((2 * IMAGES, LANE), F32)
    for k in range(IMAGES):
        facts = (
            alpha_of(ratio_ref, k),
            labels_ref[k].astype(F32),
            labelled_ref[k].astype(F32),
            order_ref[dp_index * IMAGES + k].astype(F32),
        )
        for place, fact in enumerate(facts):
            info = jnp.where((row == k) & (lane == 32 + place), fact, info)
    facts_ref[1] = info


def pooled_low(alpha, sums, stem_sums):
    total = alpha * both_halves(sums[0]) + (1.0 - alpha) * both_halves(sums[1])
    return ((total + stem_sums) / CELLS).astype(BF16)


def teacher_kernel(
    cell_count, facts_ref, second_ref, recv_ref, norm, head_ref, stem_sum_ref, image_sum_ref,
    prob_ref,
    terms,
):
    norm_rows(total_of(recv_ref), norm, terms, 4, 1, cell_count)
    plain, curved = [image_sum_ref[2 + b] for b in range(2)], [0.0] * 2
    for block in range(ALL // BLOCK):
        for b in range(2):
            values = second_ref[block * BLOCK : (block + 1) * BLOCK, b * LANE : (b + 1) * LANE]
            half = values * term(terms, b, 0) + term(terms, b, 1)
            curved[b] += eight(half * jnp.tanh(half))
    sums = [plain[b] * term(terms, b, 0) + (CELLS // 2) * term(terms, b, 1) + curved[b] for b in range(2)]
    low = pooled_low(facts_ref[0], sums, stem_sum_ref[1])
    logits = dot_lanes(low, head_rows(head_ref))
    valid = class_lanes(2 * IMAGES)
    first_rows = lax.broadcasted_iota(jnp.int32, (2 * IMAGES, LANE), 0) < IMAGES
    prob = jnp.where(valid & first_rows, jnp.exp(log_softmax(logits, valid)), 0.0)
    prob_ref[...] = pltpu.roll(prob.astype(BF16).astype(F32), 16, 1)


def student_kernel(
    cell_count, facts_ref, second_ref, recv_ref, norm, head_ref, stem_sum_ref, image_sum_ref,
    msg_ref, bent_ref,
    terms,
):
    norm_rows(total_of(recv_ref), norm, terms, 0, 1, cell_count)
    plain = [image_sum_ref[b] for b in range(2)]
    curved, bent, bent_values = ([0.0] * 2 for _ in range(3))
    for block in range(ALL // BLOCK):
        for b in range(2):
            values = second_ref[block * BLOCK : (block + 1) * BLOCK, b * LANE : (b + 1) * LANE]
            half = values * term(terms, b, 0) + term(terms, b, 1)
            tanh = jnp.tanh(half)
            product = half * tanh
            slope = slope_rest(half, tanh, product)
            bent_ref[block * BLOCK : (block + 1) * BLOCK, b * LANE : (b + 1) * LANE] = slope
            curved[b] += eight(product)
            bent[b] += eight(slope)
            bent_values[b] += eight(slope * values)
    cells = CELLS // 2
    sums = [plain[b] * term(terms, b, 0) + cells * term(terms, b, 1) + curved[b] for b in range(2)]
    slopes = [0.5 * (cells + bent[b]) for b in range(2)]
    sums += slopes
    sums += [
        term(terms, b, 2) * (0.5 * (plain[b] + bent_values[b])) + term(terms, b, 3) * slopes[b] for b in range(2)
    ]
    low = pooled_low(facts_ref[0], sums, stem_sum_ref[0])
    logits = dot_lanes(low, head_rows(head_ref))
    rows = 2 * IMAGES
    info = jnp.where(class_lanes(rows), logits, facts_ref[1])
    row = lax.broadcasted_iota(jnp.int32, (rows, LANE), 0)
    for b in range(2):
        msg_ref[:, b * LANE : (b + 1) * LANE] = jnp.where(
            row < IMAGES, both_halves(sums[2 + b]), both_halves(sums[4 + b])
        )
    msg_ref[:, 2 * LANE :] = jnp.where(row < IMAGES, info, low.astype(F32))


def assemble_kernel(facts_ref, prob_ref, out_ref):
    out_ref[0, :, 0 : 2 * LANE] = facts_ref[:, 0 : 2 * LANE]
    out_ref[0, :, 2 * LANE :] = facts_ref[:, 2 * LANE :] + prob_ref[...]


def loss_part(images, all_images, cell_count, recv_refs, head_ref, rows_ref, means, small_ref):
    view = lax.axis_index("view")
    received = jnp.concatenate([ref[...] for ref in recv_refs], axis=0)
    count = received.shape[0] * 2 * images
    received = received.reshape(count, 3 * LANE)
    raw = received[:, 2 * LANE :]
    row = lax.broadcasted_iota(jnp.int32, (count, 1), 0)
    part = row & (2 * images - 1)
    once = part < images
    facts = jnp.where(once, raw, pltpu.roll(raw, images, 0))
    group, inner = row // (2 * images), received.shape[0] // (2 * images * len(recv_refs))
    offset = (group % inner) * len(recv_refs) + group // inner
    image = ((offset ^ lax.axis_index("dp")) * images + (part & (images - 1))).astype(F32)
    alpha = facts[:, 32:33]
    label = facts[:, 33:34]
    labelled = facts[:, 34:35]
    order = facts[:, 35:36]
    eye = row == lax.broadcasted_iota(jnp.int32, (count, count), 1)
    image_lane = jnp.sum(jnp.where(eye, image, 0.0), axis=0, keepdims=True)
    order_lane = jnp.sum(jnp.where(eye, order, 0.0), axis=0, keepdims=True)
    first_lane = jnp.sum(jnp.where(eye & once, 1.0, 0.0), axis=0, keepdims=True)
    is_one = jnp.where(view == 0, 1.0, 0.0)
    ours = is_one * image + (1.0 - is_one) * order
    theirs = is_one * order_lane + (1.0 - is_one) * image_lane
    match = jnp.where((ours == theirs) & (first_lane > 0.5), 1.0, 0.0).astype(BF16)
    valid = class_lanes(count)
    other = pltpu.roll(facts, LANE - 16, 1)
    target = dot(match, jnp.where(valid, other, 0.0).astype(BF16))
    log_prob = jnp.where(valid, log_softmax(jnp.where(valid, facts, 0.0), valid), 0.0)
    probs = jnp.where(valid, jnp.exp(log_prob), 0.0)
    lane = lax.broadcasted_iota(jnp.int32, (count, LANE), 1)
    onehot = jnp.where(lane.astype(F32) == label, 1.0, 0.0)
    total = jnp.sum(jnp.where(once, labelled, 0.0), axis=0, keepdims=True)
    mask = labelled * is_one
    away = probs - target
    grad_prob = CONS_WEIGHT / all_images * away
    grad = mask * (probs - onehot) / total + probs * (
        grad_prob - jnp.sum(probs * grad_prob, axis=1, keepdims=True)
    )
    grad_low = grad.astype(BF16)
    dmix = dot(grad_low, head_rows(head_ref)) / CELLS
    weights = (dmix * alpha, dmix * (1.0 - alpha))
    for b in range(2):
        product = weights[b] * received[:, b * LANE : (b + 1) * LANE]
        plain = column_sum(jnp.where(once, product, 0.0))
        normal = column_sum(jnp.where(once, 0.0, product))
        means[2 * b : 2 * b + 1, :] = plain / cell_count
        means[2 * b + 1 : 2 * b + 2, :] = normal / cell_count
        rows_ref[b] = weights[b]
        small_ref[16 + 2 * b : 16 + 2 * b + 1, :] = plain
        small_ref[16 + 2 * b + 1 : 16 + 2 * b + 2, :] = normal
    rows_ref[2] = dmix
    cross = -jnp.sum(
        jnp.where(once, mask * jnp.sum(onehot * log_prob, axis=1, keepdims=True), 0.0), axis=0, keepdims=True
    )
    consistency = jnp.sum(
        jnp.where(once, jnp.sum(away * away, axis=1, keepdims=True), 0.0), axis=0, keepdims=True
    )
    lane_row = lax.broadcasted_iota(jnp.int32, (1, LANE), 1)
    small_ref[20:21, :] = jnp.where(
        lane_row == 0, cross, jnp.where(lane_row == 1, consistency, jnp.where(lane_row == 2, total, 0.0))
    )
    small_ref[21:24, :] = jnp.zeros((3, LANE), F32)
    pooled = jnp.where(once, 0.0, raw).astype(BF16)
    small_ref[0:16, :] = dot_rows(grad_low, pooled)[0:16, :]


def pack_grad(ref, blocks):
    side_by_side = jnp.concatenate(blocks + [jnp.zeros((CH, BLOCKS * LANE - WIDE), F32)], axis=1)
    for k in range(BLOCKS):
        ref[k * CH : (k + 1) * CH, :] = side_by_side[:, k * LANE : (k + 1) * LANE]


def keep_and_send(keep_ref, send_ref, blocks):
    view = lax.axis_index("view")
    for own, ref in ((0, keep_ref), (1, send_ref)):
        @pl.when(view == own)
        def _():
            pack_grad(ref, blocks[0])

        @pl.when(view != own)
        def _():
            pack_grad(ref, blocks[1])


def back_second_kernel(
    cell_count, all_images,
    second_ref, first_ref, bent_two, bent_one, recv1_ref, recv2_ref, recv3_ref, norm, head_ref, w_ref,
    du_ref, frames, msg_ref, small_ref, dmix_ref,
    terms1, terms2, rows_ref, means,
):
    rows = 2 * IMAGES
    norm_rows(total_of(recv1_ref), norm, terms1, 0, 0, cell_count)
    norm_rows(total_of(recv2_ref), norm, terms2, 0, 1, cell_count)
    loss_part(IMAGES, all_images, cell_count, recv3_ref, head_ref, rows_ref, means, small_ref)
    dmix_ref[...] = rows_ref[2, 0:rows, :]
    scales, linears, offsets = [], [], []
    for b in range(2):
        gain = term(terms2, b, 4)
        mean, slant = means[2 * b : 2 * b + 1, :], means[2 * b + 1 : 2 * b + 2, :]
        scales.append(0.5 * gain * rows_ref[b, 0:rows, :])
        linears.append(-gain * slant * term(terms2, b, 2))
        offsets.append(scales[b] - gain * (mean + slant * term(terms2, b, 3)))
    sums = [0.0] * 4
    carry = [blank_line()] * 2
    for b in range(2):
        clear_frame(frames.at[b])
    for step in range(STEPS):
        first_line, end = new_lines(step)
        for b in range(2):
            lanes = slice(b * LANE, (b + 1) * LANE)
            values = second_ref[first_line * LINE : end * LINE, lanes]
            bent = bent_two[first_line * LINE : end * LINE, lanes]
            shape = (values.shape[0] // 8, 8, LANE)
            dy = (bent.reshape(shape) * scales[b][None] + offsets[b][None]).reshape(values.shape) + values * linears[b]
            frame_line(frames.at[b], first_line, dy)
            dh, carry[b] = fold_lines(dot(taps(frames.at[b], step, (0, 1)), w_ref[b]), carry[b])
            before = first_ref[chunk_rows(step), lanes]
            du = dh + dh * bent_one[chunk_rows(step), lanes]
            du_ref[chunk_rows(step), lanes] = du
            sums[2 * b] += eight(du)
            sums[2 * b + 1] += eight(du * before)
    for b in range(2):
        plain, product = column_sum(sums[2 * b]), column_sum(sums[2 * b + 1])
        sums[2 * b] = plain
        sums[2 * b + 1] = term(terms1, b, 2) * product + term(terms1, b, 3) * plain
    spread_sums(msg_ref, sums)


def middle_lines(frame, first_line):
    return frame[first_line + 1 : first_line + 1 + DEEP, 1 : ACROSS + 1].reshape(CHUNK, frame.shape[-1])


def second_weight_kernel(other, frame_ref, dy_ref, grad_ref, gacc):
    view = lax.axis_index("view")
    branch = 1 - view if other else view
    for step in range(STEPS):
        pair = jnp.concatenate(
            [middle_lines(dy_ref.at[branch], step * DEEP), middle_lines(dy_ref.at[branch], step * DEEP + 1)], axis=1
        )
        product = dot_rows(pair, taps(frame_ref.at[branch], step, (0, 1)))
        gacc[...] = product if step == 0 else gacc[...] + product
    blocks = []
    for tap in range(TAPS):
        ky, kx = tap // 3, tap % 3
        row = LANE if ky == 0 else 0
        lane = (ky // 2) * 3 * LANE + kx * LANE
        blocks.append(gacc[row : row + CH, lane : lane + CH])
    pack_grad(grad_ref, blocks)


def back_weight_kernel(
    cell_count,
    du_ref, first_ref, low_ref, recv1_ref, recv5_ref, norm, small_ref,
    frame_ref, keep_ref, send_ref,
    terms1, gacc,
):
    norm_rows(total_of(recv1_ref), norm, terms1, 0, 0, cell_count)
    sums = total_of(recv5_ref)
    for ref in (keep_ref, send_ref):
        ref[GRAD_ROWS : GRAD_ROWS + 24, :] = small_ref[...]
        ref[GRAD_ROWS + 24 :, :] = sums
    means = sums / cell_count
    linears, offsets = [], []
    for b in range(2):
        mean, slant = means[2 * b : 2 * b + 1, :], means[2 * b + 1 : 2 * b + 2, :]
        linears.append(-term(terms1, b, 4) * slant * term(terms1, b, 2))
        offsets.append(-term(terms1, b, 4) * (mean + slant * term(terms1, b, 3)))
    for b in range(2):
        clear_frame(frame_ref.at[b])
    for step in range(STEPS):
        parts = []
        for b in range(2):
            lanes = slice(b * LANE, (b + 1) * LANE)
            parts.append(
                du_ref[chunk_rows(step), lanes] * term(terms1, b, 4)
                + (first_ref[chunk_rows(step), lanes] * linears[b] + offsets[b])
            )
        pair = jnp.concatenate(parts, axis=1)
        for b in range(2):
            frame_line(frame_ref.at[b], step * DEEP, parts[b])
        product = dot_rows(pair.astype(BF16), taps(low_ref, step, (-1, 0, 1)))
        gacc[...] = product if step == 0 else gacc[...] + product
    keep_and_send(
        keep_ref, send_ref,
        [[gacc[b * LANE : b * LANE + CH, tap * LANE : tap * LANE + CH] for tap in range(TAPS)] for b in range(2)],
    )


def back_stem_steps(steps, frame_ref, moved_ref, dmix_ref, w_ref, carry, total):
    for step in steps:
        both = dot(taps(frame_ref.at[0], step, (0, 1)), w_ref[0]) + dot(taps(frame_ref.at[1], step, (0, 1)), w_ref[1])
        dstem, carry = fold_lines(both, carry)
        dstem = (dstem.reshape(CHUNK // 8, 8, LANE) + dmix_ref[...][None]).reshape(CHUNK, LANE)
        total += dot(image_taps(moved_ref, step * DEEP, DEEP), dstem.astype(BF16))
    return carry, total


def back_stem_kernel(step, frame_ref, moved_ref, dmix_ref, w_ref, *refs):
    carry, total = (blank_line(), 0.0) if step == 0 else (refs[0][...], refs[1][...])
    carry, total = back_stem_steps((step,), frame_ref, moved_ref, dmix_ref, w_ref, carry, total)
    if step < STEPS - 1:
        refs[-2][...] = carry
        refs[-1][...] = total
    else:
        rows = [total[stem_row(tap) : stem_row(tap) + 3, :] for tap in range(TAPS)]
        refs[-1][...] = jnp.concatenate(rows, axis=0)


def code(values):
    top = jnp.max(jnp.abs(values), axis=0, keepdims=True)
    power = jnp.clip(jnp.ceil(jnp.log2(jnp.maximum(top, 1e-30)) + 0.01), -100.0, 100.0)
    counted = jnp.round(values * (jnp.exp2(-power) * CODE_TOP))
    return counted, power


def unit(power):
    return jnp.exp2(power) * (1.0 / CODE_TOP)


def coded_rows(values, rows):
    counted, power = code(values)
    parts = [counted, power]
    if rows - values.shape[0] - 1:
        parts.append(jnp.zeros((rows - values.shape[0] - 1, LANE), F32))
    return jnp.concatenate(parts, axis=0).astype(jnp.int32).astype(jnp.int16)


def decoded(values, count):
    whole_part = values.astype(jnp.int32).astype(F32)
    return whole_part[:count] * unit(whole_part[count : count + 1])


def encode_kernel(keep2, recv2, keep1, recv1, *refs):
    outs, total = refs[:-1], refs[-1]
    for k, (keep, recv) in enumerate(((keep1, recv1), (keep2, recv2))):
        total[k] = keep[0:GRAD_ROWS, :] + recv[0:GRAD_ROWS, :]
    mine = lax.axis_index("dp") & (QUARTERS - 1)
    for offset, out in enumerate(outs):
        place = pl.multiple_of((mine ^ offset) * SHARE, 8)
        for k in range(2):
            out[k * PIECE : (k + 1) * PIECE, :] = coded_rows(total[k, pl.ds(place, SHARE), :], PIECE)


def summed(refs, first, count, rows):
    total = decoded(refs[0][first : first + rows, :], count)
    for ref in refs[1:]:
        total += decoded(ref[first : first + rows, :], count)
    return total


def combine_kernel(recv_refs, stem_ref, out_ref):
    for k in range(2):
        out_ref[k * PIECE : (k + 1) * PIECE, :] = coded_rows(summed(recv_refs, k * PIECE, SHARE, PIECE), PIECE)
    out_ref[2 * PIECE :, :] = coded_rows(stem_ref[...], SIDE)


def recode_kernel(recv_refs, out_ref):
    for k in range(2):
        out_ref[k * PIECE : (k + 1) * PIECE, :] = coded_rows(summed(recv_refs, k * PIECE, SHARE, PIECE), PIECE)
    out_ref[2 * PIECE :, :] = coded_rows(summed(recv_refs, 2 * PIECE, 27, SIDE), SIDE)


def stack_kernel(inner, parts, out_ref):
    count = parts[0].shape[0]
    for k, part in enumerate(parts):
        if inner:
            for entry in range(count):
                out_ref[entry * len(parts) + k] = part[entry]
        else:
            out_ref[k * count : (k + 1) * count] = part[...]


def adam_terms(gradient, factor, weight, first, second, teacher):
    clipped = gradient * factor
    first_new = BETA_FIRST * first + (1.0 - BETA_FIRST) * clipped
    second_new = BETA_SECOND * second + (1.0 - BETA_SECOND) * (clipped * clipped)
    second_hat = second_new * (1.0 / (1.0 - BETA_SECOND**STEP))
    weight_new = weight * (1.0 - LEARN_RATE * WEIGHT_DECAY) - (
        first_new * (LEARN_RATE / (1.0 - BETA_FIRST**STEP)) / (jnp.sqrt(second_hat) + ADAM_EPS)
    )
    return weight_new, first_new, second_new, TEACHER_KEEP * teacher + (1.0 - TEACHER_KEEP) * weight_new


def place_codes(codes, grads):
    mine = lax.axis_index("dp") & (QUARTERS - 1)
    for offset, source in enumerate(codes):
        place = pl.multiple_of((mine ^ offset) * SHARE, 8)
        for k in range(2):
            grads[k, pl.ds(place, SHARE), :] = decoded(source[k * PIECE : (k + 1) * PIECE, :], SHARE)


def square_sums(grads):
    return sum(eight(grads[k] * grads[k]) for k in range(2))


def decode_kernel(codes, grads_ref, stem_ref, squares_ref):
    place_codes(codes, grads_ref)
    stem_ref[...] = summed(codes, 2 * PIECE, 27, SIDE)
    squares_ref[...] = square_sums(grads_ref)


def update_kernel(
    own_ref, own_stem, own_squares, other_codes, own_facts, other_facts,
    cw, cf, cs, ct, sw, sf, ss, st, hw, hf, hs, ht, nw, nf, ns, nt,
    cw_o, cf_o, cs_o, ct_o, cb_o, sw_o, sf_o, ss_o, st_o, sb_o, hw_o, hf_o, hs_o, ht_o, hb_o,
    nw_o, nf_o, ns_o, nt_o, norm_o, cross_o, count_o, consistency_o,
    factor_ref, other_ref,
):
    conv = pl.program_id(0)
    view = lax.axis_index("view")

    @pl.when(conv == 0)
    def _():
        facts = own_facts[GRAD_ROWS:, :] + other_facts[GRAD_ROWS:, :]
        small, sums = facts[:24], facts[24:]
        place_codes(other_codes, other_ref)
        stem = own_stem[...] + summed(other_codes, 2 * PIECE, 27, SIDE)
        stem = stem[:, :CH]
        head = small[:CLASSES, :CH]
        gains = jnp.concatenate([sums[1:2], small[17:18], sums[3:4], small[19:20]], axis=0)[:, :CH]
        shifts = jnp.concatenate([sums[0:1], small[16:17], sums[2:3], small[18:19]], axis=0)[:, :CH]
        total = jnp.zeros((1, 1), F32)
        for part in (stem, head, gains, shifts):
            total += jnp.sum(jnp.sum(part * part, axis=1, keepdims=True), axis=0, keepdims=True)
        squares = own_squares[...] + square_sums(other_ref)
        total += jnp.sum(jnp.sum(squares, axis=0, keepdims=True), axis=1, keepdims=True)
        norm = jnp.sqrt(total)
        factor = CLIP_LIMIT / jnp.maximum(norm, CLIP_LIMIT)
        factor_ref[...] = jnp.broadcast_to(factor, factor_ref.shape)
        norm_o[...] = norm
        cross_o[...] = small[20:21, 0:1]
        consistency_o[...] = small[20:21, 1:2]
        count_o[...] = own_facts[GRAD_ROWS + 20 : GRAD_ROWS + 21, 2:3]
        sw_o[...], sf_o[...], ss_o[...], st_o[...] = adam_terms(stem, factor, sw[...], sf[...], ss[...], st[...])
        sb_o[...] = sw_o[...].astype(BF16)
        hw_o[...], hf_o[...], hs_o[...], ht_o[...] = adam_terms(head, factor, hw[...], hf[...], hs[...], ht[...])
        hb_o[...] = hw_o[...].astype(BF16)
        for k, part in enumerate((gains, shifts)):
            nw_o[k], nf_o[k], ns_o[k], nt_o[k] = adam_terms(part, factor, nw[k], nf[k], ns[k], nt[k])

    def update(ref, second):
        factor = factor_ref[0:1, 0:1]
        for k in range(BLOCKS):
            lanes = slice(k * LANE, min((k + 1) * LANE, WIDE))
            gradient = ref[second, k * CH : (k + 1) * CH, 0 : lanes.stop - lanes.start]
            weight, first, second_moment, teacher = adam_terms(
                gradient, factor, cw[conv, :, lanes], cf[conv, :, lanes], cs[conv, :, lanes], ct[conv, :, lanes]
            )
            cw_o[:, lanes] = weight
            cf_o[:, lanes] = first
            cs_o[:, lanes] = second_moment
            ct_o[:, lanes] = teacher
            cb_o[:, lanes] = weight.astype(BF16)

    mine = conv // 2 == view

    @pl.when(mine)
    def _():
        update(own_ref, conv & 1)

    @pl.when(jnp.logical_not(mine))
    def _():
        update(other_ref, conv & 1)


def whole(shape):
    return pl.BlockSpec(shape, lambda i: (0,) * len(shape))


def scalars():
    return pl.BlockSpec(memory_space=pltpu.SMEM)


def conv_part(k):
    return pl.BlockSpec((None, CH, WIDE), lambda i: (k, 0, 0))


def held():
    return pl.BlockSpec(memory_space=pltpu.VMEM)


def hold(values):
    return pltpu.with_memory_space_constraint(values, pltpu.VMEM)


def struct(shape, kind=F32):
    return jax.ShapeDtypeStruct(shape, kind)


def to_partner(values, difference):
    return lax.ppermute(values, "dp", [(i, i ^ difference) for i in range(lax.axis_size("dp"))])


def to_other_core(values, difference):
    size = lax.axis_size("dp")
    return lax.ppermute(values, ("view", "dp"), [(i, i ^ (difference + size)) for i in range(2 * size)])


def far_last(ways):
    return (1, 3, 2) if ways == 4 else range(1, ways)


def from_partners(values, shift, ways, crossing=True):
    send = to_other_core if crossing else to_partner
    parts = [to_other_core(values, 0) if crossing else values] + [None] * (ways - 1)
    for offset in far_last(ways):
        parts[offset] = send(values, offset << shift)
    return parts


def stages():
    size = lax.axis_size("dp")
    groups = []
    shift = 0
    while (1 << shift) < size:
        ways = min(4, size >> shift)
        groups.append((shift, ways))
        shift += 2
    assert len(groups) % 2 == 0
    return groups


def sum_parts(values, beside=None):
    groups = stages()
    for shift, ways in groups[:-1]:
        parts = from_partners(values, shift, ways)
        if beside is not None:
            parts, beside = lax.optimization_barrier((parts, beside))
        values = sum(parts)
    return tuple(from_partners(values, *groups[-1])), beside


def stack(parts, inner):
    shape = (len(parts) * parts[0].shape[0],) + parts[0].shape[1:]
    return pl.pallas_call(
        functools.partial(stack_kernel, inner), out_shape=struct(shape, parts[0].dtype), compiler_params=PARAMS, name="stack"
    )(tuple(parts))


def gather_parts(values, groups):
    inner = groups[0][0] > 0
    for shift, ways in groups[:-1]:
        values = stack(from_partners(values, shift, ways), inner)
    return tuple(from_partners(values, *groups[-1]))


def swap_view(values):
    return lax.ppermute(values, "view", [(0, 1), (1, 0)])


def forward_weights(conv):
    shape = (2, 6 * LANE, 2 * LANE)
    return pl.pallas_call(
        forward_weight_kernel,
        grid=(2,),
        in_specs=[pl.BlockSpec((None, CH, WIDE), lambda i: (2 * i + 1, 0, 0))],
        out_specs=pl.BlockSpec((None,) + shape[1:], lambda i: (i, 0, 0)),
        out_shape=struct(shape, BF16),
        compiler_params=PARAMS,
        cost_estimate=pl.CostEstimate(flops=2_000_000_000, bytes_accessed=4_000_000, transcendentals=0),
        name="forward_weight",
    )(conv)


def backward_weights(conv):
    return pl.pallas_call(
        backward_weight_kernel,
        grid=(1,),
        in_specs=[conv_part(k) for k in range(4)],
        out_specs=[whole((2, 6 * LANE, 2 * LANE))] * 2,
        out_shape=[struct((2, 6 * LANE, 2 * LANE), BF16)] * 2,
        compiler_params=PARAMS,
        cost_estimate=pl.CostEstimate(flops=4_000_000_000, bytes_accessed=8_000_000, transcendentals=0),
        name="backward_weight",
    )(conv, conv, conv, conv)


def shards(
    augmented, shake_ratio, labels, labelled, view_order,
    stem_weight, conv_weight, head_weight, norm_param,
    teacher_stem, teacher_conv, teacher_head, teacher_norm,
    first_stem, first_conv, first_head, first_norm,
    second_stem, second_conv, second_head, second_norm,
):
    dp = lax.axis_size("dp")
    all_images = IMAGES * dp
    cell_count = float(all_images * CELLS)
    rows = dp * 2 * IMAGES
    conv, conv_t, conv_f, conv_s = (
        jnp.transpose(v, (0, 2, 1)) for v in (conv_weight, teacher_conv, first_conv, second_conv)
    )
    head, head_t, head_f, head_s = (v.T for v in (head_weight, teacher_head, first_head, second_head))
    pixels = jnp.transpose(augmented[0], (0, 3, 1, 2))
    msg = struct((8, LANE))
    groups = stages()
    last_ways = groups[-1][1]
    recv_spec = (held(),) * last_ways
    norm_spec = whole((2, 4, CH))
    head_spec = whole((CLASSES, CH))
    moved_shape = (3, (SIDE + 4) * 8, LANE)
    frame_one, frame_two = FRAME + (LANE,), (2,) + FRAME + (LANE,)
    values_shape, grad_shape = (ALL, 2 * LANE), struct((GRAD_ROWS, LANE))
    terms_scratch = pltpu.VMEM((16, LANE), F32)

    first_s, first_t, low, moved, stem_sums, message = pl.pallas_call(
        first_kernel,
        in_specs=[pl.BlockSpec(memory_space=pltpu.HBM)] * 5,
        out_specs=[held()] * 6,
        out_shape=[
            pltpu.VMEM(values_shape, F32), pltpu.VMEM(values_shape, F32), pltpu.VMEM(frame_one, BF16),
            pltpu.VMEM(moved_shape, F32), struct((2, 8, LANE)), msg,
        ],
        scratch_shapes=[
            pltpu.VMEM(moved_shape[1:], F32), pltpu.VMEM((STEM_ROWS, 2 * LANE), F32),
            pltpu.VMEM((STEM_ROWS, 2 * LANE), BF16), pltpu.VMEM((2, 9 * LANE, 2 * LANE), BF16),
            pltpu.VMEM(frame_one, BF16), pltpu.VMEM((IMAGES, 3, SIDE, SIDE), BF16), pltpu.VMEM((27, CH), F32),
            pltpu.VMEM((27, CH), F32), pltpu.VMEM((4, CH, WIDE), F32), pltpu.SemaphoreType.DMA((7,)),
        ],
        compiler_params=PARAMS,
        name="first_conv",
    )(*(pltpu.with_memory_space_constraint(v, pltpu.HBM) for v in (pixels, stem_weight, teacher_stem, conv, conv_t)))
    first_s, first_t, low, moved = (hold(v) for v in (first_s, first_t, low, moved))
    recv1, weight_s = sum_parts(message, forward_weights(conv))
    known = pl.pallas_call(
        facts_kernel,
        in_specs=[scalars()] * 4,
        out_specs=held(),
        out_shape=struct((2, 8, LANE)),
        compiler_params=PARAMS,
        name="facts",
    )(shake_ratio, labels, labelled, view_order)
    recv1, weight_t, known = lax.optimization_barrier((recv1, forward_weights(conv_t), known))

    second_s, second_t, hidden, bent_one, image_sums, message = pl.pallas_call(
        functools.partial(second_kernel, cell_count),
        in_specs=[held()] * 2 + [recv_spec] + [held()] * 4,
        out_specs=[held()] * 6,
        out_shape=[pltpu.VMEM(values_shape, F32)] * 2
        + [pltpu.VMEM(frame_two, BF16), pltpu.VMEM(values_shape, F32), struct((4, 8, LANE)), msg],
        scratch_shapes=[pltpu.VMEM(frame_two, BF16), terms_scratch, terms_scratch],
        compiler_params=PARAMS,
        name="second_conv",
    )(first_s, first_t, recv1, norm_param, teacher_norm, weight_s, weight_t)
    second_s, second_t, hidden, bent_one = (hold(v) for v in (second_s, second_t, hidden, bent_one))
    recv2, (back_weight_two, back_weight_one) = sum_parts(message, backward_weights(conv))

    prob = pl.pallas_call(
        functools.partial(teacher_kernel, cell_count),
        in_specs=[held()] * 2 + [recv_spec] + [held()] * 4,
        out_specs=held(),
        out_shape=struct((8, LANE)),
        scratch_shapes=[terms_scratch],
        compiler_params=PARAMS,
        name="teacher_logits",
    )(known, second_t, recv2, teacher_norm, head_t, stem_sums, image_sums)
    other = swap_view(prob)
    facts, bent_two = pl.pallas_call(
        functools.partial(student_kernel, cell_count),
        in_specs=[held()] * 2 + [recv_spec] + [held()] * 4,
        out_specs=[held()] * 2,
        out_shape=[struct((8, 3 * LANE)), pltpu.VMEM(values_shape, F32)],
        scratch_shapes=[terms_scratch],
        compiler_params=PARAMS,
        cost_estimate=pl.CostEstimate(flops=4_000_000_000, bytes_accessed=8_000_000, transcendentals=0),
        name="student_logits",
    )(known, second_s, recv2, norm_param, head, stem_sums, image_sums)
    bent_two = hold(bent_two)
    facts, other = lax.optimization_barrier((facts, other))
    facts = pl.pallas_call(
        assemble_kernel, out_shape=struct((1, 8, 3 * LANE)), compiler_params=PARAMS, name="assemble"
    )(facts, other)
    recv3 = gather_parts(facts, groups[::-1])

    du, dy, message, small, dmix = pl.pallas_call(
        functools.partial(back_second_kernel, cell_count, float(all_images)),
        in_specs=[held()] * 4 + [recv_spec] * 2 + [(held(),) * groups[0][1]] + [held()] * 3,
        out_specs=[held()] * 5,
        out_shape=[
            pltpu.VMEM(values_shape, F32), pltpu.VMEM(frame_two, BF16), msg, struct((24, LANE)), struct((8, LANE)),
        ],
        scratch_shapes=[
            terms_scratch, terms_scratch, pltpu.VMEM((3, rows, LANE), F32), pltpu.VMEM((8, LANE), F32),
        ],
        compiler_params=PARAMS,
        name="back_second",
    )(second_s, first_s, bent_two, bent_one, recv1, recv2, recv3, norm_param, head, back_weight_two)
    du, dy = hold(du), hold(dy)

    def second_weight(other):
        return pl.pallas_call(
            functools.partial(second_weight_kernel, other),
            in_specs=[held()] * 2,
            out_specs=held(),
            out_shape=grad_shape,
            scratch_shapes=[pltpu.VMEM((2 * LANE, 6 * LANE), F32)],
            compiler_params=PARAMS,
            cost_estimate=pl.CostEstimate(flops=4_000_000_000, bytes_accessed=8_000_000, transcendentals=0),
            name="second_weight",
        )(hidden, dy)

    send2, keep2 = second_weight(True), second_weight(False)
    recv5, send2 = sum_parts(message, send2)
    recv_grad2 = swap_view(send2)
    recv5, keep2, recv_grad2 = lax.optimization_barrier((recv5, keep2, recv_grad2))

    frame, keep1, send1 = pl.pallas_call(
        functools.partial(back_weight_kernel, cell_count),
        in_specs=[held()] * 3 + [recv_spec] * 2 + [held()] * 2,
        out_specs=[held()] * 3,
        out_shape=[pltpu.VMEM(frame_two, BF16)] + [struct((GRAD_ROWS + 32, LANE))] * 2,
        scratch_shapes=[terms_scratch, pltpu.VMEM((2 * LANE, 9 * LANE), F32)],
        compiler_params=PARAMS,
        cost_estimate=pl.CostEstimate(flops=8_000_000_000, bytes_accessed=16_000_000, transcendentals=0),
        name="back_weight",
    )(du, first_s, low, recv1, recv5, norm_param, small)
    frame = hold(frame)
    recv_grad1 = swap_view(send1)

    def back_stem(step, before=()):
        going = step < STEPS - 1
        return pl.pallas_call(
            functools.partial(back_stem_kernel, step),
            in_specs=[held()] * (4 + len(before)),
            out_specs=[held()] * 2 if going else held(),
            out_shape=[struct((LINE, LANE)), struct((STEM_ROWS, LANE))] if going else struct((27, LANE)),
            compiler_params=PARAMS,
            cost_estimate=pl.CostEstimate(flops=2_000_000_000, bytes_accessed=4_000_000, transcendentals=0),
            name="back_stem",
        )(frame, moved, dmix, back_weight_one, *before)

    started = back_stem(0)
    recv_grad1, started = lax.optimization_barrier((recv_grad1, started))
    coded = pl.pallas_call(
        encode_kernel,
        out_shape=[struct((2 * PIECE, LANE), jnp.int16)] * QUARTERS,
        scratch_shapes=[pltpu.VMEM((2, GRAD_ROWS, LANE), F32)],
        compiler_params=PARAMS,
        name="encode",
    )(keep2, recv_grad2, keep1, recv_grad1)
    scattered = [coded[0]] + [None] * (QUARTERS - 1)
    for offset in far_last(QUARTERS):
        scattered[offset] = to_partner(coded[offset], offset)
    scattered = tuple(scattered)

    stem_grad = started
    for step in range(1, STEPS):
        stem_grad = back_stem(step, tuple(stem_grad))

    stem_grad, scattered = lax.optimization_barrier((stem_grad, scattered))
    code_shape = struct((CODE_ROWS, LANE), jnp.int16)
    codes = pl.pallas_call(combine_kernel, out_shape=code_shape, compiler_params=PARAMS, name="combine")(
        scattered, stem_grad
    )
    for group in groups[1:]:
        codes = pl.pallas_call(recode_kernel, out_shape=code_shape, compiler_params=PARAMS, name="recode")(
            tuple(from_partners(codes, *group, crossing=False))
        )
    own = tuple(from_partners(codes, *groups[0], crossing=False))
    other_grads = tuple(swap_view(part) for part in own)
    own_parts = pl.pallas_call(
        decode_kernel,
        out_shape=[struct((2, GRAD_ROWS, LANE)), struct((27, LANE)), struct((8, LANE))],
        compiler_params=PARAMS,
        name="decode",
    )(own)
    own_parts, other_grads = lax.optimization_barrier((own_parts, other_grads))

    conv_block = pl.BlockSpec((None, CH, WIDE), lambda i: (i, 0, 0))
    stem_block, norm_block = whole((27, CH)), norm_spec
    code_spec = (held(),) * QUARTERS
    grads_scratch = pltpu.VMEM((2, GRAD_ROWS, LANE), F32)
    outs = pl.pallas_call(
        update_kernel,
        grid=(4,),
        in_specs=[held()] * 3 + [code_spec] + [held()] * 18,
        out_specs=[conv_block] * 5 + [stem_block] * 5 + [head_spec] * 5 + [norm_block] * 4 + [whole((1, 1))] * 4,
        out_shape=[struct((4, CH, WIDE))] * 4 + [struct((4, CH, WIDE), BF16)]
        + [struct((27, CH))] * 4 + [struct((27, CH), BF16)]
        + [struct((CLASSES, CH))] * 4 + [struct((CLASSES, CH), BF16)]
        + [struct((2, 4, CH))] * 4 + [struct((1, 1))] * 4,
        scratch_shapes=[pltpu.VMEM((8, LANE), F32), grads_scratch],
        compiler_params=PARAMS,
        name="update",
    )(
        *own_parts, other_grads, keep1, recv_grad1,
        conv, conv_f, conv_s, conv_t, stem_weight, first_stem, second_stem, teacher_stem,
        head, head_f, head_s, head_t, norm_param, first_norm, second_norm, teacher_norm,
    )
    convs = [jnp.transpose(v, (0, 2, 1)) for v in outs[:5]]
    stems = outs[5:10]
    heads = [v.T for v in outs[10:15]]
    norms = outs[15:19]
    return (
        *(v.reshape(()) for v in outs[19:23]),
        *stems[:4], *convs[:4], *heads[:4], *norms, stems[4], convs[4], heads[4],
    )


def solution(mesh):
    in_specs = (
        (P("view", "dp", None, None, None), P("view", "dp"), P("dp"), P("dp")) + (P(),) * 17
    )
    return jax.shard_map(shards, mesh=mesh, in_specs=in_specs, out_specs=(P(),) * 23, check_vma=False)
```

```python
import functools

import jax
import jax.numpy as jnp
from jax import lax
from jax.experimental import pallas as pl
from jax.experimental.pallas import tpu as pltpu
from jax.sharding import PartitionSpec as P

CLASSES = 10
STEP = 5
EPS_NORM = 1e-05
LEARN_RATE = 0.03
BETA_FIRST = 0.5
BETA_SECOND = 0.5
WEIGHT_DECAY = 0.0001
ADAM_EPS = 1e-08
CLIP_LIMIT = 0.02
TEACHER_KEEP = 0.9
CONS_WEIGHT = 10.0

F32 = jnp.float32
BF16 = jnp.bfloat16
LANE = 128
CH = 96
SIDE = 32
CELLS = SIDE * SIDE
IMAGES = 4
QUARTERS = 4
ACROSS = SIDE // QUARTERS
TILE = IMAGES * QUARTERS
LINE = ACROSS * TILE
STEPS = 4
DEEP = SIDE // STEPS
CHUNK = DEEP * LINE
ALL = SIDE * LINE
BLOCK = 64
TAPS = 9
WIDE = TAPS * CH
BLOCKS = -(-WIDE // LANE)
GRAD_ROWS = BLOCKS * CH
SHARE = GRAD_ROWS // QUARTERS
PIECE = -(-(SHARE + 1) // 16) * 16
CODE_ROWS = 2 * PIECE + SIDE
STEM_ROWS = 80
CODE_TOP = 32000.0
FRAME = (SIDE + 2, ACROSS + 2, TILE)
PARAMS = pltpu.CompilerParams(vmem_limit_bytes=14 * 1024 * 1024)


def dot(a, b):
    return jnp.dot(a, b, preferred_element_type=F32)


def dot_rows(a, b):
    return lax.dot_general(a, b, (((0,), (0,)), ((), ())), preferred_element_type=F32)


def dot_lanes(a, b):
    return lax.dot_general(a, b, (((1,), (1,)), ((), ())), preferred_element_type=F32)


def frame_line(frame, first_line, values):
    lines = values.shape[0] // LINE
    width = values.shape[1]
    tiles = values.reshape(lines, ACROSS, TILE, width)
    row = lax.broadcasted_iota(jnp.int32, (1, TILE, 1), 1)
    before = jnp.where(row >= IMAGES, pltpu.roll(tiles[:, ACROSS - 1], IMAGES, 1), 0.0)
    after = jnp.where(row < TILE - IMAGES, pltpu.roll(tiles[:, 0], TILE - IMAGES, 1), 0.0)
    place = slice(first_line + 1, first_line + 1 + lines)
    frame[place, 1 : ACROSS + 1] = tiles.astype(BF16)
    frame[place, 0] = before.astype(BF16)
    frame[place, ACROSS + 1] = after.astype(BF16)


def clear_frame(frame):
    blank = jnp.zeros(frame.shape[1:], BF16)
    frame[0] = blank
    frame[SIDE + 1] = blank


def taps(frame, step, rows):
    parts = []
    for dy in rows:
        for kx in range(3):
            place = step * DEEP + 1 + dy
            lines = frame[place : place + DEEP, kx : kx + ACROSS]
            parts.append(lines.reshape(CHUNK, lines.shape[-1]))
    return jnp.concatenate(parts, axis=1)


def fold_lines(both, carry):
    upper = jnp.concatenate([carry, both[: CHUNK - LINE, LANE:]], axis=0)
    return both[:, :LANE] + upper, both[CHUNK - LINE :, LANE:]


def blank_line():
    return jnp.zeros((LINE, LANE), F32)


def new_lines(step):
    first = 0 if step == 0 else step * DEEP + 1
    return first, min((step + 1) * DEEP + 1, SIDE)


def chunk_rows(step):
    return slice(step * CHUNK, (step + 1) * CHUNK)


def eight(values):
    parts = values.reshape(values.shape[0] // 8, 8, values.shape[1])
    while parts.shape[0] > 1:
        middle = parts.shape[0] // 2
        rest = parts[2 * middle :]
        parts = parts[:middle] + parts[middle : 2 * middle]
        if rest.shape[0]:
            parts = jnp.concatenate([parts[:-1], parts[-1:] + rest], axis=0) if middle > 1 else parts + rest
    return parts[0]


def both_halves(sums):
    return sums + pltpu.roll(sums, IMAGES, 0)


def tap_block(raw, tap):
    return raw[:, tap * CH : (tap + 1) * CH]


def image_lines(image_ref, plain, moved):
    plain[...] = jnp.zeros(plain.shape, F32)
    for channel in range(3):
        side_by_side = jnp.concatenate([image_ref[i, channel].astype(F32) for i in range(IMAGES)], axis=1)
        plain[pl.ds(8 + channel, SIDE, stride=8), :] = side_by_side
    source = lax.broadcasted_iota(jnp.int32, (LANE, LANE), 0)
    target = lax.broadcasted_iota(jnp.int32, (LANE, LANE), 1)
    same = source // SIDE == (target & (IMAGES - 1))
    across = ((target // IMAGES) & (QUARTERS - 1)) * ACROSS + target // TILE
    for kx in range(3):
        picks = jnp.where(same & ((source & (SIDE - 1)) == across + (kx - 1)), 1.0, 0.0).astype(BF16)
        moved[kx] = dot(plain[...].astype(BF16), picks)


def image_taps(moved, first_line, lines):
    columns = []
    for line in range(lines):
        place = (first_line + line) * 8
        parts = [moved[kx, place : place + 24, :] for kx in range(3)]
        columns.append(jnp.concatenate(parts + [jnp.zeros((8, LANE), F32)], axis=0))
    return jnp.concatenate(columns, axis=1).astype(BF16)


def stem_row(tap):
    return (tap % 3) * 24 + (tap // 3) * 8


def pad_lanes(row):
    return jnp.concatenate([row, jnp.zeros((row.shape[0], LANE - row.shape[1]), row.dtype)], axis=1)


def norm_terms(sums, squares, cell_count):
    average = sums / cell_count
    inverse = lax.rsqrt(squares / cell_count - average * average + EPS_NORM)
    return average, inverse


def column_sum(values):
    return jnp.sum(values, axis=0, keepdims=True)


def slope_rest(half, tanh, product):
    return (tanh + half) - product * tanh


def first_kernel(
    image_hbm, stem_s_hbm, stem_t_hbm, raw_s, raw_t,
    first_s, first_t, frame_s, moved_ref, pooled_ref, msg_ref,
    plain, wst32, wst, wf, frame_t, image_ref, stem_s, stem_t, raw, sems,
):
    coming = [
        pltpu.make_async_copy(source, target, sems.at[k])
        for k, (source, target) in enumerate((
            (image_hbm, image_ref), (stem_s_hbm, stem_s), (stem_t_hbm, stem_t),
            (raw_s.at[0], raw.at[0]), (raw_s.at[2], raw.at[1]), (raw_t.at[0], raw.at[2]), (raw_t.at[2], raw.at[3]),
        ))
    ]
    for copy in coming:
        copy.start()
    wf[...] = jnp.zeros(wf.shape, BF16)
    wst32[...] = jnp.zeros(wst32.shape, F32)
    clear_frame(frame_s)
    clear_frame(frame_t)
    for copy in coming[:3]:
        copy.wait()
    image_lines(image_ref, plain, moved_ref)
    for n, stem in enumerate((stem_s, stem_t)):
        for tap in range(TAPS):
            row = stem_row(tap)
            wst32[row : row + 3, n * LANE : n * LANE + CH] = stem[3 * tap : 3 * tap + 3, :]
    wst[...] = wst32[...].astype(BF16)
    for copy in coming[3:]:
        copy.wait()
    for n in range(2):
        for b in range(2):
            for tap in range(TAPS):
                wf[n, tap * LANE : tap * LANE + CH, b * LANE : b * LANE + CH] = jnp.transpose(
                    tap_block(raw.at[2 * n + b], tap)
                ).astype(BF16)
    pooled = [0.0, 0.0]
    sums = [0.0] * 8
    for step in range(STEPS):
        first_line, end = new_lines(step)
        stems = dot_rows(image_taps(moved_ref, first_line, end - first_line), wst[...])
        for n, (frame, out_ref) in enumerate(((frame_s, first_s), (frame_t, first_t))):
            stem = stems[:, n * LANE : (n + 1) * LANE]
            pooled[n] += eight(stem)
            frame_line(frame, first_line, stem)
            out = dot(taps(frame, step, (-1, 0, 1)), wf[n])
            out_ref[chunk_rows(step), :] = out
            for b in range(2):
                part = out[:, b * LANE : (b + 1) * LANE]
                sums[4 * n + 2 * b] += eight(part)
                sums[4 * n + 2 * b + 1] += eight(part * part)
    for n in range(2):
        pooled_ref[n] = both_halves(pooled[n])
    spread_sums(msg_ref, sums)


def total_of(refs):
    total = refs[0][...]
    for ref in refs[1:]:
        total = total + ref[...]
    return total


def spread_sums(msg_ref, sums):
    sums = [column_sum(part) for part in sums]
    if len(sums) < 8:
        sums.append(jnp.zeros((8 - len(sums), LANE), F32))
    msg_ref[...] = jnp.concatenate(sums, axis=0)


def forward_weight_kernel(raw_ref, w_ref):
    w_ref[...] = jnp.zeros(w_ref.shape, BF16)
    for ky in range(3):
        for kx in range(3):
            row = (ky // 2) * 3 * LANE + kx * LANE
            lane = LANE if ky == 0 else 0
            w_ref[row : row + CH, lane : lane + CH] = jnp.transpose(tap_block(raw_ref, ky * 3 + kx)).astype(BF16)


def backward_weight_kernel(cw0, cw1, cw2, cw3, two_ref, one_ref):
    two_ref[...] = jnp.zeros(two_ref.shape, BF16)
    one_ref[...] = jnp.zeros(one_ref.shape, BF16)
    for ky in range(3):
        for kx in range(3):
            tap = (2 - ky) * 3 + 2 - kx
            lane = LANE if ky == 0 else 0
            for b, (inner, outer) in enumerate(((cw0, cw1), (cw2, cw3))):
                row = (ky // 2) * 3 * LANE + kx * LANE
                two_ref[b, row : row + CH, lane : lane + CH] = (0.5 * tap_block(outer, tap)).astype(BF16)
                one_ref[b, row : row + CH, lane : lane + CH] = tap_block(inner, tap).astype(BF16)


def norm_rows(sums, norm, terms, first_row, norm_index, cell_count):
    for b in range(2):
        row = first_row + 2 * b
        average, inverse = norm_terms(sums[row : row + 1], sums[row + 1 : row + 2], cell_count)
        gain = pad_lanes(norm[0, 2 * b + norm_index : 2 * b + norm_index + 1, :])
        shift = pad_lanes(norm[1, 2 * b + norm_index : 2 * b + norm_index + 1, :])
        scale = inverse * gain
        terms[8 * b : 8 * b + 1, :] = 0.5 * scale
        terms[8 * b + 1 : 8 * b + 2, :] = 0.5 * (shift - average * scale)
        terms[8 * b + 2 : 8 * b + 3, :] = inverse
        terms[8 * b + 3 : 8 * b + 4, :] = -average * inverse
        terms[8 * b + 4 : 8 * b + 5, :] = scale


def term(terms, b, k):
    return terms[8 * b + k : 8 * b + k + 1, :]


def second_kernel(
    cell_count, first_s, first_t, recv_ref, norm_s, norm_t, ws_ref, wt_ref,
    second_s, second_t, frame_s, bent_ref, plain_ref, msg_ref,
    frame_t, terms_s, terms_t,
):
    received = total_of(recv_ref)
    norm_rows(received, norm_s, terms_s, 0, 0, cell_count)
    norm_rows(received, norm_t, terms_t, 4, 0, cell_count)
    nets = ((first_s, terms_s, frame_s, ws_ref, second_s), (first_t, terms_t, frame_t, wt_ref, second_t))
    sums = [0.0] * 8
    carry = [blank_line()] * 4
    for _, _, frames, _, _ in nets:
        for b in range(2):
            clear_frame(frames.at[b])
    for step in range(STEPS):
        first_line, end = new_lines(step)
        for n, (source, terms, frames, w, target) in enumerate(nets):
            for b in range(2):
                k = 2 * n + b
                lanes = slice(b * LANE, (b + 1) * LANE)
                half = source[first_line * LINE : end * LINE, lanes] * term(terms, b, 0) + term(terms, b, 1)
                tanh = jnp.tanh(half)
                product = half * tanh
                frame_line(frames.at[b], first_line, half + product)
                if n == 0:
                    bent_ref[first_line * LINE : end * LINE, lanes] = slope_rest(half, tanh, product)
                out, carry[k] = fold_lines(dot(taps(frames.at[b], step, (0, 1)), w[b]), carry[k])
                target[chunk_rows(step), lanes] = out
                sums[2 * k] += eight(out)
                sums[2 * k + 1] += eight(out * out)
    for k in range(4):
        plain_ref[k] = sums[2 * k]
    spread_sums(msg_ref, sums)


def head_rows(head_ref):
    padded = jnp.concatenate([head_ref[...], jnp.zeros((LANE - CLASSES, CH), F32)], axis=0)
    return pad_lanes(padded).astype(BF16)


def alpha_of(ratio_ref, image):
    return (ratio_ref[0, image].astype(F32) + 1.0) / 18.0


def alpha_rows(ratio_ref):
    row = lax.broadcasted_iota(jnp.int32, (2 * IMAGES, LANE), 0) & (IMAGES - 1)
    alpha = jnp.zeros((2 * IMAGES, LANE), F32)
    for k in range(IMAGES):
        alpha = jnp.where(row == k, alpha_of(ratio_ref, k), alpha)
    return alpha


def class_lanes(rows):
    return lax.broadcasted_iota(jnp.int32, (rows, LANE), 1) < CLASSES


def log_softmax(logits, valid):
    top = jnp.max(jnp.where(valid, logits, -3e38), axis=1, keepdims=True)
    moved = logits - top
    total = jnp.sum(jnp.where(valid, jnp.exp(moved), 0.0), axis=1, keepdims=True)
    return moved - jnp.log(total)


def facts_kernel(ratio_ref, labels_ref, labelled_ref, order_ref, facts_ref):
    dp_index = lax.axis_index("dp")
    facts_ref[0] = alpha_rows(ratio_ref)
    lane = lax.broadcasted_iota(jnp.int32, (2 * IMAGES, LANE), 1)
    row = lax.broadcasted_iota(jnp.int32, (2 * IMAGES, LANE), 0)
    info = jnp.zeros((2 * IMAGES, LANE), F32)
    for k in range(IMAGES):
        facts = (
            alpha_of(ratio_ref, k),
            labels_ref[k].astype(F32),
            labelled_ref[k].astype(F32),
            order_ref[dp_index * IMAGES + k].astype(F32),
        )
        for place, fact in enumerate(facts):
            info = jnp.where((row == k) & (lane == 32 + place), fact, info)
    facts_ref[1] = info


def pooled_low(alpha, sums, stem_sums):
    total = alpha * both_halves(sums[0]) + (1.0 - alpha) * both_halves(sums[1])
    return ((total + stem_sums) / CELLS).astype(BF16)


def teacher_kernel(
    cell_count, facts_ref, second_ref, recv_ref, norm, head_ref, stem_sum_ref, image_sum_ref,
    prob_ref,
    terms,
):
    norm_rows(total_of(recv_ref), norm, terms, 4, 1, cell_count)
    plain, curved = [image_sum_ref[2 + b] for b in range(2)], [0.0] * 2
    for block in range(ALL // BLOCK):
        for b in range(2):
            values = second_ref[block * BLOCK : (block + 1) * BLOCK, b * LANE : (b + 1) * LANE]
            half = values * term(terms, b, 0) + term(terms, b, 1)
            curved[b] += eight(half * jnp.tanh(half))
    sums = [plain[b] * term(terms, b, 0) + (CELLS // 2) * term(terms, b, 1) + curved[b] for b in range(2)]
    low = pooled_low(facts_ref[0], sums, stem_sum_ref[1])
    logits = dot_lanes(low, head_rows(head_ref))
    valid = class_lanes(2 * IMAGES)
    first_rows = lax.broadcasted_iota(jnp.int32, (2 * IMAGES, LANE), 0) < IMAGES
    prob = jnp.where(valid & first_rows, jnp.exp(log_softmax(logits, valid)), 0.0)
    prob_ref[...] = pltpu.roll(prob.astype(BF16).astype(F32), 16, 1)


def student_kernel(
    cell_count, facts_ref, second_ref, recv_ref, norm, head_ref, stem_sum_ref, image_sum_ref,
    msg_ref, bent_ref,
    terms,
):
    norm_rows(total_of(recv_ref), norm, terms, 0, 1, cell_count)
    plain = [image_sum_ref[b] for b in range(2)]
    curved, bent, bent_values = ([0.0] * 2 for _ in range(3))
    for block in range(ALL // BLOCK):
        for b in range(2):
            values = second_ref[block * BLOCK : (block + 1) * BLOCK, b * LANE : (b + 1) * LANE]
            half = values * term(terms, b, 0) + term(terms, b, 1)
            tanh = jnp.tanh(half)
            product = half * tanh
            slope = slope_rest(half, tanh, product)
            bent_ref[block * BLOCK : (block + 1) * BLOCK, b * LANE : (b + 1) * LANE] = slope
            curved[b] += eight(product)
            bent[b] += eight(slope)
            bent_values[b] += eight(slope * values)
    cells = CELLS // 2
    sums = [plain[b] * term(terms, b, 0) + cells * term(terms, b, 1) + curved[b] for b in range(2)]
    slopes = [0.5 * (cells + bent[b]) for b in range(2)]
    sums += slopes
    sums += [
        term(terms, b, 2) * (0.5 * (plain[b] + bent_values[b])) + term(terms, b, 3) * slopes[b] for b in range(2)
    ]
    low = pooled_low(facts_ref[0], sums, stem_sum_ref[0])
    logits = dot_lanes(low, head_rows(head_ref))
    rows = 2 * IMAGES
    info = jnp.where(class_lanes(rows), logits, facts_ref[1])
    row = lax.broadcasted_iota(jnp.int32, (rows, LANE), 0)
    for b in range(2):
        msg_ref[:, b * LANE : (b + 1) * LANE] = jnp.where(
            row < IMAGES, both_halves(sums[2 + b]), both_halves(sums[4 + b])
        )
    msg_ref[:, 2 * LANE :] = jnp.where(row < IMAGES, info, low.astype(F32))


def assemble_kernel(facts_ref, prob_ref, out_ref):
    out_ref[0, :, 0 : 2 * LANE] = facts_ref[:, 0 : 2 * LANE]
    out_ref[0, :, 2 * LANE :] = facts_ref[:, 2 * LANE :] + prob_ref[...]


def loss_part(images, all_images, cell_count, recv_refs, head_ref, rows_ref, means, small_ref):
    view = lax.axis_index("view")
    received = jnp.concatenate([ref[...] for ref in recv_refs], axis=0)
    count = received.shape[0] * 2 * images
    received = received.reshape(count, 3 * LANE)
    raw = received[:, 2 * LANE :]
    row = lax.broadcasted_iota(jnp.int32, (count, 1), 0)
    part = row & (2 * images - 1)
    once = part < images
    facts = jnp.where(once, raw, pltpu.roll(raw, images, 0))
    group, inner = row // (2 * images), received.shape[0] // (2 * images * len(recv_refs))
    offset = (group % inner) * len(recv_refs) + group // inner
    image = ((offset ^ lax.axis_index("dp")) * images + (part & (images - 1))).astype(F32)
    alpha = facts[:, 32:33]
    label = facts[:, 33:34]
    labelled = facts[:, 34:35]
    order = facts[:, 35:36]
    eye = row == lax.broadcasted_iota(jnp.int32, (count, count), 1)
    image_lane = jnp.sum(jnp.where(eye, image, 0.0), axis=0, keepdims=True)
    order_lane = jnp.sum(jnp.where(eye, order, 0.0), axis=0, keepdims=True)
    first_lane = jnp.sum(jnp.where(eye & once, 1.0, 0.0), axis=0, keepdims=True)
    is_one = jnp.where(view == 0, 1.0, 0.0)
    ours = is_one * image + (1.0 - is_one) * order
    theirs = is_one * order_lane + (1.0 - is_one) * image_lane
    match = jnp.where((ours == theirs) & (first_lane > 0.5), 1.0, 0.0).astype(BF16)
    valid = class_lanes(count)
    other = pltpu.roll(facts, LANE - 16, 1)
    target = dot(match, jnp.where(valid, other, 0.0).astype(BF16))
    log_prob = jnp.where(valid, log_softmax(jnp.where(valid, facts, 0.0), valid), 0.0)
    probs = jnp.where(valid, jnp.exp(log_prob), 0.0)
    lane = lax.broadcasted_iota(jnp.int32, (count, LANE), 1)
    onehot = jnp.where(lane.astype(F32) == label, 1.0, 0.0)
    total = jnp.sum(jnp.where(once, labelled, 0.0), axis=0, keepdims=True)
    mask = labelled * is_one
    away = probs - target
    grad_prob = CONS_WEIGHT / all_images * away
    grad = mask * (probs - onehot) / total + probs * (
        grad_prob - jnp.sum(probs * grad_prob, axis=1, keepdims=True)
    )
    grad_low = grad.astype(BF16)
    dmix = dot(grad_low, head_rows(head_ref)) / CELLS
    weights = (dmix * alpha, dmix * (1.0 - alpha))
    for b in range(2):
        product = weights[b] * received[:, b * LANE : (b + 1) * LANE]
        plain = column_sum(jnp.where(once, product, 0.0))
        normal = column_sum(jnp.where(once, 0.0, product))
        means[2 * b : 2 * b + 1, :] = plain / cell_count
        means[2 * b + 1 : 2 * b + 2, :] = normal / cell_count
        rows_ref[b] = weights[b]
        small_ref[16 + 2 * b : 16 + 2 * b + 1, :] = plain
        small_ref[16 + 2 * b + 1 : 16 + 2 * b + 2, :] = normal
    rows_ref[2] = dmix
    cross = -jnp.sum(
        jnp.where(once, mask * jnp.sum(onehot * log_prob, axis=1, keepdims=True), 0.0), axis=0, keepdims=True
    )
    consistency = jnp.sum(
        jnp.where(once, jnp.sum(away * away, axis=1, keepdims=True), 0.0), axis=0, keepdims=True
    )
    lane_row = lax.broadcasted_iota(jnp.int32, (1, LANE), 1)
    small_ref[20:21, :] = jnp.where(
        lane_row == 0, cross, jnp.where(lane_row == 1, consistency, jnp.where(lane_row == 2, total, 0.0))
    )
    small_ref[21:24, :] = jnp.zeros((3, LANE), F32)
    pooled = jnp.where(once, 0.0, raw).astype(BF16)
    small_ref[0:16, :] = dot_rows(grad_low, pooled)[0:16, :]


def pack_grad(ref, blocks):
    side_by_side = jnp.concatenate(blocks + [jnp.zeros((CH, BLOCKS * LANE - WIDE), F32)], axis=1)
    for k in range(BLOCKS):
        ref[k * CH : (k + 1) * CH, :] = side_by_side[:, k * LANE : (k + 1) * LANE]


def keep_and_send(keep_ref, send_ref, blocks):
    view = lax.axis_index("view")
    for own, ref in ((0, keep_ref), (1, send_ref)):
        @pl.when(view == own)
        def _():
            pack_grad(ref, blocks[0])

        @pl.when(view != own)
        def _():
            pack_grad(ref, blocks[1])


def back_second_kernel(
    cell_count, all_images,
    second_ref, first_ref, bent_two, bent_one, recv1_ref, recv2_ref, recv3_ref, norm, head_ref, w_ref,
    du_ref, frames, msg_ref, small_ref, dmix_ref,
    terms1, terms2, rows_ref, means,
):
    rows = 2 * IMAGES
    norm_rows(total_of(recv1_ref), norm, terms1, 0, 0, cell_count)
    norm_rows(total_of(recv2_ref), norm, terms2, 0, 1, cell_count)
    loss_part(IMAGES, all_images, cell_count, recv3_ref, head_ref, rows_ref, means, small_ref)
    dmix_ref[...] = rows_ref[2, 0:rows, :]
    scales, linears, offsets = [], [], []
    for b in range(2):
        gain = term(terms2, b, 4)
        mean, slant = means[2 * b : 2 * b + 1, :], means[2 * b + 1 : 2 * b + 2, :]
        scales.append(0.5 * gain * rows_ref[b, 0:rows, :])
        linears.append(-gain * slant * term(terms2, b, 2))
        offsets.append(scales[b] - gain * (mean + slant * term(terms2, b, 3)))
    sums = [0.0] * 4
    carry = [blank_line()] * 2
    for b in range(2):
        clear_frame(frames.at[b])
    for step in range(STEPS):
        first_line, end = new_lines(step)
        for b in range(2):
            lanes = slice(b * LANE, (b + 1) * LANE)
            values = second_ref[first_line * LINE : end * LINE, lanes]
            bent = bent_two[first_line * LINE : end * LINE, lanes]
            shape = (values.shape[0] // 8, 8, LANE)
            dy = (bent.reshape(shape) * scales[b][None] + offsets[b][None]).reshape(values.shape) + values * linears[b]
            frame_line(frames.at[b], first_line, dy)
            dh, carry[b] = fold_lines(dot(taps(frames.at[b], step, (0, 1)), w_ref[b]), carry[b])
            before = first_ref[chunk_rows(step), lanes]
            du = dh + dh * bent_one[chunk_rows(step), lanes]
            du_ref[chunk_rows(step), lanes] = du
            sums[2 * b] += eight(du)
            sums[2 * b + 1] += eight(du * before)
    for b in range(2):
        plain, product = column_sum(sums[2 * b]), column_sum(sums[2 * b + 1])
        sums[2 * b] = plain
        sums[2 * b + 1] = term(terms1, b, 2) * product + term(terms1, b, 3) * plain
    spread_sums(msg_ref, sums)


def middle_lines(frame, first_line):
    return frame[first_line + 1 : first_line + 1 + DEEP, 1 : ACROSS + 1].reshape(CHUNK, frame.shape[-1])


def second_weight_kernel(other, frame_ref, dy_ref, grad_ref, gacc):
    view = lax.axis_index("view")
    branch = 1 - view if other else view
    for step in range(STEPS):
        pair = jnp.concatenate(
            [middle_lines(dy_ref.at[branch], step * DEEP), middle_lines(dy_ref.at[branch], step * DEEP + 1)], axis=1
        )
        product = dot_rows(pair, taps(frame_ref.at[branch], step, (0, 1)))
        gacc[...] = product if step == 0 else gacc[...] + product
    blocks = []
    for tap in range(TAPS):
        ky, kx = tap // 3, tap % 3
        row = LANE if ky == 0 else 0
        lane = (ky // 2) * 3 * LANE + kx * LANE
        blocks.append(gacc[row : row + CH, lane : lane + CH])
    pack_grad(grad_ref, blocks)


def back_weight_kernel(
    cell_count,
    du_ref, first_ref, low_ref, recv1_ref, recv5_ref, norm, small_ref,
    frame_ref, keep_ref, send_ref,
    terms1, gacc,
):
    norm_rows(total_of(recv1_ref), norm, terms1, 0, 0, cell_count)
    sums = total_of(recv5_ref)
    for ref in (keep_ref, send_ref):
        ref[GRAD_ROWS : GRAD_ROWS + 24, :] = small_ref[...]
        ref[GRAD_ROWS + 24 :, :] = sums
    means = sums / cell_count
    linears, offsets = [], []
    for b in range(2):
        mean, slant = means[2 * b : 2 * b + 1, :], means[2 * b + 1 : 2 * b + 2, :]
        linears.append(-term(terms1, b, 4) * slant * term(terms1, b, 2))
        offsets.append(-term(terms1, b, 4) * (mean + slant * term(terms1, b, 3)))
    for b in range(2):
        clear_frame(frame_ref.at[b])
    for step in range(STEPS):
        parts = []
        for b in range(2):
            lanes = slice(b * LANE, (b + 1) * LANE)
            parts.append(
                du_ref[chunk_rows(step), lanes] * term(terms1, b, 4)
                + (first_ref[chunk_rows(step), lanes] * linears[b] + offsets[b])
            )
        pair = jnp.concatenate(parts, axis=1)
        for b in range(2):
            frame_line(frame_ref.at[b], step * DEEP, parts[b])
        product = dot_rows(pair.astype(BF16), taps(low_ref, step, (-1, 0, 1)))
        gacc[...] = product if step == 0 else gacc[...] + product
    keep_and_send(
        keep_ref, send_ref,
        [[gacc[b * LANE : b * LANE + CH, tap * LANE : tap * LANE + CH] for tap in range(TAPS)] for b in range(2)],
    )


def back_stem_steps(steps, frame_ref, moved_ref, dmix_ref, w_ref, carry, total):
    for step in steps:
        both = dot(taps(frame_ref.at[0], step, (0, 1)), w_ref[0]) + dot(taps(frame_ref.at[1], step, (0, 1)), w_ref[1])
        dstem, carry = fold_lines(both, carry)
        dstem = (dstem.reshape(CHUNK // 8, 8, LANE) + dmix_ref[...][None]).reshape(CHUNK, LANE)
        total += dot(image_taps(moved_ref, step * DEEP, DEEP), dstem.astype(BF16))
    return carry, total


def back_stem_kernel(step, frame_ref, moved_ref, dmix_ref, w_ref, *refs):
    carry, total = (blank_line(), 0.0) if step == 0 else (refs[0][...], refs[1][...])
    carry, total = back_stem_steps((step,), frame_ref, moved_ref, dmix_ref, w_ref, carry, total)
    if step < STEPS - 1:
        refs[-2][...] = carry
        refs[-1][...] = total
    else:
        rows = [total[stem_row(tap) : stem_row(tap) + 3, :] for tap in range(TAPS)]
        refs[-1][...] = jnp.concatenate(rows, axis=0)


def code(values):
    top = jnp.max(jnp.abs(values), axis=0, keepdims=True)
    power = jnp.clip(jnp.ceil(jnp.log2(jnp.maximum(top, 1e-30)) + 0.01), -100.0, 100.0)
    counted = jnp.round(values * (jnp.exp2(-power) * CODE_TOP))
    return counted, power


def unit(power):
    return jnp.exp2(power) * (1.0 / CODE_TOP)


def coded_rows(values, rows):
    counted, power = code(values)
    parts = [counted, power]
    if rows - values.shape[0] - 1:
        parts.append(jnp.zeros((rows - values.shape[0] - 1, LANE), F32))
    return jnp.concatenate(parts, axis=0).astype(jnp.int32).astype(jnp.int16)


def decoded(values, count):
    whole_part = values.astype(jnp.int32).astype(F32)
    return whole_part[:count] * unit(whole_part[count : count + 1])


def encode_kernel(keep2, recv2, keep1, recv1, *refs):
    outs, total = refs[:-1], refs[-1]
    for k, (keep, recv) in enumerate(((keep1, recv1), (keep2, recv2))):
        total[k] = keep[0:GRAD_ROWS, :] + recv[0:GRAD_ROWS, :]
    mine = lax.axis_index("dp") & (QUARTERS - 1)
    for offset, out in enumerate(outs):
        place = pl.multiple_of((mine ^ offset) * SHARE, 8)
        for k in range(2):
            out[k * PIECE : (k + 1) * PIECE, :] = coded_rows(total[k, pl.ds(place, SHARE), :], PIECE)


def summed(refs, first, count, rows):
    total = decoded(refs[0][first : first + rows, :], count)
    for ref in refs[1:]:
        total += decoded(ref[first : first + rows, :], count)
    return total


def combine_kernel(recv_refs, stem_ref, out_ref):
    for k in range(2):
        out_ref[k * PIECE : (k + 1) * PIECE, :] = coded_rows(summed(recv_refs, k * PIECE, SHARE, PIECE), PIECE)
    out_ref[2 * PIECE :, :] = coded_rows(stem_ref[...], SIDE)


def recode_kernel(recv_refs, out_ref):
    for k in range(2):
        out_ref[k * PIECE : (k + 1) * PIECE, :] = coded_rows(summed(recv_refs, k * PIECE, SHARE, PIECE), PIECE)
    out_ref[2 * PIECE :, :] = coded_rows(summed(recv_refs, 2 * PIECE, 27, SIDE), SIDE)


def stack_kernel(inner, parts, out_ref):
    count = parts[0].shape[0]
    for k, part in enumerate(parts):
        if inner:
            for entry in range(count):
                out_ref[entry * len(parts) + k] = part[entry]
        else:
            out_ref[k * count : (k + 1) * count] = part[...]


def adam_terms(gradient, factor, weight, first, second, teacher):
    clipped = gradient * factor
    first_new = BETA_FIRST * first + (1.0 - BETA_FIRST) * clipped
    second_new = BETA_SECOND * second + (1.0 - BETA_SECOND) * (clipped * clipped)
    second_hat = second_new * (1.0 / (1.0 - BETA_SECOND**STEP))
    weight_new = weight * (1.0 - LEARN_RATE * WEIGHT_DECAY) - (
        first_new * (LEARN_RATE / (1.0 - BETA_FIRST**STEP)) / (jnp.sqrt(second_hat) + ADAM_EPS)
    )
    return weight_new, first_new, second_new, TEACHER_KEEP * teacher + (1.0 - TEACHER_KEEP) * weight_new


def place_codes(codes, grads):
    mine = lax.axis_index("dp") & (QUARTERS - 1)
    for offset, source in enumerate(codes):
        place = pl.multiple_of((mine ^ offset) * SHARE, 8)
        for k in range(2):
            grads[k, pl.ds(place, SHARE), :] = decoded(source[k * PIECE : (k + 1) * PIECE, :], SHARE)


def square_sums(grads):
    return sum(eight(grads[k] * grads[k]) for k in range(2))


def decode_kernel(codes, grads_ref, stem_ref, squares_ref):
    place_codes(codes, grads_ref)
    stem_ref[...] = summed(codes, 2 * PIECE, 27, SIDE)
    squares_ref[...] = square_sums(grads_ref)


def update_kernel(
    own_ref, own_stem, own_squares, other_codes, own_facts, other_facts,
    cw, cf, cs, ct, sw, sf, ss, st, hw, hf, hs, ht, nw, nf, ns, nt,
    cw_o, cf_o, cs_o, ct_o, cb_o, sw_o, sf_o, ss_o, st_o, sb_o, hw_o, hf_o, hs_o, ht_o, hb_o,
    nw_o, nf_o, ns_o, nt_o, norm_o, cross_o, count_o, consistency_o,
    factor_ref, other_ref,
):
    conv = pl.program_id(0)
    view = lax.axis_index("view")

    @pl.when(conv == 0)
    def _():
        facts = own_facts[GRAD_ROWS:, :] + other_facts[GRAD_ROWS:, :]
        small, sums = facts[:24], facts[24:]
        place_codes(other_codes, other_ref)
        stem = own_stem[...] + summed(other_codes, 2 * PIECE, 27, SIDE)
        stem = stem[:, :CH]
        head = small[:CLASSES, :CH]
        gains = jnp.concatenate([sums[1:2], small[17:18], sums[3:4], small[19:20]], axis=0)[:, :CH]
        shifts = jnp.concatenate([sums[0:1], small[16:17], sums[2:3], small[18:19]], axis=0)[:, :CH]
        total = jnp.zeros((1, 1), F32)
        for part in (stem, head, gains, shifts):
            total += jnp.sum(jnp.sum(part * part, axis=1, keepdims=True), axis=0, keepdims=True)
        squares = own_squares[...] + square_sums(other_ref)
        total += jnp.sum(jnp.sum(squares, axis=0, keepdims=True), axis=1, keepdims=True)
        norm = jnp.sqrt(total)
        factor = CLIP_LIMIT / jnp.maximum(norm, CLIP_LIMIT)
        factor_ref[...] = jnp.broadcast_to(factor, factor_ref.shape)
        norm_o[...] = norm
        cross_o[...] = small[20:21, 0:1]
        consistency_o[...] = small[20:21, 1:2]
        count_o[...] = own_facts[GRAD_ROWS + 20 : GRAD_ROWS + 21, 2:3]
        sw_o[...], sf_o[...], ss_o[...], st_o[...] = adam_terms(stem, factor, sw[...], sf[...], ss[...], st[...])
        sb_o[...] = sw_o[...].astype(BF16)
        hw_o[...], hf_o[...], hs_o[...], ht_o[...] = adam_terms(head, factor, hw[...], hf[...], hs[...], ht[...])
        hb_o[...] = hw_o[...].astype(BF16)
        for k, part in enumerate((gains, shifts)):
            nw_o[k], nf_o[k], ns_o[k], nt_o[k] = adam_terms(part, factor, nw[k], nf[k], ns[k], nt[k])

    def update(ref, second):
        factor = factor_ref[0:1, 0:1]
        for k in range(BLOCKS):
            lanes = slice(k * LANE, min((k + 1) * LANE, WIDE))
            gradient = ref[second, k * CH : (k + 1) * CH, 0 : lanes.stop - lanes.start]
            weight, first, second_moment, teacher = adam_terms(
                gradient, factor, cw[conv, :, lanes], cf[conv, :, lanes], cs[conv, :, lanes], ct[conv, :, lanes]
            )
            cw_o[:, lanes] = weight
            cf_o[:, lanes] = first
            cs_o[:, lanes] = second_moment
            ct_o[:, lanes] = teacher
            cb_o[:, lanes] = weight.astype(BF16)

    mine = conv // 2 == view

    @pl.when(mine)
    def _():
        update(own_ref, conv & 1)

    @pl.when(jnp.logical_not(mine))
    def _():
        update(other_ref, conv & 1)


def whole(shape):
    return pl.BlockSpec(shape, lambda i: (0,) * len(shape))


def scalars():
    return pl.BlockSpec(memory_space=pltpu.SMEM)


def conv_part(k):
    return pl.BlockSpec((None, CH, WIDE), lambda i: (k, 0, 0))


def held():
    return pl.BlockSpec(memory_space=pltpu.VMEM)


def hold(values):
    return pltpu.with_memory_space_constraint(values, pltpu.VMEM)


def struct(shape, kind=F32):
    return jax.ShapeDtypeStruct(shape, kind)


def to_partner(values, difference):
    return lax.ppermute(values, "dp", [(i, i ^ difference) for i in range(lax.axis_size("dp"))])


def to_other_core(values, difference):
    size = lax.axis_size("dp")
    return lax.ppermute(values, ("view", "dp"), [(i, i ^ (difference + size)) for i in range(2 * size)])


def issue_order(ways, shift, crossing):
    if ways < 4:
        return range(1, ways)
    if shift == 0:
        return (1, 3, 2)
    return (1, 2, 3) if crossing else (1, 3, 2)


def from_partners(values, shift, ways, crossing=True):
    send = to_other_core if crossing else to_partner
    parts = [to_other_core(values, 0) if crossing else values] + [None] * (ways - 1)
    for offset in issue_order(ways, shift, crossing):
        parts[offset] = send(values, offset << shift)
    return parts


def stages():
    size = lax.axis_size("dp")
    groups = []
    shift = 0
    while (1 << shift) < size:
        ways = min(4, size >> shift)
        groups.append((shift, ways))
        shift += 2
    assert len(groups) % 2 == 0
    return groups


def sum_parts(values, beside=None):
    groups = stages()
    for shift, ways in groups[:-1]:
        parts = from_partners(values, shift, ways)
        if beside is not None:
            parts, beside = lax.optimization_barrier((parts, beside))
        values = sum(parts)
    return tuple(from_partners(values, *groups[-1])), beside


def stack(parts, inner):
    shape = (len(parts) * parts[0].shape[0],) + parts[0].shape[1:]
    return pl.pallas_call(
        functools.partial(stack_kernel, inner), out_shape=struct(shape, parts[0].dtype), compiler_params=PARAMS, name="stack"
    )(tuple(parts))


def gather_parts(values, groups):
    inner = groups[0][0] > 0
    for shift, ways in groups[:-1]:
        values = stack(from_partners(values, shift, ways), inner)
    return tuple(from_partners(values, *groups[-1]))


def swap_view(values):
    return lax.ppermute(values, "view", [(0, 1), (1, 0)])


def forward_weights(conv):
    shape = (2, 6 * LANE, 2 * LANE)
    return pl.pallas_call(
        forward_weight_kernel,
        grid=(2,),
        in_specs=[pl.BlockSpec((None, CH, WIDE), lambda i: (2 * i + 1, 0, 0))],
        out_specs=pl.BlockSpec((None,) + shape[1:], lambda i: (i, 0, 0)),
        out_shape=struct(shape, BF16),
        compiler_params=PARAMS,
        cost_estimate=pl.CostEstimate(flops=2_000_000_000, bytes_accessed=4_000_000, transcendentals=0),
        name="forward_weight",
    )(conv)


def backward_weights(conv):
    return pl.pallas_call(
        backward_weight_kernel,
        grid=(1,),
        in_specs=[conv_part(k) for k in range(4)],
        out_specs=[whole((2, 6 * LANE, 2 * LANE))] * 2,
        out_shape=[struct((2, 6 * LANE, 2 * LANE), BF16)] * 2,
        compiler_params=PARAMS,
        cost_estimate=pl.CostEstimate(flops=4_000_000_000, bytes_accessed=8_000_000, transcendentals=0),
        name="backward_weight",
    )(conv, conv, conv, conv)


def shards(
    augmented, shake_ratio, labels, labelled, view_order,
    stem_weight, conv_weight, head_weight, norm_param,
    teacher_stem, teacher_conv, teacher_head, teacher_norm,
    first_stem, first_conv, first_head, first_norm,
    second_stem, second_conv, second_head, second_norm,
):
    dp = lax.axis_size("dp")
    all_images = IMAGES * dp
    cell_count = float(all_images * CELLS)
    rows = dp * 2 * IMAGES
    conv, conv_t, conv_f, conv_s = (
        jnp.transpose(v, (0, 2, 1)) for v in (conv_weight, teacher_conv, first_conv, second_conv)
    )
    head, head_t, head_f, head_s = (v.T for v in (head_weight, teacher_head, first_head, second_head))
    pixels = jnp.transpose(augmented[0], (0, 3, 1, 2))
    msg = struct((8, LANE))
    groups = stages()
    last_ways = groups[-1][1]
    recv_spec = (held(),) * last_ways
    norm_spec = whole((2, 4, CH))
    head_spec = whole((CLASSES, CH))
    moved_shape = (3, (SIDE + 4) * 8, LANE)
    frame_one, frame_two = FRAME + (LANE,), (2,) + FRAME + (LANE,)
    values_shape, grad_shape = (ALL, 2 * LANE), struct((GRAD_ROWS, LANE))
    terms_scratch = pltpu.VMEM((16, LANE), F32)

    first_s, first_t, low, moved, stem_sums, message = pl.pallas_call(
        first_kernel,
        in_specs=[pl.BlockSpec(memory_space=pltpu.HBM)] * 5,
        out_specs=[held()] * 6,
        out_shape=[
            pltpu.VMEM(values_shape, F32), pltpu.VMEM(values_shape, F32), pltpu.VMEM(frame_one, BF16),
            pltpu.VMEM(moved_shape, F32), struct((2, 8, LANE)), msg,
        ],
        scratch_shapes=[
            pltpu.VMEM(moved_shape[1:], F32), pltpu.VMEM((STEM_ROWS, 2 * LANE), F32),
            pltpu.VMEM((STEM_ROWS, 2 * LANE), BF16), pltpu.VMEM((2, 9 * LANE, 2 * LANE), BF16),
            pltpu.VMEM(frame_one, BF16), pltpu.VMEM((IMAGES, 3, SIDE, SIDE), BF16), pltpu.VMEM((27, CH), F32),
            pltpu.VMEM((27, CH), F32), pltpu.VMEM((4, CH, WIDE), F32), pltpu.SemaphoreType.DMA((7,)),
        ],
        compiler_params=PARAMS,
        name="first_conv",
    )(*(pltpu.with_memory_space_constraint(v, pltpu.HBM) for v in (pixels, stem_weight, teacher_stem, conv, conv_t)))
    first_s, first_t, low, moved = (hold(v) for v in (first_s, first_t, low, moved))
    recv1, weight_s = sum_parts(message, forward_weights(conv))
    known = pl.pallas_call(
        facts_kernel,
        in_specs=[scalars()] * 4,
        out_specs=held(),
        out_shape=struct((2, 8, LANE)),
        compiler_params=PARAMS,
        name="facts",
    )(shake_ratio, labels, labelled, view_order)
    recv1, weight_t, known = lax.optimization_barrier((recv1, forward_weights(conv_t), known))

    second_s, second_t, hidden, bent_one, image_sums, message = pl.pallas_call(
        functools.partial(second_kernel, cell_count),
        in_specs=[held()] * 2 + [recv_spec] + [held()] * 4,
        out_specs=[held()] * 6,
        out_shape=[pltpu.VMEM(values_shape, F32)] * 2
        + [pltpu.VMEM(frame_two, BF16), pltpu.VMEM(values_shape, F32), struct((4, 8, LANE)), msg],
        scratch_shapes=[pltpu.VMEM(frame_two, BF16), terms_scratch, terms_scratch],
        compiler_params=PARAMS,
        name="second_conv",
    )(first_s, first_t, recv1, norm_param, teacher_norm, weight_s, weight_t)
    second_s, second_t, hidden, bent_one = (hold(v) for v in (second_s, second_t, hidden, bent_one))
    recv2, (back_weight_two, back_weight_one) = sum_parts(message, backward_weights(conv))

    prob = pl.pallas_call(
        functools.partial(teacher_kernel, cell_count),
        in_specs=[held()] * 2 + [recv_spec] + [held()] * 4,
        out_specs=held(),
        out_shape=struct((8, LANE)),
        scratch_shapes=[terms_scratch],
        compiler_params=PARAMS,
        name="teacher_logits",
    )(known, second_t, recv2, teacher_norm, head_t, stem_sums, image_sums)
    other = swap_view(prob)
    facts, bent_two = pl.pallas_call(
        functools.partial(student_kernel, cell_count),
        in_specs=[held()] * 2 + [recv_spec] + [held()] * 4,
        out_specs=[held()] * 2,
        out_shape=[struct((8, 3 * LANE)), pltpu.VMEM(values_shape, F32)],
        scratch_shapes=[terms_scratch],
        compiler_params=PARAMS,
        cost_estimate=pl.CostEstimate(flops=4_000_000_000, bytes_accessed=8_000_000, transcendentals=0),
        name="student_logits",
    )(known, second_s, recv2, norm_param, head, stem_sums, image_sums)
    bent_two = hold(bent_two)
    facts, other = lax.optimization_barrier((facts, other))
    facts = pl.pallas_call(
        assemble_kernel, out_shape=struct((1, 8, 3 * LANE)), compiler_params=PARAMS, name="assemble"
    )(facts, other)
    recv3 = gather_parts(facts, groups[::-1])

    du, dy, message, small, dmix = pl.pallas_call(
        functools.partial(back_second_kernel, cell_count, float(all_images)),
        in_specs=[held()] * 4 + [recv_spec] * 2 + [(held(),) * groups[0][1]] + [held()] * 3,
        out_specs=[held()] * 5,
        out_shape=[
            pltpu.VMEM(values_shape, F32), pltpu.VMEM(frame_two, BF16), msg, struct((24, LANE)), struct((8, LANE)),
        ],
        scratch_shapes=[
            terms_scratch, terms_scratch, pltpu.VMEM((3, rows, LANE), F32), pltpu.VMEM((8, LANE), F32),
        ],
        compiler_params=PARAMS,
        name="back_second",
    )(second_s, first_s, bent_two, bent_one, recv1, recv2, recv3, norm_param, head, back_weight_two)
    du, dy = hold(du), hold(dy)

    def second_weight(other):
        return pl.pallas_call(
            functools.partial(second_weight_kernel, other),
            in_specs=[held()] * 2,
            out_specs=held(),
            out_shape=grad_shape,
            scratch_shapes=[pltpu.VMEM((2 * LANE, 6 * LANE), F32)],
            compiler_params=PARAMS,
            cost_estimate=pl.CostEstimate(flops=4_000_000_000, bytes_accessed=8_000_000, transcendentals=0),
            name="second_weight",
        )(hidden, dy)

    send2, keep2 = second_weight(True), second_weight(False)
    recv5, send2 = sum_parts(message, send2)
    recv_grad2 = swap_view(send2)
    recv5, keep2, recv_grad2 = lax.optimization_barrier((recv5, keep2, recv_grad2))

    frame, keep1, send1 = pl.pallas_call(
        functools.partial(back_weight_kernel, cell_count),
        in_specs=[held()] * 3 + [recv_spec] * 2 + [held()] * 2,
        out_specs=[held()] * 3,
        out_shape=[pltpu.VMEM(frame_two, BF16)] + [struct((GRAD_ROWS + 32, LANE))] * 2,
        scratch_shapes=[terms_scratch, pltpu.VMEM((2 * LANE, 9 * LANE), F32)],
        compiler_params=PARAMS,
        cost_estimate=pl.CostEstimate(flops=8_000_000_000, bytes_accessed=16_000_000, transcendentals=0),
        name="back_weight",
    )(du, first_s, low, recv1, recv5, norm_param, small)
    frame = hold(frame)
    recv_grad1 = swap_view(send1)

    def back_stem(step, before=()):
        going = step < STEPS - 1
        return pl.pallas_call(
            functools.partial(back_stem_kernel, step),
            in_specs=[held()] * (4 + len(before)),
            out_specs=[held()] * 2 if going else held(),
            out_shape=[struct((LINE, LANE)), struct((STEM_ROWS, LANE))] if going else struct((27, LANE)),
            compiler_params=PARAMS,
            cost_estimate=pl.CostEstimate(flops=2_000_000_000, bytes_accessed=4_000_000, transcendentals=0),
            name="back_stem",
        )(frame, moved, dmix, back_weight_one, *before)

    started = back_stem(0)
    recv_grad1, started = lax.optimization_barrier((recv_grad1, started))
    coded = pl.pallas_call(
        encode_kernel,
        out_shape=[struct((2 * PIECE, LANE), jnp.int16)] * QUARTERS,
        scratch_shapes=[pltpu.VMEM((2, GRAD_ROWS, LANE), F32)],
        compiler_params=PARAMS,
        name="encode",
    )(keep2, recv_grad2, keep1, recv_grad1)
    scattered = [coded[0]] + [None] * (QUARTERS - 1)
    for offset in issue_order(QUARTERS, 0, False):
        scattered[offset] = to_partner(coded[offset], offset)
    scattered = tuple(scattered)

    stem_grad = started
    for step in range(1, STEPS):
        stem_grad = back_stem(step, tuple(stem_grad))

    stem_grad, scattered = lax.optimization_barrier((stem_grad, scattered))
    code_shape = struct((CODE_ROWS, LANE), jnp.int16)
    codes = pl.pallas_call(combine_kernel, out_shape=code_shape, compiler_params=PARAMS, name="combine")(
        scattered, stem_grad
    )
    for group in groups[1:]:
        codes = pl.pallas_call(recode_kernel, out_shape=code_shape, compiler_params=PARAMS, name="recode")(
            tuple(from_partners(codes, *group, crossing=False))
        )
    own = tuple(from_partners(codes, *groups[0], crossing=False))
    other_grads = tuple(swap_view(part) for part in own)
    own_parts = pl.pallas_call(
        decode_kernel,
        out_shape=[struct((2, GRAD_ROWS, LANE)), struct((27, LANE)), struct((8, LANE))],
        compiler_params=PARAMS,
        name="decode",
    )(own)
    own_parts, other_grads = lax.optimization_barrier((own_parts, other_grads))

    conv_block = pl.BlockSpec((None, CH, WIDE), lambda i: (i, 0, 0))
    stem_block, norm_block = whole((27, CH)), norm_spec
    code_spec = (held(),) * QUARTERS
    grads_scratch = pltpu.VMEM((2, GRAD_ROWS, LANE), F32)
    outs = pl.pallas_call(
        update_kernel,
        grid=(4,),
        in_specs=[held()] * 3 + [code_spec] + [held()] * 18,
        out_specs=[conv_block] * 5 + [stem_block] * 5 + [head_spec] * 5 + [norm_block] * 4 + [whole((1, 1))] * 4,
        out_shape=[struct((4, CH, WIDE))] * 4 + [struct((4, CH, WIDE), BF16)]
        + [struct((27, CH))] * 4 + [struct((27, CH), BF16)]
        + [struct((CLASSES, CH))] * 4 + [struct((CLASSES, CH), BF16)]
        + [struct((2, 4, CH))] * 4 + [struct((1, 1))] * 4,
        scratch_shapes=[pltpu.VMEM((8, LANE), F32), grads_scratch],
        compiler_params=PARAMS,
        name="update",
    )(
        *own_parts, other_grads, keep1, recv_grad1,
        conv, conv_f, conv_s, conv_t, stem_weight, first_stem, second_stem, teacher_stem,
        head, head_f, head_s, head_t, norm_param, first_norm, second_norm, teacher_norm,
    )
    convs = [jnp.transpose(v, (0, 2, 1)) for v in outs[:5]]
    stems = outs[5:10]
    heads = [v.T for v in outs[10:15]]
    norms = outs[15:19]
    return (
        *(v.reshape(()) for v in outs[19:23]),
        *stems[:4], *convs[:4], *heads[:4], *norms, stems[4], convs[4], heads[4],
    )


def solution(mesh):
    in_specs = (
        (P("view", "dp", None, None, None), P("view", "dp"), P("dp"), P("dp")) + (P(),) * 17
    )
    return jax.shard_map(shards, mesh=mesh, in_specs=in_specs, out_specs=(P(),) * 23, check_vma=False)
```
